32 devices in a mesh: shard: 4 (over y, x), ctx: 4 (over z), tp: 2 (over core).
Axes of the slice: x: 2, y: 2, z: 4, core: 2. Of those that a mesh axis runs over, the one named last changes fastest.
Arguments:
- inputs: float32 [32, 512, 1024], P('shard', 'ctx'), may hold values from -6 to 6
- lengths: int32 [32], P('shard'), may hold values from 128 to 512, as said below
- query_weight: bfloat16 [1024, 1024], P('shard', 'tp'), may hold values from -0.1875 to 0.1875
- key_weight: bfloat16 [1024, 1024], P('shard', 'tp'), may hold values from -0.1875 to 0.1875
- value_weight: bfloat16 [1024, 1024], P('shard', 'tp'), may hold values from -0.1875 to 0.1875
- output_weight: bfloat16 [1024, 1024], P('tp', 'shard'), may hold values from -1.5 to 1.5
- expand_weight: bfloat16 [1024, 4096], P('shard', 'tp'), may hold values from -0.1875 to 0.1875
- reduce_weight: bfloat16 [4096, 1024], P('tp', 'shard'), may hold values from -0.09375 to 0.09375
- query_bias: bfloat16 [16, 64], P('tp', 'shard'), may hold values from -3 to 3
- value_bias: bfloat16 [16, 64], P('tp', 'shard'), may hold values from -0.59765625 to 0.59765625
- expand_bias: bfloat16 [64, 64], P('tp', 'shard'), may hold values from -3 to 3
- output_bias: bfloat16 [1024], P('shard'), may hold values from -3 to 3
- reduce_bias: bfloat16 [1024], P('shard'), may hold values from -3 to 3
- first_gain: bfloat16 [1024], P('shard'), may hold values from 0.25 to 1.75
- first_shift: bfloat16 [1024], P('shard'), may hold values from -3 to 3
- second_gain: bfloat16 [1024], P('shard'), may hold values from 0.25 to 1.75
- second_shift: bfloat16 [1024], P('shard'), may hold values from -3 to 3
- cotangent: float32 [32, 512, 1024], P('shard', 'ctx'), may hold values from -6 to 6
Outputs:
- layer_out: float32 [32, 512, 1024], P('shard', 'ctx')
- input_grad: float32 [32, 512, 1024], P('shard', 'ctx')
- query_weight_grad: float32 [1024, 1024], P('shard', 'tp')
- key_weight_grad: float32 [1024, 1024], P('shard', 'tp')
- value_weight_grad: float32 [1024, 1024], P('shard', 'tp')
- output_weight_grad: float32 [1024, 1024], P('tp', 'shard')
- expand_weight_grad: float32 [1024, 4096], P('shard', 'tp')
- reduce_weight_grad: float32 [4096, 1024], P('tp', 'shard')
- query_bias_grad: float32 [16, 64], P('tp', 'shard')
- value_bias_grad: float32 [16, 64], P('tp', 'shard')
- expand_bias_grad: float32 [64, 64], P('tp', 'shard')
- output_bias_grad: float32 [1024], P('shard')
- reduce_bias_grad: float32 [1024], P('shard')
- first_gain_grad: float32 [1024], P('shard')
- first_shift_grad: float32 [1024], P('shard')
- second_gain_grad: float32 [1024], P('shard')
- second_shift_grad: float32 [1024], P('shard')
The draws below stay inside these ranges and needn't reach their ends.
Inputs may be any that keep to these rules, and one draw needn't show every extreme that they name: `lengths`: in each group of 8 sequences held by one index of shard, one sequence has all 512 slots valid.
All inputs are finite; a program needn't handle non-finite values.
Results may differ from the reference program's by a relative error of at most 0.019.
Values may be sent and summed in bfloat16 or wider, within the bound.
A program may use at most 192 MiB of HBM per device.

```python
import jax
import jax.numpy as jnp
from jax import lax

D = 1024
HEADS = 16
HD = 64
FF = 4096
LEN = 512
SEQ_DEV = 8
SEQS = 32


def draw_lengths(key, part):
    key = jax.random.fold_in(key, 7)
    random_lengths = jax.random.randint(jax.random.fold_in(key, 1), (SEQS,), LEN // 4, LEN + 1)
    group_count = SEQS // SEQ_DEV
    chosen = jax.random.randint(jax.random.fold_in(key, 2), (group_count,), 0, SEQ_DEV)
    filled = (jnp.arange(SEQ_DEV)[None, :] == chosen[:, None]).reshape(SEQS)
    return jnp.where(filled, LEN, random_lengths).astype(jnp.int32)


def level_of(key, dims, pieces, smallest, high):
    factor_of = 1.0
    for dim, shards_of in pieces:
        steps = jax.random.uniform(jax.random.fold_in(jax.random.fold_in(key, 6), dim), (shards_of,), jnp.float32, smallest / len(pieces), high / len(pieces))
        factor_of = factor_of * jnp.repeat(jnp.exp(steps), dims[dim] // shards_of).reshape((-1,) + (1,) * (len(dims) - 1 - dim))
    return factor_of


def gaussian(stream_key, shape, scale, limit, split=(), held_as=jnp.bfloat16):
    drawn = jax.random.normal(stream_key, shape, jnp.float32) * scale
    if len(split) > 0:
        drawn = level_of(stream_key, shape, split, -0.22, 0.18) * drawn
    return jnp.clip(drawn, min=-limit, max=limit).astype(held_as)


def setup_inputs(seed: int = 0) -> dict:
    keys = jax.random.split(jax.random.key(seed), 19)
    inputs = gaussian(keys[0], (SEQS, LEN, D), 1.0, 6.0, ((0, 4), (1, 4)), jnp.float32)
    lengths = draw_lengths(jax.random.fold_in(keys[18], 71), 0)
    query_weight = gaussian(keys[2], (D, D), D ** -0.5, 0.1875, ((0, 4), (1, 2)))
    key_weight = gaussian(keys[3], (D, D), D ** -0.5, 0.1875, ((0, 4), (1, 2)))
    value_weight = gaussian(keys[4], (D, D), D ** -0.5, 0.1875, ((0, 4), (1, 2)))
    output_weight = gaussian(keys[5], (D, D), (max(D // 64, 1)) ** -0.5, 1.5, ((0, 2), (1, 4)))
    expand_weight = gaussian(keys[6], (D, FF), D ** -0.5, 0.1875, ((0, 4), (1, 2)))
    reduce_weight = gaussian(keys[7], (FF, D), FF ** -0.5, 0.09375, ((0, 2), (1, 4)))
    query_bias = gaussian(keys[8], (HEADS, HD), 0.5, 3.0, ((0, 2), (1, 4)))
    value_bias = gaussian(keys[9], (HEADS, HD), 0.1, 0.59765625, ((0, 2), (1, 4)))
    expand_bias = gaussian(keys[10], (FF // HD, HD), 0.5, 3.0, ((0, 2), (1, 4)))
    output_bias = gaussian(keys[11], (D,), 0.5, 3.0, ((0, 4),))
    reduce_bias = gaussian(keys[12], (D,), 0.5, 3.0, ((0, 4),))
    first_gain = jnp.clip(1.0 + 0.15 * jax.random.normal(keys[13], (D,), jnp.float32), 0.25, 1.75).astype(jnp.bfloat16)
    first_shift = gaussian(keys[14], (D,), 0.5, 3.0, ((0, 4),))
    second_gain = jnp.clip(1.0 + 0.15 * jax.random.normal(keys[15], (D,), jnp.float32), 0.25, 1.75).astype(jnp.bfloat16)
    second_shift = gaussian(keys[16], (D,), 0.5, 3.0, ((0, 4),))
    cotangent = gaussian(keys[17], (SEQS, LEN, D), 1.0, 6.0, ((0, 4), (1, 4)), jnp.float32)
    return dict(inputs=inputs, lengths=lengths, query_weight=query_weight, key_weight=key_weight, value_weight=value_weight, output_weight=output_weight, expand_weight=expand_weight, reduce_weight=reduce_weight, query_bias=query_bias, value_bias=value_bias, expand_bias=expand_bias, output_bias=output_bias, reduce_bias=reduce_bias, first_gain=first_gain, first_shift=first_shift, second_gain=second_gain, second_shift=second_shift, cotangent=cotangent)


EPSILON = 1e-05
MASKED = -1e+30
PRECISE = lax.Precision.HIGHEST

@jax.custom_vjp
def low(v):
    return lax.optimization_barrier(v.astype(jnp.bfloat16)).astype(jnp.float32)

@jax.custom_vjp
def low_back(v):
    return v

def low_keep(v):
    return (low(v), None)

def low_pass(kept, grad):
    return (grad,)

def back_keep(v):
    return (v, None)

def back_low(kept, grad):
    return (low(grad),)
low.defvjp(low_keep, low_pass)
low_back.defvjp(back_keep, back_low)

def layer_norm(hidden, gain, shift):
    row_mean = lax.optimization_barrier(jnp.mean(hidden, -1, keepdims=True))
    centred = hidden - row_mean
    inv_std = lax.rsqrt(lax.optimization_barrier(jnp.mean(centred * centred, -1, keepdims=True)) + EPSILON)
    return centred * inv_std * gain + shift

def product(left, right):
    return jnp.matmul(left, right, precision=PRECISE)

def bert_layer(inputs, live_keys, params):
    query_weight, key_weight, value_weight, output_weight, expand_weight, reduce_weight, query_bias, value_bias, expand_bias, output_bias, reduce_bias, first_gain, first_shift, second_gain, second_shift = params
    groups, columns, model_width = inputs.shape
    head_count = model_width // HD
    head_shape = (groups, columns, head_count, HD)
    inputs_low = low(inputs)
    queries = low(low_back(product(inputs_low, query_weight) + query_bias.reshape(-1)))
    key_rows = low(low_back(product(inputs_low, key_weight)))
    values = low(low_back(product(inputs_low, value_weight) + value_bias.reshape(-1)))
    scores = jnp.einsum('gqhe,gkhe->ghqk', queries.reshape(head_shape), key_rows.reshape(head_shape), precision=PRECISE) * HD ** (-0.5)
    scores = low_back(jnp.where(live_keys[:, None, None, :], scores, MASKED))
    probabilities = low(jax.nn.softmax(scores, axis=-1))
    attended = jnp.einsum('ghqk,gkhe->gqhe', probabilities, values.reshape(head_shape), precision=PRECISE).reshape(groups, columns, model_width)
    branch = low_back(product(low(low_back(attended)), output_weight) + output_bias)
    normed = layer_norm(inputs + branch, first_gain, first_shift)
    pre_act = low_back(product(low(normed), expand_weight) + expand_bias.reshape(-1))
    hidden = low(jax.nn.gelu(pre_act, approximate=False))
    second = normed + low_back(product(hidden, reduce_weight) + reduce_bias)
    return layer_norm(second, second_gain, second_shift)

def reference(inputs, lengths, query_weight, key_weight, value_weight, output_weight, expand_weight, reduce_weight, query_bias, value_bias, expand_bias, output_bias, reduce_bias, first_gain, first_shift, second_gain, second_shift, cotangent):
    params = tuple((piece.astype(jnp.float32) for piece in (query_weight, key_weight, value_weight, output_weight, expand_weight, reduce_weight, query_bias, value_bias, expand_bias, output_bias, reduce_bias, first_gain, first_shift, second_gain, second_shift)))
    live_keys = jnp.arange(LEN).astype(jnp.int32)[None, :] < lengths[:, None]
    group_count = SEQS // SEQ_DEV

    def advance(totals, portion):
        x_group, live_group, grad_group = portion
        output, pullback = jax.vjp(lambda xx, pp: bert_layer(xx, live_group, pp), x_group, params)
        masked_grad = grad_group * live_group[..., None].astype(jnp.float32)
        input_grads, param_grads = pullback(masked_grad)
        return (jax.tree.map(jnp.add, totals, param_grads), (output, input_grads))
    zeros = jax.tree.map(jnp.zeros_like, params)
    grouped = (inputs.reshape(group_count, SEQ_DEV, LEN, D), live_keys.reshape(group_count, SEQ_DEV, LEN), cotangent.reshape(group_count, SEQ_DEV, LEN, D))
    totals, (outputs, input_grads) = lax.scan(advance, zeros, grouped)
    return (outputs.reshape(SEQS, LEN, D), input_grads.reshape(SEQS, LEN, D), totals[0], totals[1], totals[2], totals[3], totals[4], totals[5], totals[6], totals[7], totals[8], totals[9], totals[10], totals[11], totals[12], totals[13], totals[14])
```

```python
import functools

import jax
import jax.numpy as jnp
from jax import lax
from jax.experimental import pallas as pl
from jax.experimental.pallas import tpu as pltpu
from jax.sharding import PartitionSpec as P

HD = 64
UNIT = 512
EPSILON = 1e-05
MASKED = -1e30
MESH = pl.DeviceIdType.MESH
F32 = jnp.float32
BF16 = jnp.bfloat16


def place():
    return lax.axis_index("shard"), lax.axis_index("ctx"), lax.axis_index("tp")


def rcopy(src, dst, send, recv, dev):
    return pltpu.make_async_remote_copy(
        src_ref=src, dst_ref=dst, send_sem=send, recv_sem=recv, device_id=dev, device_id_type=MESH
    )


def greet(devices):
    barrier = pltpu.get_barrier_semaphore()
    for dev in devices:
        pl.semaphore_signal(barrier, inc=1, device_id=dev, device_id_type=MESH)
    pl.semaphore_wait(barrier, len(devices))


def partners(n, nz):
    s, z, c = place()
    return (
        [(s ^ k, z, c) for k in range(1, n)]
        + [(s, z, 1 - c)]
        + [(s, lax.rem(z + k, nz), c) for k in range(1, nz)]
    )


def gather_kernel(
    n, nz, own_ref, x_ref, g_ref, full_ref, xs_ref, gs_ref,
    own_send, own_recv, fwd_send, fwd_recv, core_send, core_recv, act_send, act_recv, local_sem,
):
    s, z, c = place()
    units, rows, width = own_ref.shape
    half = rows // 2
    greet(partners(n, nz))
    mine = pl.ds(pl.multiple_of(s * rows, rows), rows)
    block = x_ref.shape[1]
    zrows = pl.ds(pl.multiple_of(z * block, block), block)

    def block_at(k):
        return pl.ds(pl.multiple_of((s ^ k) * rows, rows), rows)

    def half_at(k, h):
        return pl.ds(pl.multiple_of((s ^ k) * rows + h * half, half), half)

    keep = pltpu.make_async_copy(own_ref, full_ref.at[c, :, mine, :], local_sem.at[0])
    keep.start()
    share = rcopy(
        own_ref, full_ref.at[c, :, mine, :], core_send.at[units, 0], core_recv.at[units, 0], (s, z, 1 - c)
    )
    share.start()

    def act(k, which):
        src, dst = ((x_ref, xs_ref), (g_ref, gs_ref))[which]
        to = lax.rem(z + k, nz)
        return rcopy(
            src.at[2 * to + c], dst.at[zrows, :], act_send.at[which, k], act_recv.at[which, k], (s, to, c)
        )

    def act_in(k, which):
        dst = (xs_ref, gs_ref)[which]
        src = lax.rem(z + nz - k, nz)
        at = dst.at[pl.ds(pl.multiple_of(src * block, block), block), :]
        return rcopy(at, at, act_send.at[which, k], act_recv.at[which, k], (s, src, c))

    for which in range(2):
        for k in range(1, nz):
            act(k, which).start()
    keep_x = pltpu.make_async_copy(x_ref.at[2 * z + c], xs_ref.at[zrows, :], local_sem.at[1])
    keep_g = pltpu.make_async_copy(g_ref.at[2 * z + c], gs_ref.at[zrows, :], local_sem.at[2])
    keep_x.start()
    keep_g.start()
    direct = [1, 2] if n == 4 else list(range(1, n))

    def own_copy(u, k):
        return rcopy(
            own_ref.at[u], full_ref.at[c, u, mine, :], own_send.at[u, k], own_recv.at[u, k], (s ^ k, z, c)
        )

    def own_in(u, k):
        at = full_ref.at[c, u, block_at(k), :]
        return rcopy(at, at, own_send.at[u, k], own_recv.at[u, k], (s ^ k, z, c))

    def fwd_copy(u, h):
        at = full_ref.at[c, u, half_at(2 - h, h), :]
        return rcopy(at, at, fwd_send.at[u, h], fwd_recv.at[u, h], (s ^ (1 + h), z, c))

    def fwd_in(u, h):
        at = full_ref.at[c, u, half_at(3, h), :]
        return rcopy(at, at, fwd_send.at[u, h], fwd_recv.at[u, h], (s ^ (1 + h), z, c))

    def core_copy(u, k):
        at = full_ref.at[c, u, block_at(k), :]
        return rcopy(at, at, core_send.at[u, k], core_recv.at[u, k], (s, z, 1 - c))

    def core_in(u, k):
        at = full_ref.at[1 - c, u, block_at(k), :]
        return rcopy(at, at, core_send.at[u, k], core_recv.at[u, k], (s, z, 1 - c))

    ahead = 2
    for u in range(ahead):
        for k in direct:
            own_copy(u, k).start()

    def step(u, carry):
        @pl.when(u + ahead < units)
        def _():
            for k in direct:
                own_copy(u + ahead, k).start()

        for k in direct:
            own_in(u, k).wait_recv()
            if n == 4:
                fwd_copy(u, 2 - k).start()
            core_copy(u, k).start()
        if n == 4:
            @pl.when(u > 0)
            def _():
                for h in range(2):
                    fwd_in(u - 1, h).wait_recv()
                core_copy(u - 1, 3).start()

        return carry

    lax.fori_loop(0, units, step, 0)
    if n == 4:
        for h in range(2):
            fwd_in(units - 1, h).wait_recv()
        core_copy(units - 1, 3).start()

    def finish(u, carry):
        for k in direct:
            own_copy(u, k).wait_send()
        if n == 4:
            for h in range(2):
                fwd_copy(u, h).wait_send()
        for k in range(1, n):
            core_copy(u, k).wait_send()
            core_in(u, k).wait_recv()
        return carry

    lax.fori_loop(0, units, finish, 0)
    share.wait_send()
    theirs = full_ref.at[1 - c, :, mine, :]
    rcopy(theirs, theirs, core_send.at[units, 0], core_recv.at[units, 0], (s, z, 1 - c)).wait_recv()
    for which in range(2):
        for k in range(1, nz):
            act(k, which).wait_send()
            act_in(k, which).wait_recv()
    keep.wait()
    keep_x.wait()
    keep_g.wait()


def gather(n, nz, own, x_low, g_low):
    units, rows, width = own.shape
    block, model = x_low.shape[1:]
    return pl.pallas_call(
        functools.partial(gather_kernel, n, nz),
        name="gather_weights",
        out_shape=(
            jax.ShapeDtypeStruct((2, units, rows * n, width), BF16),
            jax.ShapeDtypeStruct((nz * block, model), BF16),
            jax.ShapeDtypeStruct((nz * block, model), BF16),
        ),
        in_specs=[pl.BlockSpec(memory_space=pl.ANY)] * 3,
        out_specs=[pl.BlockSpec(memory_space=pl.ANY)] * 3,
        scratch_shapes=[
            pltpu.SemaphoreType.DMA((units, n)),
            pltpu.SemaphoreType.DMA((units, n)),
            pltpu.SemaphoreType.DMA((units, 2)),
            pltpu.SemaphoreType.DMA((units, 2)),
            pltpu.SemaphoreType.DMA((units + 1, n)),
            pltpu.SemaphoreType.DMA((units + 1, n)),
            pltpu.SemaphoreType.DMA((2, nz)),
            pltpu.SemaphoreType.DMA((2, nz)),
            pltpu.SemaphoreType.DMA((3,)),
        ],
        compiler_params=pltpu.CompilerParams(collective_id=0, has_side_effects=True),
    )(own, x_low, g_low)


def reduce_kernel(
    n, nz, part_ref, out_ref, in_ref, grad_ref, outs_ref, ins_ref,
    stage, got, total, near, far, pair_sum, up, across, down, block_out,
    core_send, core_recv, near_send, near_recv, far_send, far_recv, z_send, z_recv,
    act_send, act_recv, pass_send, pass_recv, load_sem, store_sem, keep_sem,
):
    s, z, c = place()
    units = part_ref.shape[1]
    rows = total.shape[1] // n
    half = rows // 2
    greet(partners(n, nz))
    block = outs_ref.shape[1]
    zrows = pl.ds(pl.multiple_of(z * block, block), block)

    def act(k, which):
        src, dst = ((out_ref, outs_ref), (in_ref, ins_ref))[which]
        to = lax.rem(z + k, nz)
        at = src.at[pl.ds(pl.multiple_of(to * block, block), block), :]
        return rcopy(at, dst.at[2 * z + c], act_send.at[which, k], act_recv.at[which, k], (s, to, c))

    def act_in(k, which):
        dst = (outs_ref, ins_ref)[which]
        src = lax.rem(z + nz - k, nz)
        at = dst.at[2 * src + c]
        return rcopy(at, at, act_send.at[which, k], act_recv.at[which, k], (s, src, c))

    def pass_copy(k, which):
        dst = (outs_ref, ins_ref)[which]
        src = lax.rem(z + nz - k, nz)
        at = dst.at[2 * src + c]
        return rcopy(at, at, pass_send.at[which, k], pass_recv.at[which, k], (s, z, 1 - c))

    def pass_in(k, which):
        dst = (outs_ref, ins_ref)[which]
        src = lax.rem(z + nz - k, nz)
        at = dst.at[2 * src + 1 - c]
        return rcopy(at, at, pass_send.at[which, k], pass_recv.at[which, k], (s, z, 1 - c))

    for which in range(2):
        src, dst = ((out_ref, outs_ref), (in_ref, ins_ref))[which]
        for k in range(1, nz):
            act(k, which).start()
        pltpu.make_async_copy(src.at[zrows, :], dst.at[2 * z + c], keep_sem.at[which]).start()

    def core_copy(u):
        return rcopy(
            part_ref.at[1 - c, u], got.at[u], core_send.at[u], core_recv.at[u], (s, z, 1 - c)
        )

    def load(u):
        return pltpu.make_async_copy(part_ref.at[c, u], stage.at[lax.rem(u, 2)], load_sem.at[lax.rem(u, 2)])

    def rows_of(k):
        return pl.ds(pl.multiple_of((s ^ k) * rows, rows), rows)

    def half_of(k, h):
        return pl.ds(pl.multiple_of((s ^ k) * rows + h * half, half), half)

    def near_copy(u, h, i):
        k = (1 + h, 3)[i]
        return rcopy(
            total.at[lax.rem(u, 2), half_of(k, h), :], near.at[u, h, i],
            near_send.at[u, h, i], near_recv.at[u, h, i], (s ^ (1 + h), z, c),
        )

    def far_copy(u, h):
        return rcopy(
            pair_sum.at[u, h], far.at[u, h], far_send.at[u, h], far_recv.at[u, h], (s ^ (2 - h), z, c)
        )

    def straight(u, k):
        return rcopy(
            total.at[lax.rem(u, 2), rows_of(k), :], near.at[u, k - 1],
            near_send.at[u, k - 1], near_recv.at[u, k - 1], (s ^ k, z, c),
        )

    def z_to(u, src, dst, i, to):
        return rcopy(src.at[u], dst.at[u], z_send.at[u, i], z_recv.at[u, i], (s, to, c))

    last = nz - 1
    edge = jnp.logical_or(z == 0, z == last)
    inner = jnp.where(z == 0, 1, nz - 2)
    outer = jnp.where(z == 1, 0, last)
    other = jnp.where(z == 1, 2, 1)

    def first(u):
        core_copy(u).start()
        load(u).start()

    def second(u):
        @pl.when(u >= 2)
        def _():
            if n == 4:
                for h in range(2):
                    for i in range(2):
                        near_copy(u - 2, h, i).wait_send()
            else:
                for k in range(1, n):
                    straight(u - 2, k).wait_send()
        load(u).wait()
        core_copy(u).wait_recv()
        slot = lax.rem(u, 2)

        def add(i, carry):
            at = pl.ds(pl.multiple_of(i * rows, rows), rows)
            total[slot, at, :] = (stage[slot, at, :].astype(F32) + got[u, at, :].astype(F32)).astype(BF16)
            return carry

        lax.fori_loop(0, n, add, 0)
        if n == 4:
            for h in range(2):
                for i in range(2):
                    near_copy(u, h, i).start()
        else:
            for k in range(1, n):
                straight(u, k).start()

    def third(u):
        slot = lax.rem(u, 2)
        if n == 4:
            for h in range(2):
                for i in range(2):
                    near_copy(u, h, i).wait_recv()
                pair_sum[u, h] = (
                    total[slot, half_of(2 - h, h), :].astype(F32) + near[u, h, 1].astype(F32)
                ).astype(BF16)
                far_copy(u, h).start()
        else:
            for k in range(1, n):
                straight(u, k).wait_recv()

    def fourth(u):
        slot = lax.rem(u, 2)
        if n == 4:
            for h in range(2):
                far_copy(u, h).wait_recv()
                block_out[u, h * half : (h + 1) * half] = (
                    total[slot, half_of(0, h), :].astype(F32)
                    + near[u, h, 0].astype(F32)
                    + far[u, h].astype(F32)
                ).astype(BF16)
        else:
            acc = total[slot, rows_of(0), :].astype(F32)
            for k in range(1, n):
                acc = acc + near[u, k - 1].astype(F32)
            block_out[u] = acc.astype(BF16)

        @pl.when(edge)
        def _():
            z_to(u, block_out, up, 0, inner).start()

    def fifth(u):
        @pl.when(jnp.logical_not(edge))
        def _():
            z_to(u, block_out, up, 0, outer).wait_recv()
            block_out[u] = (block_out[u].astype(F32) + up[u].astype(F32)).astype(BF16)
            z_to(u, block_out, across, 1, other).start()

    def sixth(u):
        @pl.when(jnp.logical_not(edge))
        def _():
            z_to(u, block_out, across, 1, other).wait_recv()
            down[u] = (block_out[u].astype(F32) + across[u].astype(F32)).astype(BF16)
            z_to(u, down, down, 2, outer).start()

    def seventh(u):
        @pl.when(edge)
        def _():
            z_to(u, down, down, 2, inner).wait_recv()

        pltpu.make_async_copy(down.at[u], grad_ref.at[u], store_sem.at[u]).start()

    stages = [first, second, third, fourth, fifth, sixth, seventh]

    def step(t, carry):
        for i, stage_of in reversed(list(enumerate(stages))):
            @pl.when(jnp.logical_and(t >= i, t - i < units))
            def _(stage_of=stage_of, i=i):
                stage_of(t - i)

        @pl.when(t == 3)
        def _():
            for which in range(2):
                for k in range(1, nz):
                    act_in(k, which).wait_recv()
                    pass_copy(k, which).start()
                src, dst = ((out_ref, outs_ref), (in_ref, ins_ref))[which]
                pltpu.make_async_copy(src.at[zrows, :], dst.at[2 * z + c], keep_sem.at[which]).wait()
                at = dst.at[2 * z + c]
                rcopy(at, at, pass_send.at[which, 0], pass_recv.at[which, 0], (s, z, 1 - c)).start()

        return carry

    lax.fori_loop(0, units + len(stages) - 1, step, 0)

    def finish(u, carry):
        core_copy(u).wait_send()
        if n == 4:
            for h in range(2):
                far_copy(u, h).wait_send()

        @pl.when(edge)
        def _():
            z_to(u, block_out, up, 0, inner).wait_send()

        @pl.when(jnp.logical_not(edge))
        def _():
            z_to(u, block_out, across, 1, other).wait_send()
            z_to(u, down, down, 2, outer).wait_send()

        pltpu.make_async_copy(down.at[u], grad_ref.at[u], store_sem.at[u]).wait()
        return carry

    lax.fori_loop(0, units, finish, 0)
    for u in (units - 2, units - 1):
        if n == 4:
            for h in range(2):
                for i in range(2):
                    near_copy(u, h, i).wait_send()
        else:
            for k in range(1, n):
                straight(u, k).wait_send()
    for which in range(2):
        for k in range(1, nz):
            act(k, which).wait_send()
        for k in range(nz):
            pass_copy(k, which).wait_send()
            pass_in(k, which).wait_recv()


def reduce(n, nz, parts, out_low, in_low):
    _, units, model, width = parts.shape
    rows = model // n
    half = rows // 2
    block = out_low.shape[0] // nz
    near_shape = (units, 2, 2, half, width) if n == 4 else (units, n - 1, rows, width)
    near_sems = (units, 2, 2) if n == 4 else (units, n - 1)
    dma = pltpu.SemaphoreType.DMA
    return pl.pallas_call(
        functools.partial(reduce_kernel, n, nz),
        name="reduce_grads",
        out_shape=(
            jax.ShapeDtypeStruct((units, rows, width), BF16),
            jax.ShapeDtypeStruct((2 * nz, block, model), BF16),
            jax.ShapeDtypeStruct((2 * nz, block, model), BF16),
        ),
        in_specs=[pl.BlockSpec(memory_space=pl.ANY)] * 3,
        out_specs=[pl.BlockSpec(memory_space=pl.ANY)] * 3,
        scratch_shapes=[
            pltpu.VMEM((2, model, width), BF16),
            pltpu.VMEM((units, model, width), BF16),
            pltpu.VMEM((2, model, width), BF16),
            pltpu.VMEM(near_shape, BF16),
            pltpu.VMEM((units, 2, half, width), BF16),
            pltpu.VMEM((units, 2, half, width), BF16),
            pltpu.VMEM((units, rows, width), BF16),
            pltpu.VMEM((units, rows, width), BF16),
            pltpu.VMEM((units, rows, width), BF16),
            pltpu.VMEM((units, rows, width), BF16),
            dma((units,)), dma((units,)),
            dma(near_sems), dma(near_sems),
            dma((units, 2)), dma((units, 2)),
            dma((units, 3)), dma((units, 3)),
            dma((2, nz)), dma((2, nz)),
            dma((2, nz)), dma((2, nz)),
            dma((2,)), dma((units,)), dma((2,)),
        ],
        compiler_params=pltpu.CompilerParams(
            collective_id=1, has_side_effects=True, vmem_limit_bytes=58 * 2**20
        ),
    )(parts, out_low, in_low)


def layer_norm(hidden):
    row_mean = jnp.mean(hidden, -1, keepdims=True)
    centred = hidden - row_mean
    inv_std = lax.rsqrt(jnp.mean(centred * centred, -1, keepdims=True) + EPSILON)
    return centred * inv_std, inv_std


def norm_back(gradient, normed, inv_std, gain):
    scaled = gradient * gain
    back = (
        scaled
        - jnp.mean(scaled, -1, keepdims=True)
        - normed * jnp.mean(scaled * normed, -1, keepdims=True)
    ) * inv_std
    return back, jnp.sum(gradient * normed, 0), jnp.sum(gradient, 0)


def mm(form, a, b):
    return jnp.einsum(form, a, b, preferred_element_type=F32)


def body(n, nz, inputs, lengths, wq, wk, wv, wo, we, wr, qb, vb, eb, ob, rb, g1, s1, g2, s2, cotangent):
    z, c = lax.axis_index("ctx"), lax.axis_index("tp")
    s = lax.axis_index("shard")
    seqs, block, model = inputs.shape
    rows = wq.shape[0]
    heads_half = qb.shape[0]
    heads = 2 * heads_half
    hidden_half = we.shape[1]

    def split(w):
        return w.reshape(rows, -1, UNIT).swapaxes(0, 1)

    own = jnp.concatenate([split(w) for w in (wq, wk, wv, wo.T, we, wr.T)], 0)
    units = own.shape[0]
    e_units = hidden_half // UNIT
    packed = jnp.concatenate([v.reshape(-1) for v in (qb, vb, eb, ob, rb, g1, s1, g2, s2)])
    packed = lax.all_gather(packed, ("shard", "tp"), axis=0).astype(F32).reshape(n, 2, -1)
    sizes = [v.size for v in (qb, vb, eb, ob, rb, g1, s1, g2, s2)]
    starts = [sum(sizes[:i]) for i in range(len(sizes))]

    def unpack(i, shape):
        piece = packed[:, :, starts[i] : starts[i] + sizes[i]]
        if shape is None:
            return piece[:, 0].reshape(-1)
        return piece.reshape(n, 2, shape[0], shape[1]).transpose(1, 2, 0, 3).reshape(-1)

    q_bias, v_bias, e_bias = unpack(0, qb.shape), unpack(1, vb.shape), unpack(2, eb.shape)
    o_bias, r_bias, gain1, shift1, gain2, shift2 = [unpack(i, None) for i in range(3, 9)]

    full, x_low, cot = gather(n, nz, own, inputs.astype(BF16), cotangent.astype(BF16))
    length = lengths[2 * z + c]
    slots = nz * block
    live = jnp.arange(slots) < length
    w_all = [full[:, i].transpose(1, 0, 2).reshape(model, -1) for i in range(4)]
    we_f = full[:, 4 : 4 + e_units].transpose(2, 0, 1, 3).reshape(model, -1)
    wr_f = full[:, 4 + e_units :].transpose(2, 0, 1, 3).reshape(model, -1)
    q = (mm("td,dc->tc", x_low, w_all[0]) + q_bias).astype(BF16)
    k = mm("td,dc->tc", x_low, w_all[1]).astype(BF16)
    v = (mm("td,dc->tc", x_low, w_all[2]) + v_bias).astype(BF16)
    qh, kh, vh = [a.reshape(slots, heads, HD) for a in (q, k, v)]
    scores = mm("qhe,khe->hqk", qh, kh) * HD**-0.5
    scores = jnp.where(live[None, None, :], scores, MASKED)
    probs = jax.nn.softmax(scores, -1)
    p_low = probs.astype(BF16)
    o = mm("hqk,khe->qhe", p_low, vh).reshape(slots, model).astype(BF16)
    first = x_low.astype(F32) + mm("tc,dc->td", o, w_all[3]) + o_bias
    n1, r1 = layer_norm(first)
    u = n1 * gain1 + shift1
    u_low = u.astype(BF16)
    pre = mm("td,df->tf", u_low, we_f) + e_bias
    gelu = lambda t: jax.nn.gelu(t, approximate=False)
    h = gelu(pre).astype(BF16)
    second = u + mm("tf,df->td", h, wr_f) + r_bias
    n2, r2 = layer_norm(second)
    out = n2 * gain2 + shift2

    grad = cot.astype(F32) * live[:, None].astype(F32)
    dsecond, dgain2, dshift2 = norm_back(grad, n2, r2, gain2)
    dz = dsecond.astype(BF16)
    drb = jnp.sum(dz.astype(F32), 0)
    dwr = mm("td,tf->df", dz, h)
    dh = mm("td,df->tf", dz, wr_f)
    dpre = jax.vjp(gelu, pre)[1](dh)[0].astype(BF16)
    deb = jnp.sum(dpre.astype(F32), 0)
    dwe = mm("td,tf->df", u_low, dpre)
    du = dsecond + mm("tf,df->td", dpre, we_f)
    dfirst, dgain1, dshift1 = norm_back(du, n1, r1, gain1)
    db = dfirst.astype(BF16)
    dob = jnp.sum(db.astype(F32), 0)
    dwo = mm("td,tc->dc", db, o)
    do = mm("td,dc->tc", db, w_all[3]).astype(BF16).reshape(slots, heads, HD)
    dv = mm("hqk,qhe->khe", p_low, do).reshape(slots, model).astype(BF16)
    dp = mm("qhe,khe->hqk", do, vh)
    ds = (probs * (dp - jnp.sum(dp * probs, -1, keepdims=True))).astype(BF16)
    dq = (mm("hqk,khe->qhe", ds, kh) * HD**-0.5).reshape(slots, model).astype(BF16)
    dk = (mm("hqk,qhe->khe", ds, qh) * HD**-0.5).reshape(slots, model).astype(BF16)
    dqb = jnp.sum(dq.astype(F32), 0)
    dvb = jnp.sum(dv.astype(F32), 0)
    dws = [mm("td,tc->dc", x_low, t) for t in (dq, dk, dv)]
    dx = dfirst + mm("tc,dc->td", dq, w_all[0]) + mm("tc,dc->td", dk, w_all[1]) + mm("tc,dc->td", dv, w_all[2])

    def unit_form(w):
        return w.astype(BF16).reshape(model, 2, -1, UNIT).transpose(1, 2, 0, 3)

    order = [unit_form(w) for w in (dwr, dwe, dwo, *dws)]
    parts = jnp.concatenate(order, 1)
    grads, outs, ins = reduce(n, nz, parts, out.astype(BF16), dx.astype(BF16))
    grads = grads.astype(F32)

    def joined(i, count):
        return grads[i : i + count].swapaxes(0, 1).reshape(rows, -1)

    dwr_s, dwe_s = joined(0, e_units), joined(e_units, e_units)
    dwo_s, dwq_s, dwk_s, dwv_s = [joined(2 * e_units + i, 1) for i in range(4)]
    small = jnp.concatenate([dqb, dvb, deb, dob, drb, dgain1, dshift1, dgain2, dshift2])
    small = lax.psum(small, ("shard", "ctx", "tp"))
    per = model // n
    he = HD // n
    vectors = []
    at = 0
    for size, heads_of in ((model, heads), (model, heads), (2 * hidden_half, eb.shape[0] * 2)):
        m = small[at : at + size].reshape(2, heads_of // 2, n, he)
        m = lax.dynamic_slice(m, (c, 0, s, 0), (1, heads_of // 2, 1, he))
        vectors.append(m.reshape(heads_of // 2, he))
        at += size
    for _ in range(6):
        vectors.append(lax.dynamic_slice(small, (at + s * per,), (per,)))
        at += model
    return (
        outs.astype(F32), ins.astype(F32),
        dwq_s, dwk_s, dwv_s, dwo_s.T, dwe_s, dwr_s.T, *vectors,
    )


def solution(mesh):
    w, wt, v = P("shard", "tp"), P("tp", "shard"), P("shard")
    rows = P("shard", "ctx", None)
    return jax.shard_map(
        functools.partial(body, mesh.shape["shard"], mesh.shape["ctx"]),
        mesh=mesh,
        in_specs=(rows, v, w, w, w, wt, w, wt, wt, wt, wt, v, v, v, v, v, v, rows),
        out_specs=(rows, rows, w, w, w, wt, w, wt, wt, wt, wt, v, v, v, v, v, v),
        check_vma=False,
    )
```

```python
import functools

import jax
import jax.numpy as jnp
from jax import lax
from jax.experimental import pallas as pl
from jax.experimental.pallas import tpu as pltpu
from jax.sharding import PartitionSpec as P

HD = 64
UNIT = 512
SUB = 256
EPSILON = 1e-05
MASKED = -1e30
MESH = pl.DeviceIdType.MESH
F32 = jnp.float32
BF16 = jnp.bfloat16
DMA = pltpu.SemaphoreType.DMA
ANY = pl.BlockSpec(memory_space=pl.ANY)
VMEM = pl.BlockSpec(memory_space=pltpu.VMEM)
SMEM = pl.BlockSpec(memory_space=pltpu.SMEM)


def place():
    return lax.axis_index("shard"), lax.axis_index("ctx"), lax.axis_index("tp")


def rcopy(src, dst, send, recv, dev):
    return pltpu.make_async_remote_copy(
        src_ref=src, dst_ref=dst, send_sem=send, recv_sem=recv, device_id=dev, device_id_type=MESH
    )


def lcopy(src, dst, sem):
    return pltpu.make_async_copy(src, dst, sem)


def greet(devices):
    barrier = pltpu.get_barrier_semaphore()
    for dev in devices:
        pl.semaphore_signal(barrier, inc=1, device_id=dev, device_id_type=MESH)
    pl.semaphore_wait(barrier, len(devices))


def rows_at(i, size):
    return pl.ds(pl.multiple_of(i * size, size), size)


def mm(a, b):
    return jnp.dot(a, b, preferred_element_type=F32)


def mm_nt(a, b):
    return lax.dot_general(a, b, (((1,), (1,)), ((), ())), preferred_element_type=F32)


def mm_tn(a, b):
    return lax.dot_general(a, b, (((0,), (0,)), ((), ())), preferred_element_type=F32)


def loop(count, fn):
    def step(i, carry):
        fn(i)
        return carry

    lax.fori_loop(0, count, step, 0)


def mean(v):
    return jnp.mean(v, -1, keepdims=True)


def forward_kernel(
    n, nz,
    len_ref, x_ref, g_ref, wq_ref, wk_ref, wv_ref, wo_ref, we_ref, wr_ref, pk_ref,
    full_ref, x_out, q_out, k_out, v_out, o_out, lse_out, n1_out, r1_out, u_out, h_out, gp_out,
    ds_out, dz_out, y_out, vec_out, small_out,
    own, wo_in, wr_in, xin, act_low, xv, cotv, qkv, o_v, lse_v, n1_v, r1_v, u_v, ulow_v, h_v, gp_v, acc,
    dz_v, y_v, wbuf, pkall, bias, vec, small,
    own_send, own_recv, fwd_send, fwd_recv, core_send, core_recv, act_send, act_recv,
    pk_send, pk_recv, in_sem, act_sem, fetch_sem, out_sem,
):
    s, z, c = place()
    units, rows, width = own.shape
    half = rows // 2
    model = rows * n
    slots = xv.shape[0]
    block = slots // nz
    e_units = we_ref.shape[1] // width
    group = [(s ^ k, z, c if j == 0 else 1 - c) for k in range(n) for j in range(2) if k + j > 0]
    greet(group + [(s, lax.rem(z + k, nz), c) for k in range(1, nz)])
    mine = rows_at(s, rows)
    zrows = rows_at(z, block)

    ins = [lcopy(r, own.at[i], in_sem.at[i]) for i, r in enumerate((wq_ref, wk_ref, wv_ref))]
    ins += [
        lcopy(we_ref.at[:, pl.ds(j * width, width)], own.at[4 + j], in_sem.at[3 + j]) for j in range(e_units)
    ]
    ins_o = lcopy(wo_ref, wo_in, in_sem.at[3 + e_units])
    ins_r = lcopy(wr_ref, wr_in, in_sem.at[4 + e_units])

    def to(k):
        return lax.rem(z + k, nz)

    def act_load(which, k):
        src = (x_ref, g_ref)[which]
        return lcopy(src.at[2 * to(k) + c], xin.at[k], act_sem.at[k])

    def act(which, k):
        dst = (xv, cotv)[which]
        return rcopy(
            act_low.at[which, k], dst.at[zrows, :], act_send.at[which, k], act_recv.at[which, k], (s, to(k), c)
        )

    def act_in(which, k):
        dst = (xv, cotv)[which]
        src = lax.rem(z + nz - k, nz)
        at = dst.at[rows_at(src, block), :]
        return rcopy(at, at, act_send.at[which, k], act_recv.at[which, k], (s, src, c))

    def act_share(which):
        for k in range(1, nz):
            act_load(which, k).wait()
            act_low[which, k] = xin[k].astype(BF16)
            act(which, k).start()
        act_load(which, 0).wait()
        (xv, cotv)[which][zrows, :] = xin[0].astype(BF16)

    for k in range(1, nz):
        act_load(0, k).start()
    for i in ins:
        i.start()
    act_load(0, 0).start()
    ins_o.start()
    ins_r.start()

    def pk_copy(k, j):
        return rcopy(
            pk_ref, pkall.at[s, c], pk_send.at[k, j], pk_recv.at[k, j], (s ^ k, z, c if j == 0 else 1 - c)
        )

    def pk_in(k, j):
        at = pkall.at[s ^ k, c if j == 0 else 1 - c]
        return rcopy(at, at, pk_send.at[k, j], pk_recv.at[k, j], (s ^ k, z, c if j == 0 else 1 - c))

    pk_pairs = [(k, j) for k in range(n) for j in range(2) if k + j > 0]
    for k, j in pk_pairs:
        pk_copy(k, j).start()
    pkall[s, c] = pk_ref[...]

    direct = [1, 2] if n == 4 else list(range(1, n))

    def own_copy(u, k):
        return rcopy(
            own.at[u], full_ref.at[c, u, mine, :], own_send.at[u, k], own_recv.at[u, k], (s ^ k, z, c)
        )

    def own_in(u, k):
        at = full_ref.at[c, u, rows_at(s ^ k, rows), :]
        return rcopy(at, at, own_send.at[u, k], own_recv.at[u, k], (s ^ k, z, c))

    def half_at(k, h):
        return pl.ds(pl.multiple_of((s ^ k) * rows + h * half, half), half)

    def fwd_copy(u, h):
        at = full_ref.at[c, u, half_at(2 - h, h), :]
        return rcopy(at, at, fwd_send.at[u, h], fwd_recv.at[u, h], (s ^ (1 + h), z, c))

    def fwd_in(u, h):
        at = full_ref.at[c, u, half_at(3, h), :]
        return rcopy(at, at, fwd_send.at[u, h], fwd_recv.at[u, h], (s ^ (1 + h), z, c))

    def core_copy(u, k):
        at = full_ref.at[c, u, rows_at(s ^ k, rows), :]
        return rcopy(at, at, core_send.at[u, k], core_recv.at[u, k], (s, z, 1 - c))

    def core_in(u, k):
        at = full_ref.at[1 - c, u, rows_at(s ^ k, rows), :]
        return rcopy(at, at, core_send.at[u, k], core_recv.at[u, k], (s, z, 1 - c))

    ahead = 2
    for i in ins[:ahead]:
        i.wait()
    for u in range(ahead):
        for k in direct:
            own_copy(u, k).start()
    act_share(0)
    for k in range(nz):
        act_load(1, k).start()
    for i in ins[ahead:]:
        i.wait()
    ins_o.wait()
    own[3] = wo_in[...].T
    ins_r.wait()

    def turn(j):
        own[4 + e_units + j] = wr_in[rows_at(j, width), :].T

    loop(e_units, turn)
    keep = lcopy(own, full_ref.at[c, :, mine, :], in_sem.at[5 + e_units])
    keep.start()
    share = rcopy(
        own, full_ref.at[c, :, mine, :], core_send.at[units, 0], core_recv.at[units, 0], (s, z, 1 - c)
    )
    share.start()
    theirs = full_ref.at[1 - c, :, mine, :]
    share_in = rcopy(theirs, theirs, core_send.at[units, 0], core_recv.at[units, 0], (s, z, 1 - c))
    act_share(1)

    for k, j in pk_pairs:
        pk_in(k, j).wait_recv()
    wide = pk_ref.shape[1]
    he = HD // n
    bias[...] = jnp.zeros_like(bias)
    vec[...] = jnp.zeros_like(vec)

    def place_one(sh):
        r = lax.broadcasted_iota(jnp.int32, (wide, width), 0)
        col = lax.broadcasted_iota(jnp.int32, (wide, width), 1)
        hit = jnp.logical_and(r < width // n, col == (r // he) * HD + sh * he + r % he)
        pick = jnp.where(hit, 1.0, 0.0).astype(BF16)
        for j in range(2):
            bias[j] += mm(pkall[sh, j], pick)
        r = lax.broadcasted_iota(jnp.int32, (wide, model), 0)
        col = lax.broadcasted_iota(jnp.int32, (wide, model), 1)
        hit = jnp.logical_and(r < rows, col == sh * rows + r)
        vec[...] += mm(pkall[sh, 0], jnp.where(hit, 1.0, 0.0).astype(BF16))

    loop(n, place_one)
    small[...] = jnp.zeros_like(small)
    vec_copy = lcopy(vec, vec_out, out_sem.at[0])
    vec_copy.start()
    length = len_ref[2 * z + c]
    live_keys = lax.broadcasted_iota(jnp.int32, (1, slots), 1) < length
    lane = lax.broadcasted_iota(jnp.int32, (slots, 128), 1)
    outs = []

    def fetch(u):
        return lcopy(full_ref.at[:, u], wbuf.at[lax.rem(u, 2)], fetch_sem.at[lax.rem(u, 2)])

    def ready(u):
        @pl.when(u == 0)
        def _():
            keep.wait()
            share_in.wait_recv()

        for k in range(1, n):
            core_in(u, k).wait_recv()

    def attention(p):
        hf, at = p // 4, rows_at(lax.rem(p, 4), 128)
        q, k, v = qkv[0, hf, :, at], qkv[1, hf, :, at], qkv[2, hf, :, at]
        out = None
        for h in range(2):
            part = lane < HD if h == 0 else lane >= HD
            scores = mm_nt(jnp.where(part, q, 0), k) * HD ** (-0.5)
            scores = jnp.where(live_keys, scores, MASKED)
            peak = jnp.max(scores, -1, keepdims=True)
            e = jnp.exp(scores - peak)
            total = jnp.sum(e, -1, keepdims=True)
            term = mm((e * (1.0 / total)).astype(BF16), jnp.where(part, v, 0))
            out = term if out is None else out + term
            lse_v[...] = jnp.where(lane == 2 * p + h, peak + jnp.log(total), lse_v[...])
        o_v[hf, :, at] = out.astype(BF16)

    lse_v[...] = jnp.zeros_like(lse_v)
    rb = 128

    def compute(u):
        w = wbuf.at[lax.rem(u, 2)]

        @pl.when(u == 0)
        def _():
            for k in range(1, nz):
                act_in(0, k).wait_recv()

        @pl.when(u < 3)
        def _():
            def one(hf):
                add = jnp.where(u == 0, bias[hf, 0:1, :], jnp.where(u == 2, bias[hf, 1:2, :], 0.0))
                qkv[u, hf] = (mm(xv[...], w[hf]) + add).astype(BF16)

            loop(2, one)

        @pl.when(u == 2)
        def _():
            loop(4, attention)

        @pl.when(u == 3)
        def _():
            loop(4, lambda p: attention(p + 4))
            acc[...] = mm_nt(o_v[0], w[0]) + xv[...].astype(F32)
            acc[...] += mm_nt(o_v[1], w[1])

            def norm(i):
                at = rows_at(i, rb)
                first = acc[at, :] + vec[8:9, :]
                centred = first - mean(first)
                inv = lax.rsqrt(mean(centred * centred) + EPSILON)
                n1 = centred * inv
                n1_v[at, :] = n1
                r1_v[at, :] = jnp.broadcast_to(inv, (rb, 128))
                up = n1 * vec[10:11, :] + vec[11:12, :]
                ulow_v[at, :] = up.astype(BF16)
                u_v[at, :] = up

            loop(slots // rb, norm)
            for i, (src, dst) in enumerate(
                ((qkv.at[0], q_out), (qkv.at[1], k_out), (qkv.at[2], v_out), (o_v, o_out), (lse_v, lse_out),
                 (n1_v, n1_out), (r1_v, r1_out), (ulow_v, u_out), (xv, x_out))
            ):
                lcopy(src, dst, out_sem.at[1 + i]).start()

        @pl.when(jnp.logical_and(u >= 4, u < 4 + e_units))
        def _():
            j = u - 4

            def one(hf):
                pre = mm(ulow_v[...], w[hf]) + bias[hf, pl.ds(2 + j, 1), :]
                phi = 0.5 * (1.0 + lax.erf(pre * 0.7071067811865476))
                h_v[j, hf] = (pre * phi).astype(BF16)
                gp_v[j, hf] = (phi + pre * jnp.exp(-0.5 * pre * pre) * 0.3989422804014327).astype(BF16)

            loop(2, one)
            lcopy(h_v.at[j], h_out.at[j], out_sem.at[10]).start()
            lcopy(gp_v.at[j], gp_out.at[j], out_sem.at[11]).start()
            lcopy(h_v.at[j], h_out.at[j], out_sem.at[10]).wait()
            lcopy(gp_v.at[j], gp_out.at[j], out_sem.at[11]).wait()

        @pl.when(u >= 4 + e_units)
        def _():
            j = u - 4 - e_units
            u_v[...] += mm_nt(h_v[j, 0], w[0])
            u_v[...] += mm_nt(h_v[j, 1], w[1])

    def step(u):
        @pl.when(u < units)
        def _():
            @pl.when(u + ahead < units)
            def _():
                for k in direct:
                    own_copy(u + ahead, k).start()

            for k in direct:
                own_in(u, k).wait_recv()
                if n == 4:
                    fwd_copy(u, 2 - k).start()
                core_copy(u, k).start()

        if n == 4:
            @pl.when(jnp.logical_and(u > 0, u <= units))
            def _():
                for h in range(2):
                    fwd_in(u - 1, h).wait_recv()
                core_copy(u - 1, 3).start()

        @pl.when(u >= 2)
        def _():
            fetch(u - 2).wait()
            compute(u - 2)

        @pl.when(jnp.logical_and(u > 0, u <= units))
        def _():
            ready(u - 1)
            fetch(u - 1).start()

    loop(units + 2, step)

    for k in range(1, nz):
        act_in(1, k).wait_recv()

    def norm2(i):
        at = rows_at(i, rb)
        second = u_v[at, :] + vec[9:10, :]
        centred = second - mean(second)
        inv = lax.rsqrt(mean(centred * centred) + EPSILON)
        n2 = centred * inv
        gain = vec[12:13, :]
        y_v[at, :] = (n2 * gain + vec[13:14, :]).astype(BF16)
        row = lax.broadcasted_iota(jnp.int32, (rb, 1), 0) + i * rb
        grad = jnp.where(row < length, cotv[at, :].astype(F32), 0.0)
        scaled = grad * gain
        back = inv * (scaled - mean(scaled) - n2 * mean(scaled * n2))
        acc[at, :] = back
        low = back.astype(BF16)
        dz_v[at, :] = low
        for r, v in ((14, low.astype(F32)), (20, grad * n2), (22, grad)):
            v = jnp.sum(v, 0, keepdims=True)
            small[r : r + 1, :] += v[:, :width]
            small[r + 1 : r + 2, :] += v[:, width:]

    loop(slots // rb, norm2)
    last = [
        lcopy(src, dst, out_sem.at[12 + i])
        for i, (src, dst) in enumerate(((acc, ds_out), (dz_v, dz_out), (y_v, y_out), (small, small_out)))
    ]
    for i in last:
        i.start()

    def finish(u):
        for k in direct:
            own_copy(u, k).wait_send()
        if n == 4:
            for h in range(2):
                fwd_copy(u, h).wait_send()
        for k in range(1, n):
            core_copy(u, k).wait_send()

    loop(units, finish)
    share.wait_send()
    for k, j in pk_pairs:
        pk_copy(k, j).wait_send()
    for which in range(2):
        for k in range(1, nz):
            act(which, k).wait_send()
    vec_copy.wait()
    for i, (src, dst) in enumerate(
        ((qkv.at[0], q_out), (qkv.at[1], k_out), (qkv.at[2], v_out), (o_v, o_out), (lse_v, lse_out),
         (n1_v, n1_out), (r1_v, r1_out), (ulow_v, u_out), (xv, x_out))
    ):
        lcopy(src, dst, out_sem.at[1 + i]).wait()
    for i in last:
        i.wait()


def forward(n, nz, lengths, inputs, cotangent, wq, wk, wv, wo, we, wr, pk):
    seqs, block, model = inputs.shape
    rows = wq.shape[0]
    e_units = we.shape[1] // UNIT
    units = 4 + 2 * e_units
    slots = nz * block
    by_half = (2, slots, UNIT)
    outs = [
        ((2, units, model, UNIT), BF16), ((slots, model), BF16),
        (by_half, BF16), (by_half, BF16), (by_half, BF16), (by_half, BF16), ((slots, 128), F32),
        ((slots, model), F32), ((slots, 128), F32), ((slots, model), BF16),
        ((e_units, *by_half), BF16), ((e_units, *by_half), BF16),
        ((slots, model), F32), ((slots, model), BF16), ((slots, model), BF16), ((16, model), F32),
        ((24, UNIT), F32),
    ]
    scratch = [
        ((units, rows, UNIT), BF16), (wo.shape, BF16), (wr.shape, BF16), ((nz, block, model), F32),
        ((2, nz, block, model), BF16), ((slots, model), BF16), ((slots, model), BF16), ((3, *by_half), BF16),
        (by_half, BF16), ((slots, 128), F32), ((slots, model), F32), ((slots, 128), F32), ((slots, model), F32),
        ((slots, model), BF16), ((e_units, *by_half), BF16), ((e_units, *by_half), BF16), ((slots, model), F32),
        ((slots, model), BF16), ((slots, model), BF16), ((2, 2, model, UNIT), BF16), ((n, 2, *pk.shape), BF16),
        ((2, 16, UNIT), F32), ((16, model), F32), ((24, UNIT), F32),
    ]
    return pl.pallas_call(
        functools.partial(forward_kernel, n, nz),
        name="gather_and_forward",
        out_shape=[jax.ShapeDtypeStruct(a, b) for a, b in outs],
        in_specs=[SMEM] + [ANY] * 8 + [VMEM],
        out_specs=[ANY] * len(outs),
        scratch_shapes=[pltpu.VMEM(a, b) for a, b in scratch]
        + [
            DMA((units, n)), DMA((units, n)), DMA((units, 2)), DMA((units, 2)),
            DMA((units + 1, n)), DMA((units + 1, n)), DMA((2, nz)), DMA((2, nz)),
            DMA((n, 2)), DMA((n, 2)), DMA((6 + e_units,)), DMA((nz,)), DMA((2,)), DMA((16,)),
        ],
        compiler_params=pltpu.CompilerParams(
            collective_id=0, has_side_effects=True, vmem_limit_bytes=60 * 2**20
        ),
    )(lengths, inputs, cotangent, wq, wk, wv, wo, we, wr, pk)


def backward_kernel(
    n, nz,
    len_ref, full_ref, x_ref, q_ref, k_ref, v_ref, o_ref, lse_ref, n1_ref, r1_ref, u_ref, h_ref, gp_ref,
    ds_ref, dz_ref, y_ref, vec_ref, small_ref,
    grad_ref, ys_ref, dx_ref, small_out, part_ref, got_ref,
    x_v, qkv, o_v, lse_v, n1_v, r1_v, u_v, dz_v, du, do_v, dqkv, wr_v, we_v, h_v, gp_v, dpre, pbuf, small, round_in,
    stage, gstage, total, near, pair_sum, far, up, across, down, block_out, dx_low,
    load_sem, w_sem, part_sem, core_send, core_recv, stage_sem, near_send, near_recv, far_send, far_recv,
    z_send, z_recv, store_sem, act_send, act_recv, pass_send, pass_recv, keep_sem, small_send, small_recv,
):
    s, z, c = place()
    units = part_ref.shape[0]
    subs = 2 * units
    e_units = h_ref.shape[0]
    model = total.shape[1]
    rows = model // n
    half = rows // 2
    slots = x_v.shape[0]
    block = slots // nz
    greet(
        [(s ^ k, z, c) for k in range(1, n)]
        + [(s, z, 1 - c)]
        + [(s, lax.rem(z + k, nz), c) for k in range(1, nz)]
    )
    zrows = rows_at(z, block)
    mates = [(dz_ref, dz_v), (ds_ref, du), (small_ref, small), (u_ref, u_v), (r1_ref, r1_v), (n1_ref, n1_v),
             (o_ref, o_v), (lse_ref, lse_v), (q_ref, qkv.at[0]), (k_ref, qkv.at[1]), (v_ref, qkv.at[2]), (x_ref, x_v)]
    loads = [lcopy(a, b, load_sem.at[i]) for i, (a, b) in enumerate(mates)]

    def load_r(j):
        return [
            lcopy(full_ref.at[:, 4 + e_units + j], wr_v, w_sem.at[0]),
            lcopy(h_ref.at[j], h_v, w_sem.at[1]),
            lcopy(gp_ref.at[j], gp_v, w_sem.at[2]),
        ]

    def load_e(j):
        return lcopy(full_ref.at[:, 4 + j], we_v, w_sem.at[3])

    def load_into(u, buf, i):
        return lcopy(full_ref.at[:, u], buf, w_sem.at[i])

    for i in load_r(0):
        i.start()
    for i in loads:
        i.start()

    def act(which, k):
        src, dst = ((y_ref, ys_ref), (dx_low, dx_ref))[which]
        to = lax.rem(z + k, nz)
        return rcopy(
            src.at[rows_at(to, block), :], dst.at[2 * z + c], act_send.at[which, k], act_recv.at[which, k], (s, to, c)
        )

    def act_in(which, k):
        src = lax.rem(z + nz - k, nz)
        at = (ys_ref, dx_ref)[which].at[2 * src + c]
        return rcopy(at, at, act_send.at[which, k], act_recv.at[which, k], (s, src, c))

    def act_keep(which):
        src, dst = ((y_ref, ys_ref), (dx_low, dx_ref))[which]
        return lcopy(src.at[zrows, :], dst.at[2 * z + c], keep_sem.at[which])

    def pass_copy(which, k):
        at = (ys_ref, dx_ref)[which].at[2 * lax.rem(z + nz - k, nz) + c]
        return rcopy(at, at, pass_send.at[which, k], pass_recv.at[which, k], (s, z, 1 - c))

    def pass_in(which, k):
        at = (ys_ref, dx_ref)[which].at[2 * lax.rem(z + nz - k, nz) + 1 - c]
        return rcopy(at, at, pass_send.at[which, k], pass_recv.at[which, k], (s, z, 1 - c))

    def act_start(which):
        for k in range(1, nz):
            act(which, k).start()
        act_keep(which).start()

    def act_pass(which):
        for k in range(1, nz):
            act_in(which, k).wait_recv()
            pass_copy(which, k).start()
        act_keep(which).wait()
        pass_copy(which, 0).start()

    act_start(0)

    def core_copy(u):
        return rcopy(pbuf.at[0], got_ref.at[u], core_send.at[u], core_recv.at[u], (s, z, 1 - c))

    def core_in(u):
        return rcopy(got_ref.at[u], got_ref.at[u], core_send.at[u], core_recv.at[u], (s, z, 1 - c))

    def part_copy(u):
        return lcopy(pbuf.at[1], part_ref.at[u], part_sem.at[0])

    def free_part(u):
        @pl.when(u > 0)
        def _():
            core_copy(u - 1).wait_send()

    def emit(u, i, value):
        low = value.astype(BF16)
        for b in range(2):
            pbuf[i, b] = low[:, b * SUB : (b + 1) * SUB]

    def produce(u, make):
        free_part(u)

        def one(i):
            emit(u, i, make(lax.rem(1 - c + i, 2)))

            @pl.when(i == 0)
            def _():
                core_copy(u).start()

        loop(2, one)
        part_copy(u).start()
        part_copy(u).wait()

    length = len_ref[2 * z + c]
    live_keys = lax.broadcasted_iota(jnp.int32, (1, slots), 1) < length
    lane = lax.broadcasted_iota(jnp.int32, (slots, 128), 1)
    rb = 128

    def add_small(r, v):
        small[pl.ds(r, 1), :] += v

    def tick_r(j):
        load_e(j).start()
        for i in load_r(j):
            i.wait()

        def one(hf):
            low = (mm(dz_v[...], wr_v[hf]) * gp_v[hf].astype(F32)).astype(BF16)
            dpre[hf] = low
            add_small(4 + hf * e_units + j, jnp.sum(low.astype(F32), 0, keepdims=True))

        loop(2, one)
        produce(2 * j, lambda hf: mm_tn(dz_v[...], h_v[hf]))

    def tick_e(j):
        load_e(j).wait()

        @pl.when(j + 1 < e_units)
        def _():
            for i in load_r(j + 1):
                i.start()

        @pl.when(j + 1 == e_units)
        def _():
            load_into(3, wr_v, 0).start()

        produce(2 * j + 1, lambda hf: mm_tn(u_v[...], dpre[hf]))

        def one(hf):
            du[...] += mm_nt(dpre[hf], we_v[hf])

        loop(2, one)

    def tick_o():
        load_into(1, we_v, 3).start()

        def norm(i):
            at = rows_at(i, rb)
            grad = du[at, :]
            n1 = n1_v[at, :]
            scaled = grad * vec_ref[10:11, :]
            back = r1_v[at, 0:1] * (scaled - mean(scaled) - n1 * mean(scaled * n1))
            du[at, :] = back
            low = back.astype(BF16)
            dz_v[at, :] = low
            for r, v in ((12, low.astype(F32)), (16, grad * n1), (18, grad)):
                v = jnp.sum(v, 0, keepdims=True)
                small[r : r + 1, :] += v[:, :UNIT]
                small[r + 1 : r + 2, :] += v[:, UNIT:]

        loop(slots // rb, norm)
        load_into(3, wr_v, 0).wait()
        produce(2 * e_units, lambda hf: mm_tn(dz_v[...], o_v[hf]))

        def one(hf):
            do_v[hf] = mm(dz_v[...], wr_v[hf]).astype(BF16)

        loop(2, one)
        load_into(0, wr_v, 0).start()

    def attention(p):
        hf, at = p // 4, rows_at(lax.rem(p, 4), 128)
        q, k, v = qkv[0, hf, :, at], qkv[1, hf, :, at], qkv[2, hf, :, at]
        do = do_v[hf, :, at]
        dq = dk = dv = None
        for h in range(2):
            part = lane < HD if h == 0 else lane >= HD
            qh, kh, doh = jnp.where(part, q, 0), jnp.where(part, k, 0), jnp.where(part, do, 0)
            scores = mm_nt(qh, k) * HD ** (-0.5)
            scores = jnp.where(live_keys, scores, MASKED)
            lse = jnp.sum(jnp.where(lane == 2 * p + h, lse_v[...], 0.0), -1, keepdims=True)
            probs = jnp.exp(scores - lse)
            dp = mm_nt(doh, v)
            low = (probs * (dp - jnp.sum(dp * probs, -1, keepdims=True))).astype(BF16)
            tv, tk, tq = mm_tn(probs.astype(BF16), doh), mm_tn(low, qh), mm(low, kh)
            dv, dk, dq = (tv, tk, tq) if h == 0 else (dv + tv, dk + tk, dq + tq)
        dqkv[0, hf, :, at] = (dq * HD ** (-0.5)).astype(BF16)
        dqkv[1, hf, :, at] = (dk * HD ** (-0.5)).astype(BF16)
        dqkv[2, hf, :, at] = dv.astype(BF16)

    def tick_qkv(i, buf, sem, u):
        load_into(u, buf, sem).wait()
        produce(2 * e_units + 1 + u, lambda hf: mm_tn(x_v[...], dqkv[u, hf]))

        def one(hf):
            du[...] += mm_nt(dqkv[u, hf], buf[hf])
            if u != 1:
                add_small(u + hf, jnp.sum(dqkv[u, hf].astype(F32), 0, keepdims=True))

        loop(2, one)

    def compute(t):
        ffn = 2 * e_units

        @pl.when(jnp.logical_and(t < ffn, lax.rem(t, 2) == 0))
        def _():
            tick_r(t // 2)

        @pl.when(jnp.logical_and(t < ffn, lax.rem(t, 2) == 1))
        def _():
            tick_e(t // 2)

        pl.when(t == ffn)(tick_o)

        @pl.when(jnp.logical_and(t > ffn, t <= ffn + 4))
        def _():
            loop(2, lambda i: attention(2 * (t - ffn - 1) + i))

        @pl.when(t == ffn + 5)
        def _():
            tick_qkv(0, wr_v, 0, 0)
            load_into(2, wr_v, 0).start()

        @pl.when(t == ffn + 6)
        def _():
            tick_qkv(1, we_v, 3, 1)

        @pl.when(t == ffn + 7)
        def _():
            tick_qkv(2, wr_v, 0, 2)
            dx_low[...] = du[...].astype(BF16)
            act_start(1)

    def loads_of(w):
        slot = lax.rem(w, 2)
        u, b = w // 2, lax.rem(w, 2)
        return [
            lcopy(part_ref.at[u, b], stage.at[slot], stage_sem.at[slot, 0]),
            lcopy(got_ref.at[u, b], gstage.at[slot], stage_sem.at[slot, 1]),
        ]

    def blk(k):
        return rows_at(s ^ k, rows)

    def blk_half(k, h):
        return pl.ds(pl.multiple_of((s ^ k) * rows + h * half, half), half)

    def near_copy(w, h, i):
        k = (1 + h, 3)[i]
        return rcopy(
            total.at[lax.rem(w, 2), blk_half(k, h), :], near.at[w, h, i],
            near_send.at[w, h, i], near_recv.at[w, h, i], (s ^ (1 + h), z, c),
        )

    def far_copy(w, h):
        return rcopy(
            pair_sum.at[w, h], far.at[w, h], far_send.at[w, h], far_recv.at[w, h], (s ^ (2 - h), z, c)
        )

    def straight(w, k):
        return rcopy(
            total.at[lax.rem(w, 2), blk(k), :], near.at[w, k - 1],
            near_send.at[w, k - 1], near_recv.at[w, k - 1], (s ^ k, z, c),
        )

    def sends_of(w):
        if n == 4:
            return [near_copy(w, h, i) for h in range(2) for i in range(2)]
        return [straight(w, k) for k in range(1, n)]

    def z_to(w, src, dst, i, to):
        return rcopy(src.at[w], dst.at[w], z_send.at[w, i], z_recv.at[w, i], (s, to, c))

    last = nz - 1
    edge = jnp.logical_or(z == 0, z == last)
    inner = jnp.where(z == 0, 1, nz - 2)
    outer = jnp.where(z == 1, 0, last)
    other = jnp.where(z == 1, 2, 1)

    def s0(w):
        @pl.when(lax.rem(w, 2) == 0)
        def _():
            core_in(w // 2).wait_recv()

        for i in loads_of(w):
            i.start()

    def s1(w):
        @pl.when(w >= 2)
        def _():
            for i in sends_of(w - 2):
                i.wait_send()

        for i in loads_of(w):
            i.wait()
        slot = lax.rem(w, 2)

        def add(i):
            at = rows_at(i, 256)
            total[slot, at, :] = (stage[slot, at, :].astype(F32) + gstage[slot, at, :].astype(F32)).astype(BF16)

        loop(model // 256, add)
        for i in sends_of(w):
            i.start()

    def s2(w):
        slot = lax.rem(w, 2)
        for i in sends_of(w):
            i.wait_recv()
        if n == 4:
            for h in range(2):
                pair_sum[w, h] = (
                    total[slot, blk_half(2 - h, h), :].astype(F32) + near[w, h, 1].astype(F32)
                ).astype(BF16)
                far_copy(w, h).start()

    def s3(w):
        slot = lax.rem(w, 2)
        if n == 4:
            for h in range(2):
                far_copy(w, h).wait_recv()
                block_out[w, h * half : (h + 1) * half] = (
                    total[slot, blk_half(0, h), :].astype(F32) + near[w, h, 0].astype(F32) + far[w, h].astype(F32)
                ).astype(BF16)
        else:
            acc = total[slot, blk(0), :].astype(F32)
            for k in range(1, n):
                acc = acc + near[w, k - 1].astype(F32)
            block_out[w] = acc.astype(BF16)

        @pl.when(edge)
        def _():
            z_to(w, block_out, up, 0, inner).start()

    def s4(w):
        @pl.when(jnp.logical_not(edge))
        def _():
            z_to(w, block_out, up, 0, outer).wait_recv()
            block_out[w] = (block_out[w].astype(F32) + up[w].astype(F32)).astype(BF16)
            z_to(w, block_out, across, 1, other).start()

    def s5(w):
        @pl.when(jnp.logical_not(edge))
        def _():
            z_to(w, block_out, across, 1, other).wait_recv()
            down[w] = (block_out[w].astype(F32) + across[w].astype(F32)).astype(BF16)
            z_to(w, down, down, 2, outer).start()

    def s6(w):
        @pl.when(edge)
        def _():
            z_to(w, down, down, 2, inner).wait_recv()

        lcopy(down.at[w], grad_ref.at[w], store_sem.at[w]).start()

    stages = [s0, s1, s2, s3, s4, s5, s6]

    hops = [(s, z, 1 - c)]
    hops += [(s ^ (1 << b), z, c) for b in range(n.bit_length() - 1)]
    hops += [(s, z ^ (1 << b), c) for b in range(nz.bit_length() - 1)]

    def small_copy(i):
        return rcopy(small, round_in.at[i], small_send.at[i], small_recv.at[i], hops[i])

    for i in loads:
        i.wait()
    done = 2 * e_units + 8

    def step(t):
        @pl.when(t < done)
        def _():
            compute(t)

        for i, stage_of in reversed(list(enumerate(stages))):
            @pl.when(jnp.logical_and(t >= i, t - i < subs))
            def _(stage_of=stage_of, i=i):
                stage_of(t - i)

        @pl.when(t == 4)
        def _():
            act_pass(0)

        @pl.when(t == done + 5)
        def _():
            act_pass(1)

        for i in range(len(hops) + 1):
            @pl.when(t == done + i)
            def _(i=i):
                if i > 0:
                    small_copy(i - 1).wait_send()
                    small_copy(i - 1).wait_recv()
                    small[...] += round_in[i - 1]
                if i < len(hops):
                    small_copy(i).start()
                else:
                    lcopy(small, small_out, keep_sem.at[2]).start()

    loop(subs + len(stages) - 1, step)

    def finish(w):
        if n == 4:
            for h in range(2):
                far_copy(w, h).wait_send()

        @pl.when(edge)
        def _():
            z_to(w, block_out, up, 0, inner).wait_send()

        @pl.when(jnp.logical_not(edge))
        def _():
            z_to(w, block_out, across, 1, other).wait_send()
            z_to(w, down, down, 2, outer).wait_send()

        lcopy(down.at[w], grad_ref.at[w], store_sem.at[w]).wait()

    loop(subs, finish)
    core_copy(units - 1).wait_send()
    for w in (subs - 2, subs - 1):
        for i in sends_of(w):
            i.wait_send()
    for which in range(2):
        for k in range(1, nz):
            act(which, k).wait_send()
        for k in range(nz):
            pass_copy(which, k).wait_send()
            pass_in(which, k).wait_recv()
    lcopy(small, small_out, keep_sem.at[2]).wait()


def backward(n, nz, lengths, full, x, q, k, v, o, lse, n1, r1, u, h, gp, ds, dz, y, vec, small):
    _, units, model, width = full.shape
    e_units = h.shape[0]
    rows = model // n
    half = rows // 2
    slots = x.shape[0]
    block = slots // nz
    subs = 2 * units
    by_half = (2, slots, UNIT)
    near = (subs, 2, 2, half, SUB) if n == 4 else (subs, n - 1, rows, SUB)
    near_sems = near[:3] if n == 4 else near[:2]
    far = (subs, 2, half, SUB) if n == 4 else (1, 2, 16, SUB)
    blocks = (subs, rows, SUB)
    hops = 1 + (n.bit_length() - 1) + (nz.bit_length() - 1)
    outs = [
        (blocks, BF16), ((2 * nz, block, model), BF16), ((2 * nz, block, model), BF16), ((24, UNIT), F32),
        ((units, 2, model, SUB), BF16), ((units, 2, model, SUB), BF16),
    ]
    scratch = [
        ((slots, model), BF16), ((3, *by_half), BF16), (by_half, BF16), ((slots, 128), F32), ((slots, model), F32),
        ((slots, 128), F32), ((slots, model), BF16), ((slots, model), BF16), ((slots, model), F32), (by_half, BF16),
        ((3, *by_half), BF16), ((2, model, UNIT), BF16), ((2, model, UNIT), BF16), (by_half, BF16), (by_half, BF16),
        (by_half, BF16), ((2, 2, model, SUB), BF16), ((24, UNIT), F32), ((hops, 24, UNIT), F32),
        ((2, model, SUB), BF16), ((2, model, SUB), BF16), ((2, model, SUB), BF16),
        (near, BF16), (far, BF16), (far, BF16), (blocks, BF16), (blocks, BF16), (blocks, BF16), (blocks, BF16),
        ((slots, model), BF16),
    ]
    return pl.pallas_call(
        functools.partial(backward_kernel, n, nz),
        name="backward_and_reduce",
        out_shape=[jax.ShapeDtypeStruct(a, b) for a, b in outs],
        in_specs=[SMEM] + [ANY] * 15 + [VMEM, ANY],
        out_specs=[ANY] * len(outs),
        scratch_shapes=[pltpu.VMEM(a, b) for a, b in scratch]
        + [
            DMA((12,)), DMA((4,)), DMA((1,)), DMA((units,)), DMA((units,)), DMA((2, 2)),
            DMA(near_sems), DMA(near_sems), DMA((subs, 2)), DMA((subs, 2)),
            DMA((subs, 3)), DMA((subs, 3)), DMA((subs,)),
            DMA((2, nz)), DMA((2, nz)), DMA((2, nz)), DMA((2, nz)), DMA((3,)), DMA((hops,)), DMA((hops,)),
        ],
        compiler_params=pltpu.CompilerParams(
            collective_id=1, has_side_effects=True, vmem_limit_bytes=61 * 2**20
        ),
    )(lengths, full, x, q, k, v, o, lse, n1, r1, u, h, gp, ds, dz, y, vec, small)


def body(n, nz, inputs, lengths, wq, wk, wv, wo, we, wr, qb, vb, eb, ob, rb, g1, s1, g2, s2, cotangent):
    s, c = lax.axis_index("shard"), lax.axis_index("tp")
    rows = wq.shape[0]
    model = rows * n
    e_units = we.shape[1] // UNIT
    wide = max(rows, 128)

    def lines(v, count):
        v = v.reshape(count, -1)
        return jnp.pad(v, ((0, 0), (0, wide - v.shape[1])))

    blank = jnp.zeros((2, wide), BF16)
    pk = jnp.concatenate(
        [lines(qb, 1), lines(vb, 1), lines(eb, e_units), blank]
        + [lines(v, 1) for v in (ob, rb, g1, s1, g2, s2)]
        + [blank]
    )
    (full, x, q, k, v, o, lse, n1, r1, u, h, gp, ds, dz, y, vec, small) = forward(
        n, nz, lengths, inputs, cotangent, wq, wk, wv, wo, we, wr, pk
    )
    grads, ys, dx, small, _, _ = backward(
        n, nz, lengths, full, x, q, k, v, o, lse, n1, r1, u, h, gp, ds, dz, y, vec, small
    )

    def joined(picks):
        return jnp.concatenate([grads[i] for i in picks], 1).astype(F32)

    dwr = joined([4 * j + b for j in range(e_units) for b in range(2)])
    dwe = joined([4 * j + 2 + b for j in range(e_units) for b in range(2)])
    at = 4 * e_units
    dwo, dwq, dwk, dwv = [joined([at + 2 * i, at + 2 * i + 1]) for i in range(4)]
    he = HD // n
    small = small.reshape(-1)
    vectors = []
    at = 0
    for v in (qb, vb, eb):
        m = small[at : at + 2 * v.shape[0] * HD].reshape(2, v.shape[0], n, he)
        m = lax.dynamic_slice(m, (c, 0, s, 0), (1, v.shape[0], 1, he))
        vectors.append(m.reshape(v.shape))
        at += 2 * v.shape[0] * HD
    for _ in range(6):
        vectors.append(lax.dynamic_slice(small, (at + s * rows,), (rows,)))
        at += model
    return (ys.astype(F32), dx.astype(F32), dwq, dwk, dwv, dwo.T, dwe, dwr.T, *vectors)


def solution(mesh):
    w, wt, v = P("shard", "tp"), P("tp", "shard"), P("shard")
    rows = P("shard", "ctx", None)
    return jax.shard_map(
        functools.partial(body, mesh.shape["shard"], mesh.shape["ctx"]),
        mesh=mesh,
        in_specs=(rows, v, w, w, w, wt, w, wt, wt, wt, wt, v, v, v, v, v, v, rows),
        out_specs=(rows, rows, w, w, w, wt, w, wt, wt, wt, wt, v, v, v, v, v, v),
        check_vma=False,
    )
```

```python
import functools

import jax
import jax.numpy as jnp
from jax import lax
from jax.experimental import pallas as pl
from jax.experimental.pallas import tpu as pltpu
from jax.sharding import PartitionSpec as P

HD = 64
UNIT = 512
SUB = 256
SLOTS = 4
LAGS = (0, 5, 3, 1, 11, 9, 7)
PACE = 5
PASS = 24
PIECES = 8
ACTS = (0, 10)
EPSILON = 1e-05
MASKED = -1e30
MESH = pl.DeviceIdType.MESH
F32 = jnp.float32
BF16 = jnp.bfloat16
DMA = pltpu.SemaphoreType.DMA
ANY = pl.BlockSpec(memory_space=pl.ANY)
VMEM = pl.BlockSpec(memory_space=pltpu.VMEM)
SMEM = pl.BlockSpec(memory_space=pltpu.SMEM)


def place():
    return lax.axis_index("shard"), lax.axis_index("ctx"), lax.axis_index("tp")


def rcopy(src, dst, send, recv, dev):
    return pltpu.make_async_remote_copy(
        src_ref=src, dst_ref=dst, send_sem=send, recv_sem=recv, device_id=dev, device_id_type=MESH
    )


def lcopy(src, dst, sem):
    return pltpu.make_async_copy(src, dst, sem)


def greet(devices):
    barrier = pltpu.get_barrier_semaphore()
    for dev in devices:
        pl.semaphore_signal(barrier, inc=1, device_id=dev, device_id_type=MESH)
    pl.semaphore_wait(barrier, len(devices))


def rows_at(i, size):
    return pl.ds(pl.multiple_of(i * size, size), size)


def mm(a, b):
    return jnp.dot(a, b, preferred_element_type=F32)


def mm_nt(a, b):
    return lax.dot_general(a, b, (((1,), (1,)), ((), ())), preferred_element_type=F32)


def mm_tn(a, b):
    return lax.dot_general(a, b, (((0,), (0,)), ((), ())), preferred_element_type=F32)


def loop(count, fn):
    def step(i, carry):
        fn(i)
        return carry

    lax.fori_loop(0, count, step, 0)


def mean(v):
    return jnp.mean(v, -1, keepdims=True)


def forward_kernel(
    n, nz,
    len_ref, x_ref, g_ref, wq_ref, wk_ref, wv_ref, wo_ref, we_ref, wr_ref,
    qb_ref, vb_ref, eb_ref, ob_ref, rb_ref, g1_ref, s1_ref, g2_ref, s2_ref,
    full_ref, x_out, q_out, k_out, v_out, o_out, p_out, n1_out, r1_out, u_out, h_out, gp_out,
    ds_out, dz_out, y_out, vec_out, small_out,
    own, wo_in, wr_in, xin, act_low, xv, cotv, qkv, o_v, p_v, n1_v, r1_v, u_v, ulow_v, h_v, gp_v, acc,
    dz_v, y_v, wbuf, pk_ref, pk_wide, pkall, head_bias, bias, vec, small,
    own_send, own_recv, fwd_send, fwd_recv, core_send, core_recv, act_send, act_recv,
    pk_send, pk_recv, in_sem, act_sem, fetch_sem, out_sem, p_sem,
):
    s, z, c = place()
    units, rows, width = own.shape
    half = rows // 2
    model = rows * n
    slots = xv.shape[0]
    block = slots // nz
    e_units = we_ref.shape[1] // width
    group = [(s ^ k, z, c if j == 0 else 1 - c) for k in range(n) for j in range(2) if k + j > 0]
    mine = rows_at(s, rows)
    zrows = rows_at(z, block)

    ins = [lcopy(r, own.at[i], in_sem.at[i]) for i, r in enumerate((wq_ref, wk_ref, wv_ref))]
    ins += [
        lcopy(we_ref.at[:, pl.ds(j * width, width)], own.at[4 + j], in_sem.at[3 + j]) for j in range(e_units)
    ]
    ins_o = lcopy(wo_ref, wo_in, in_sem.at[3 + e_units])
    ins_r = lcopy(wr_ref, wr_in, in_sem.at[4 + e_units])

    def to(k):
        return lax.rem(z + k, nz)

    def act_load(which, k):
        src = (x_ref, g_ref)[which]
        return lcopy(src.at[2 * to(k) + c], xin.at[k], act_sem.at[k])

    def act(which, k):
        dst = (xv, cotv)[which]
        return rcopy(
            act_low.at[which, k], dst.at[zrows, :], act_send.at[which, k], act_recv.at[which, k], (s, to(k), c)
        )

    def act_in(which, k):
        dst = (xv, cotv)[which]
        src = lax.rem(z + nz - k, nz)
        at = dst.at[rows_at(src, block), :]
        return rcopy(at, at, act_send.at[which, k], act_recv.at[which, k], (s, src, c))

    def act_share(which):
        for k in range(1, nz):
            act_load(which, k).wait()
            act_low[which, k] = xin[k].astype(BF16)
            act(which, k).start()
        act_load(which, 0).wait()
        (xv, cotv)[which][zrows, :] = xin[0].astype(BF16)

    for k in range(1, nz):
        act_load(0, k).start()
    for i in ins:
        i.start()
    act_load(0, 0).start()
    ins_o.start()
    ins_r.start()

    he = HD // n
    heads = [qb_ref, vb_ref, eb_ref]
    head_rows = sum(r.shape[0] for r in heads)
    pk_wide[...] = jnp.zeros_like(pk_wide)
    at = 0
    for r in heads:
        pk_wide[at : at + r.shape[0], :he] = r[...].astype(F32)
        at += r.shape[0]
    for i, r in enumerate((ob_ref, rb_ref, g1_ref, s1_ref, g2_ref, s2_ref)):
        pk_wide[at + 8 + i : at + 9 + i, :rows] = r[...].reshape(1, rows).astype(F32)
    pk_ref[...] = pk_wide[...].astype(BF16)
    greet(group + [(s, lax.rem(z + k, nz), c) for k in range(1, nz)])

    def pk_copy(k, j):
        return rcopy(
            pk_ref, pkall.at[s, c], pk_send.at[k, j], pk_recv.at[k, j], (s ^ k, z, c if j == 0 else 1 - c)
        )

    def pk_in(k, j):
        at = pkall.at[s ^ k, c if j == 0 else 1 - c]
        return rcopy(at, at, pk_send.at[k, j], pk_recv.at[k, j], (s ^ k, z, c if j == 0 else 1 - c))

    pk_pairs = [(k, j) for k in range(n) for j in range(2) if k + j > 0]
    for k, j in pk_pairs:
        pk_copy(k, j).start()
    pkall[s, c] = pk_ref[...]

    direct = [1, 2] if n == 4 else list(range(1, n))

    def own_copy(u, k):
        return rcopy(
            own.at[u], full_ref.at[c, u, mine, :], own_send.at[u, k], own_recv.at[u, k], (s ^ k, z, c)
        )

    def own_in(u, k):
        at = full_ref.at[c, u, rows_at(s ^ k, rows), :]
        return rcopy(at, at, own_send.at[u, k], own_recv.at[u, k], (s ^ k, z, c))

    def half_at(k, h):
        return pl.ds(pl.multiple_of((s ^ k) * rows + h * half, half), half)

    def fwd_copy(u, h):
        at = full_ref.at[c, u, half_at(2 - h, h), :]
        return rcopy(at, at, fwd_send.at[u, h], fwd_recv.at[u, h], (s ^ (1 + h), z, c))

    def fwd_in(u, h):
        at = full_ref.at[c, u, half_at(3, h), :]
        return rcopy(at, at, fwd_send.at[u, h], fwd_recv.at[u, h], (s ^ (1 + h), z, c))

    def core_copy(u, k):
        at = full_ref.at[c, u, rows_at(s ^ k, rows), :]
        return rcopy(at, at, core_send.at[u, k], core_recv.at[u, k], (s, z, 1 - c))

    def core_in(u, k):
        at = full_ref.at[1 - c, u, rows_at(s ^ k, rows), :]
        return rcopy(at, at, core_send.at[u, k], core_recv.at[u, k], (s, z, 1 - c))

    ahead = 2
    for i in ins[:ahead]:
        i.wait()
    for u in range(ahead):
        for k in direct:
            own_copy(u, k).start()
    act_share(0)
    for k in range(nz):
        act_load(1, k).start()
    for i in ins[ahead:]:
        i.wait()
    ins_o.wait()
    own[3] = wo_in[...].T
    ins_r.wait()

    def turn(j):
        own[4 + e_units + j] = wr_in[rows_at(j, width), :].T

    loop(e_units, turn)
    keep = lcopy(own, full_ref.at[c, :, mine, :], in_sem.at[5 + e_units])
    keep.start()
    share = rcopy(
        own, full_ref.at[c, :, mine, :], core_send.at[units, 0], core_recv.at[units, 0], (s, z, 1 - c)
    )
    share.start()
    theirs = full_ref.at[1 - c, :, mine, :]
    share_in = rcopy(theirs, theirs, core_send.at[units, 0], core_recv.at[units, 0], (s, z, 1 - c))
    act_share(1)

    for k, j in pk_pairs:
        pk_in(k, j).wait_recv()
    wide = pk_ref.shape[1]
    head_bias[...] = jnp.zeros_like(head_bias)
    vec[...] = jnp.zeros_like(vec)

    def place_one(sh):
        r = lax.broadcasted_iota(jnp.int32, (wide, width), 0)
        col = lax.broadcasted_iota(jnp.int32, (wide, width), 1)
        pick = jnp.where(jnp.logical_and(r < he, col % HD == sh * he + r), 1.0, 0.0).astype(BF16)
        row = lax.broadcasted_iota(jnp.int32, (head_rows, width), 0)
        col = lax.broadcasted_iota(jnp.int32, (head_rows, width), 1)
        own_head = col // HD == row % 8
        for j in range(2):
            head_bias[j] += jnp.where(own_head, mm(pkall[sh, j, :head_rows, :], pick), 0.0)
        r = lax.broadcasted_iota(jnp.int32, (wide, model), 0)
        col = lax.broadcasted_iota(jnp.int32, (wide, model), 1)
        hit = jnp.logical_and(r < rows, col == sh * rows + r)
        vec[...] += mm(pkall[sh, 0, head_rows:, :], jnp.where(hit, 1.0, 0.0).astype(BF16))

    loop(n, place_one)
    for j in range(2):
        for i in range(head_rows // 8):
            bias[i : i + 1, j * width : (j + 1) * width] = jnp.sum(
                head_bias[j, 8 * i : 8 * i + 8, :], 0, keepdims=True
            )
    small[...] = jnp.zeros_like(small)
    vec_copy = lcopy(vec, vec_out, out_sem.at[0])
    vec_copy.start()
    length = len_ref[2 * z + c]
    live_keys = lax.broadcasted_iota(jnp.int32, (1, slots), 1) < length
    lane = lax.broadcasted_iota(jnp.int32, (slots, 128), 1)
    outs = []

    def fetch(u):
        slot = lax.rem(u, 2)
        return [
            lcopy(full_ref.at[hf, u], wbuf.at[slot, :, hf * width : (hf + 1) * width], fetch_sem.at[slot, hf])
            for hf in range(2)
        ]

    def ready(u):
        @pl.when(u == 0)
        def _():
            keep.wait()
            share_in.wait_recv()

        for k in range(1, n):
            core_in(u, k).wait_recv()

    def p_copy(p):
        return lcopy(p_v.at[lax.rem(p, 2)], p_out.at[p], p_sem.at[lax.rem(p, 2)])

    def attention(p):
        at = rows_at(p, 128)
        q, k, v = qkv[0, :, at], qkv[1, :, at], qkv[2, :, at]

        @pl.when(p >= 2)
        def _():
            p_copy(p - 2).wait()

        out = None
        for h in range(2):
            part = lane < HD if h == 0 else lane >= HD
            scores = mm_nt(jnp.where(part, q, 0), k) * HD ** (-0.5)
            scores = jnp.where(live_keys, scores, MASKED)
            e = jnp.exp(scores - jnp.max(scores, -1, keepdims=True))
            low = (e * (1.0 / jnp.sum(e, -1, keepdims=True))).astype(BF16)
            p_v[lax.rem(p, 2), h] = low
            term = mm(low, jnp.where(part, v, 0))
            out = term if out is None else out + term
        o_v[:, at] = out.astype(BF16)
        p_copy(p).start()

    pairs = model // 128
    rb = 128

    def compute(u):
        w = wbuf.at[lax.rem(u, 2)]

        @pl.when(u == 0)
        def _():
            for k in range(1, nz):
                act_in(0, k).wait_recv()

        @pl.when(u < 3)
        def _():
            add = jnp.where(u == 0, bias[0:1, :], jnp.where(u == 2, bias[1:2, :], 0.0))
            qkv[u] = (mm(xv[...], w[...]) + add).astype(BF16)

        @pl.when(u == 2)
        def _():
            loop(pairs // 2, attention)

        @pl.when(u == 3)
        def _():
            loop(pairs // 2, lambda p: attention(p + pairs // 2))
            acc[...] = mm_nt(o_v[...], w[...]) + xv[...].astype(F32)

            def norm(i):
                at = rows_at(i, rb)
                first = acc[at, :] + vec[8:9, :]
                centred = first - mean(first)
                inv = lax.rsqrt(mean(centred * centred) + EPSILON)
                n1 = centred * inv
                n1_v[at, :] = n1
                r1_v[at, :] = jnp.broadcast_to(inv, (rb, 128))
                up = n1 * vec[10:11, :] + vec[11:12, :]
                ulow_v[at, :] = up.astype(BF16)
                u_v[at, :] = up

            loop(slots // rb, norm)
            for i, (src, dst) in enumerate(
                ((qkv.at[0], q_out), (qkv.at[1], k_out), (qkv.at[2], v_out), (o_v, o_out),
                 (n1_v, n1_out), (r1_v, r1_out), (ulow_v, u_out), (xv, x_out))
            ):
                lcopy(src, dst, out_sem.at[1 + i]).start()

        @pl.when(jnp.logical_and(u >= 4, u < 4 + e_units))
        def _():
            j = u - 4
            pre = mm(ulow_v[...], w[...]) + bias[pl.ds(2 + j, 1), :]
            phi = 0.5 * (1.0 + lax.erf(pre * 0.7071067811865476))
            h_v[j] = (pre * phi).astype(BF16)
            gp_v[j] = (phi + pre * jnp.exp(-0.5 * pre * pre) * 0.3989422804014327).astype(BF16)
            lcopy(h_v.at[j], h_out.at[j], out_sem.at[10]).start()
            lcopy(gp_v.at[j], gp_out.at[j], out_sem.at[11]).start()
            lcopy(h_v.at[j], h_out.at[j], out_sem.at[10]).wait()
            lcopy(gp_v.at[j], gp_out.at[j], out_sem.at[11]).wait()

        @pl.when(u >= 4 + e_units)
        def _():
            u_v[...] += mm_nt(h_v[u - 4 - e_units], w[...])

    def step(u):
        @pl.when(u < units)
        def _():
            @pl.when(u + ahead < units)
            def _():
                for k in direct:
                    own_copy(u + ahead, k).start()

            for k in direct:
                own_in(u, k).wait_recv()
                if n == 4:
                    fwd_copy(u, 2 - k).start()
                core_copy(u, k).start()

        if n == 4:
            @pl.when(jnp.logical_and(u > 0, u <= units))
            def _():
                for h in range(2):
                    fwd_in(u - 1, h).wait_recv()
                core_copy(u - 1, 3).start()

        @pl.when(u >= 2)
        def _():
            for i in fetch(u - 2):
                i.wait()
            compute(u - 2)

        @pl.when(jnp.logical_and(u > 0, u <= units))
        def _():
            ready(u - 1)
            for i in fetch(u - 1):
                i.start()

    loop(units + 2, step)

    for k in range(1, nz):
        act_in(1, k).wait_recv()

    def norm2(i):
        at = rows_at(i, rb)
        second = u_v[at, :] + vec[9:10, :]
        centred = second - mean(second)
        inv = lax.rsqrt(mean(centred * centred) + EPSILON)
        n2 = centred * inv
        gain = vec[12:13, :]
        y_v[at, :] = (n2 * gain + vec[13:14, :]).astype(BF16)
        row = lax.broadcasted_iota(jnp.int32, (rb, 1), 0) + i * rb
        grad = jnp.where(row < length, cotv[at, :].astype(F32), 0.0)
        scaled = grad * gain
        back = inv * (scaled - mean(scaled) - n2 * mean(scaled * n2))
        acc[at, :] = back
        low = back.astype(BF16)
        dz_v[at, :] = low
        for r, v in ((14, low.astype(F32)), (20, grad * n2), (22, grad)):
            v = jnp.sum(v, 0, keepdims=True)
            small[r : r + 1, :] += v[:, :width]
            small[r + 1 : r + 2, :] += v[:, width:]

    loop(slots // rb, norm2)
    last = [
        lcopy(src, dst, out_sem.at[12 + i])
        for i, (src, dst) in enumerate(((acc, ds_out), (dz_v, dz_out), (y_v, y_out), (small, small_out)))
    ]
    for i in last:
        i.start()

    def finish(u):
        for k in direct:
            own_copy(u, k).wait_send()
        if n == 4:
            for h in range(2):
                fwd_copy(u, h).wait_send()
        for k in range(1, n):
            core_copy(u, k).wait_send()

    loop(units, finish)
    share.wait_send()
    for k, j in pk_pairs:
        pk_copy(k, j).wait_send()
    for which in range(2):
        for k in range(1, nz):
            act(which, k).wait_send()
    vec_copy.wait()
    for p in (pairs - 2, pairs - 1):
        p_copy(p).wait()
    for i, (src, dst) in enumerate(
        ((qkv.at[0], q_out), (qkv.at[1], k_out), (qkv.at[2], v_out), (o_v, o_out),
         (n1_v, n1_out), (r1_v, r1_out), (ulow_v, u_out), (xv, x_out))
    ):
        lcopy(src, dst, out_sem.at[1 + i]).wait()
    for i in last:
        i.wait()


def forward(n, nz, lengths, inputs, cotangent, wq, wk, wv, wo, we, wr, heads, vectors):
    seqs, block, model = inputs.shape
    rows = wq.shape[0]
    e_units = we.shape[1] // UNIT
    units = 4 + 2 * e_units
    slots = nz * block
    head_rows = sum(v.shape[0] for v in heads)
    pk = (head_rows + 16, max(rows, 128))
    outs = [
        ((2, units, model, UNIT), BF16), ((slots, model), BF16),
        ((slots, model), BF16), ((slots, model), BF16), ((slots, model), BF16), ((slots, model), BF16),
        ((model // 128, 2, slots, slots), BF16), ((slots, model), F32), ((slots, 128), F32), ((slots, model), BF16),
        ((e_units, slots, model), BF16), ((e_units, slots, model), BF16),
        ((slots, model), F32), ((slots, model), BF16), ((slots, model), BF16), ((16, model), F32),
        ((24, UNIT), F32),
    ]
    scratch = [
        ((units, rows, UNIT), BF16), (wo.shape, BF16), (wr.shape, BF16), ((nz, block, model), F32),
        ((2, nz, block, model), BF16), ((slots, model), BF16), ((slots, model), BF16), ((3, slots, model), BF16),
        ((slots, model), BF16), ((2, 2, slots, slots), BF16), ((slots, model), F32), ((slots, 128), F32),
        ((slots, model), F32), ((slots, model), BF16), ((e_units, slots, model), BF16),
        ((e_units, slots, model), BF16), ((slots, model), F32),
        ((slots, model), BF16), ((slots, model), BF16), ((2, model, 2 * UNIT), BF16),
        (pk, BF16), (pk, F32), ((n, 2, *pk), BF16), ((2, head_rows, UNIT), F32), ((16, 2 * UNIT), F32), ((16, model), F32), ((24, UNIT), F32),
    ]
    return pl.pallas_call(
        functools.partial(forward_kernel, n, nz),
        name="gather_and_forward",
        out_shape=[jax.ShapeDtypeStruct(a, b) for a, b in outs],
        in_specs=[SMEM] + [ANY] * 8 + [VMEM] * 9,
        out_specs=[ANY] * len(outs),
        scratch_shapes=[pltpu.VMEM(a, b) for a, b in scratch]
        + [
            DMA((units, n)), DMA((units, n)), DMA((units, 2)), DMA((units, 2)),
            DMA((units + 1, n)), DMA((units + 1, n)), DMA((2, nz)), DMA((2, nz)),
            DMA((n, 2)), DMA((n, 2)), DMA((6 + e_units,)), DMA((nz,)), DMA((2, 2)), DMA((16,)), DMA((2,)),
        ],
        compiler_params=pltpu.CompilerParams(
            collective_id=0, has_side_effects=True, vmem_limit_bytes=60 * 2**20
        ),
    )(lengths, inputs, cotangent, wq, wk, wv, wo, we, wr, *heads, *vectors)


def backward_kernel(
    n, nz,
    full_ref, x_ref, q_ref, k_ref, v_ref, o_ref, p_ref, n1_ref, r1_ref, u_ref, h_ref, gp_ref,
    ds_ref, dz_ref, y_ref, vec_ref, small_ref,
    grad_ref, ys_ref, dx_ref, small_out, part_ref, got_ref,
    x_v, qkv, o_v, p_v, n1_v, r1_v, u_v, dz_v, du, wr_v, we_v, h_v, gp_v, dpre, pbuf, small, round_in,
    stage, gstage, total, near, pair_sum, far, up, across, down, block_out,
    load_sem, w_sem, p_sem, part_sem, core_send, core_recv, stage_sem, near_send, near_recv, far_send, far_recv,
    z_send, z_recv, store_sem, act_send, act_recv, pass_send, pass_recv, keep_sem, small_send, small_recv,
):
    s, z, c = place()
    units = part_ref.shape[0]
    subs = 2 * units
    e_units = h_ref.shape[0]
    model = total.shape[1]
    width = UNIT
    rows = model // n
    half = rows // 2
    slots = x_v.shape[0]
    block = slots // nz
    zrows = rows_at(z, block)
    mates = [(dz_ref, dz_v), (small_ref, small), (ds_ref, du), (n1_ref, n1_v), (r1_ref, r1_v), (o_ref, o_v),
             (u_ref, u_v), (q_ref, qkv.at[0]), (k_ref, qkv.at[1]), (v_ref, qkv.at[2]), (x_ref, x_v)]
    loads = [lcopy(a, b, load_sem.at[i]) for i, (a, b) in enumerate(mates)]

    class Weights:
        def __init__(self, buf, i):
            self.buf, self.i = buf, i

        def copies(self, u):
            return [
                lcopy(full_ref.at[hf, u], self.buf.at[:, hf * width : (hf + 1) * width], w_sem.at[self.i, hf])
                for hf in range(2)
            ]

        def start(self, u):
            for i in self.copies(u):
                i.start()

        def wait(self, u):
            for i in self.copies(u):
                i.wait()

    wr, we = Weights(wr_v, 0), Weights(we_v, 1)

    def load_h(j):
        return lcopy(h_ref.at[j], h_v, w_sem.at[2, 0])

    def load_gp(j):
        return lcopy(gp_ref.at[j], gp_v, w_sem.at[2, 1])

    def load_p(p):
        return lcopy(p_ref.at[p], p_v.at[lax.rem(p, 2)], p_sem.at[lax.rem(p, 2)])

    loads[0].start()
    load_h(0).start()
    loads[1].start()
    load_gp(0).start()
    wr.start(4 + e_units)
    we.start(4)
    for i in loads[2:]:
        i.start()
    for p in range(2):
        load_p(p).start()
    greet(
        [(s ^ k, z, c) for k in range(1, n)]
        + [(s, z, 1 - c)]
        + [(s, lax.rem(z + k, nz), c) for k in range(1, nz)]
    )

    def act(which, k, i):
        src, dst = ((y_ref, ys_ref), (dz_v, dx_ref))[which]
        to = lax.rem(z + k, nz)
        some = block // PIECES
        return rcopy(
            src.at[pl.ds(pl.multiple_of(to * block + i * some, some), some), :],
            dst.at[2 * z + c, rows_at(i, some), :],
            act_send.at[which, k, i], act_recv.at[which, k, i], (s, to, c),
        )

    def act_in(which, k, i):
        src = lax.rem(z + nz - k, nz)
        at = (ys_ref, dx_ref)[which].at[2 * src + c, rows_at(i, block // PIECES), :]
        return rcopy(at, at, act_send.at[which, k, i], act_recv.at[which, k, i], (s, src, c))

    def act_keep(which):
        src, dst = ((y_ref, ys_ref), (dz_v, dx_ref))[which]
        return lcopy(src.at[zrows, :], dst.at[2 * z + c], keep_sem.at[which])

    def pass_copy(which, k):
        at = (ys_ref, dx_ref)[which].at[2 * lax.rem(z + nz - k, nz) + c]
        return rcopy(at, at, pass_send.at[which, k], pass_recv.at[which, k], (s, z, 1 - c))

    def pass_in(which, k):
        at = (ys_ref, dx_ref)[which].at[2 * lax.rem(z + nz - k, nz) + 1 - c]
        return rcopy(at, at, pass_send.at[which, k], pass_recv.at[which, k], (s, z, 1 - c))

    def act_some(which, i):
        for k in range(1, nz):
            act(which, k, i).start()

    def act_pass(which):
        for k in range(1, nz):
            loop(PIECES, lambda i: act_in(which, k, i).wait_recv())
            pass_copy(which, k).start()
        act_keep(which).wait()
        pass_copy(which, 0).start()

    act_keep(0).start()

    def core_copy(u):
        return rcopy(pbuf.at[0], got_ref.at[u], core_send.at[u], core_recv.at[u], (s, z, 1 - c))

    def core_in(u):
        return rcopy(got_ref.at[u], got_ref.at[u], core_send.at[u], core_recv.at[u], (s, z, 1 - c))

    def part_copy(u):
        return lcopy(pbuf.at[1], part_ref.at[u], part_sem.at[0])

    def settle(u):
        core_copy(u).wait_send()
        part_copy(u).wait()

    def emit(u, i, value):
        low = value.astype(BF16)
        for b in range(2):
            pbuf[i, b] = low[:, b * SUB : (b + 1) * SUB]

    def produce(u, make):
        def one(i):
            emit(u, i, make(lax.rem(1 - c + i, 2)))

            @pl.when(i == 0)
            def _():
                core_copy(u).start()

        loop(2, one)
        part_copy(u).start()

    lane = lax.broadcasted_iota(jnp.int32, (slots, 128), 1)
    rb = 128
    last_e = e_units - 1

    def cols(hf):
        return rows_at(hf, width)

    def add_small(r, v):
        v = jnp.sum(v, 0, keepdims=True)
        for hf in range(2):
            small[pl.ds(r[hf], 1), :] += v[:, hf * width : (hf + 1) * width]

    def make_r(j):
        load_h(j).wait()
        produce(j, lambda hf: mm_tn(dz_v[...], h_v[:, cols(hf)]))

        @pl.when(j < last_e)
        def _():
            load_h(j + 1).start()

    def make_dpre(j):
        wr.wait(4 + e_units + j)
        load_gp(j).wait()
        low = (mm(dz_v[...], wr_v[...]) * gp_v[...].astype(F32)).astype(BF16)
        dpre[j] = low
        add_small((4 + j, 4 + e_units + j), low.astype(F32))

        @pl.when(j < last_e)
        def _():
            wr.start(5 + e_units + j)
            load_gp(j + 1).start()

        @pl.when(j == last_e)
        def _():
            wr.start(3)

    def make_du(j):
        we.wait(4 + j)
        du[...] += mm_nt(dpre[j], we_v[...])

        @pl.when(j < last_e)
        def _():
            we.start(5 + j)

        @pl.when(j == last_e)
        def _():
            we.start(1)

    def make_e(u, j):
        produce(u, lambda hf: mm_tn(u_v[...], dpre[j, :, cols(hf)]))

    def norm(i):
        at = rows_at(i, rb)
        grad = du[at, :]
        n1 = n1_v[at, :]
        scaled = grad * vec_ref[10:11, :]
        back = r1_v[at, 0:1] * (scaled - mean(scaled) - n1 * mean(scaled * n1))
        du[at, :] = back
        low = back.astype(BF16)
        dz_v[at, :] = low
        for r, v in ((12, low.astype(F32)), (16, grad * n1), (18, grad)):
            add_small((r, r + 1), v)

    def make_o():
        for i in loads[3:6]:
            i.wait()
        loop(slots // rb, norm)
        produce(e_units, lambda hf: mm_tn(dz_v[...], o_v[:, cols(hf)]))

    def make_do():
        wr.wait(3)
        o_v[...] = mm(dz_v[...], wr_v[...]).astype(BF16)
        wr.start(0)

    def attention(p):
        at = rows_at(p, 128)
        q, k, v, do = qkv[0, :, at], qkv[1, :, at], qkv[2, :, at], o_v[:, at]
        load_p(p).wait()
        dq = dk = dv = None
        for h in range(2):
            part = lane < HD if h == 0 else lane >= HD
            qh, kh, doh = jnp.where(part, q, 0), jnp.where(part, k, 0), jnp.where(part, do, 0)
            low = p_v[lax.rem(p, 2), h]
            probs = low.astype(F32)
            dp = mm_nt(doh, v)
            ds = (probs * (dp - jnp.sum(dp * probs, -1, keepdims=True))).astype(BF16)
            tv, tk, tq = mm_tn(low, doh), mm_tn(ds, qh), mm(ds, kh)
            dv, dk, dq = (tv, tk, tq) if h == 0 else (dv + tv, dk + tk, dq + tq)
        qkv[0, :, at] = (dq * HD ** (-0.5)).astype(BF16)
        qkv[1, :, at] = (dk * HD ** (-0.5)).astype(BF16)
        qkv[2, :, at] = dv.astype(BF16)

        @pl.when(p + 2 < pairs)
        def _():
            load_p(p + 2).start()

    pairs = model // 128

    def make_w(u, i):
        produce(u, lambda hf: mm_tn(x_v[...], qkv[i, :, cols(hf)]))

    def make_dx(i, weights):
        weights.wait(i)
        du[...] += mm_nt(qkv[i], weights.buf[...])
        if i != 1:
            add_small((i, i + 1), qkv[i].astype(F32))

    def one_of(t, ticks):
        hit = t == ticks[0]
        for i in ticks[1:]:
            hit = jnp.logical_or(hit, t == i)
        return hit

    makes = {0: 0, 1: 1, 2: 2, 3: 3, 4: 4, 6: 5, 7: 6, 8: 7, 10: 8, 11: 9, 12: 10, 13: 11}

    def unit_of(t):
        return t - jnp.where(t > 4, 1, 0) - jnp.where(t > 9, 1, 0)

    def compute(t):
        @pl.when(t == 0)
        def _():
            loads[0].wait()
            loads[1].wait()

        pl.when(t < 4)(lambda: make_r(t))
        pl.when(t == 1)(lambda: loads[2].wait())
        pl.when(jnp.logical_and(t > 0, t < 5))(lambda: make_du(t - 1))
        pl.when(t < 4)(lambda: make_dpre(t))
        pl.when(t == 4)(make_o)

        @pl.when(t == 5)
        def _():
            make_do()
            for i in loads[6:]:
                i.wait()

        pl.when(jnp.logical_and(t > 4, t < 9))(lambda: loop(2, lambda i: attention(2 * (t - 5) + i)))

        @pl.when(one_of(t, (6, 7, 12, 13)))
        def _():
            make_e(unit_of(t), t - jnp.where(t > 7, 10, 6))

        @pl.when(one_of(t, (8, 10, 11)))
        def _():
            make_w(unit_of(t), t - jnp.where(t > 8, 9, 8))

        @pl.when(t == 9)
        def _():
            make_dx(0, wr)
            wr.start(2)
            make_dx(1, we)
            make_dx(2, wr)
            dz_v[...] = du[...].astype(BF16)
            act_keep(1).start()

    def loads_of(w):
        slot = lax.rem(w, 2)
        u, b = w // 2, lax.rem(w, 2)
        return [
            lcopy(part_ref.at[u, b], stage.at[slot], stage_sem.at[slot, 0]),
            lcopy(got_ref.at[u, b], gstage.at[slot], stage_sem.at[slot, 1]),
        ]

    def blk(k):
        return rows_at(s ^ k, rows)

    def blk_half(k, h):
        return pl.ds(pl.multiple_of((s ^ k) * rows + h * half, half), half)

    def near_copy(w, h, i):
        k = (1 + h, 3)[i]
        return rcopy(
            total.at[lax.rem(w, SLOTS), blk_half(k, h), :], near.at[w, h, i],
            near_send.at[w, h, i], near_recv.at[w, h, i], (s ^ (1 + h), z, c),
        )

    def far_copy(w, h):
        return rcopy(
            pair_sum.at[w, h], far.at[w, h], far_send.at[w, h], far_recv.at[w, h], (s ^ (2 - h), z, c)
        )

    def straight(w, k):
        return rcopy(
            total.at[lax.rem(w, SLOTS), blk(k), :], near.at[w, k - 1],
            near_send.at[w, k - 1], near_recv.at[w, k - 1], (s ^ k, z, c),
        )

    def sends_of(w):
        if n == 4:
            return [near_copy(w, h, i) for h in range(2) for i in range(2)]
        return [straight(w, k) for k in range(1, n)]

    def z_to(w, src, dst, i, to):
        return rcopy(src.at[w], dst.at[w], z_send.at[w, i], z_recv.at[w, i], (s, to, c))

    last = nz - 1
    edge = jnp.logical_or(z == 0, z == last)
    inner = jnp.where(z == 0, 1, nz - 2)
    outer = jnp.where(z == 1, 0, last)
    other = jnp.where(z == 1, 2, 1)

    def s0(w):
        @pl.when(lax.rem(w, 2) == 0)
        def _():
            core_in(w // 2).wait_recv()

        for i in loads_of(w):
            i.start()

    def s1(w):
        @pl.when(w >= SLOTS)
        def _():
            for i in sends_of(w - SLOTS):
                i.wait_send()

        for i in loads_of(w):
            i.wait()
        slot, to = lax.rem(w, 2), lax.rem(w, SLOTS)

        def add(i):
            at = rows_at(i, 256)
            total[to, at, :] = (stage[slot, at, :].astype(F32) + gstage[slot, at, :].astype(F32)).astype(BF16)

        loop(model // 256, add)
        for i in sends_of(w):
            i.start()

    def s2(w):
        slot = lax.rem(w, SLOTS)
        for i in sends_of(w):
            i.wait_recv()
        if n == 4:
            for h in range(2):
                pair_sum[w, h] = (
                    total[slot, blk_half(2 - h, h), :].astype(F32) + near[w, h, 1].astype(F32)
                ).astype(BF16)
                far_copy(w, h).start()

    def s3(w):
        slot = lax.rem(w, SLOTS)
        if n == 4:
            for h in range(2):
                far_copy(w, h).wait_recv()
                block_out[w, h * half : (h + 1) * half] = (
                    total[slot, blk_half(0, h), :].astype(F32) + near[w, h, 0].astype(F32) + far[w, h].astype(F32)
                ).astype(BF16)
        else:
            acc = total[slot, blk(0), :].astype(F32)
            for k in range(1, n):
                acc = acc + near[w, k - 1].astype(F32)
            block_out[w] = acc.astype(BF16)

        @pl.when(edge)
        def _():
            z_to(w, block_out, up, 0, inner).start()

    def s4(w):
        @pl.when(jnp.logical_not(edge))
        def _():
            z_to(w, block_out, up, 0, outer).wait_recv()
            block_out[w] = (block_out[w].astype(F32) + up[w].astype(F32)).astype(BF16)
            z_to(w, block_out, across, 1, other).start()

    def s5(w):
        @pl.when(jnp.logical_not(edge))
        def _():
            z_to(w, block_out, across, 1, other).wait_recv()
            down[w] = (block_out[w].astype(F32) + across[w].astype(F32)).astype(BF16)
            z_to(w, down, down, 2, outer).start()

    def s6(w):
        @pl.when(edge)
        def _():
            z_to(w, down, down, 2, inner).wait_recv()

        lcopy(down.at[w], grad_ref.at[w], store_sem.at[w]).start()

    stages = list(zip(LAGS, (s0, s3, s2, s1, s6, s5, s4)))

    def serve(w):
        for lag, stage_of in stages:
            @pl.when(jnp.logical_and(w >= lag, w - lag < subs))
            def _(stage_of=stage_of, lag=lag):
                stage_of(w - lag)

    hops = [(s, z, 1 - c)]
    hops += [(s ^ (1 << b), z, c) for b in range(n.bit_length() - 1)]
    hops += [(s, z ^ (1 << b), c) for b in range(nz.bit_length() - 1)]

    def small_copy(i):
        return rcopy(small, round_in.at[i], small_send.at[i], small_recv.at[i], hops[i])

    done = max(makes) + 2

    def served(t):
        return jnp.clip(2 * (t - 1), 0, 4) + jnp.maximum(PACE * (t - 3) // 4, 0)

    def step(t):
        pl.when(one_of(t, [i + 1 for i in makes]))(lambda: settle(unit_of(t - 1)))

        lax.fori_loop(served(t), served(t + 1), lambda w, carry: (serve(w), carry)[1], 0)
        pl.when(t <= max(makes))(lambda: compute(t))

        for which, first in enumerate(ACTS):
            pl.when(jnp.logical_and(t >= first, t < first + PIECES))(lambda: act_some(which, t - first))

        @pl.when(t == PIECES)
        def _():
            act_pass(0)

        @pl.when(t == PASS)
        def _():
            act_pass(1)

        for i in range(len(hops) + 1):
            @pl.when(t == done + i)
            def _(i=i):
                if i > 0:
                    small_copy(i - 1).wait_send()
                    small_copy(i - 1).wait_recv()
                    small[...] += round_in[i - 1]
                if i < len(hops):
                    small_copy(i).start()
                else:
                    lcopy(small, small_out, keep_sem.at[2]).start()

    ticks = (4 * (subs + max(LAGS) - 4) + PACE - 1) // PACE + 3
    loop(ticks, step)

    def finish(w):
        if n == 4:
            for h in range(2):
                far_copy(w, h).wait_send()

        @pl.when(edge)
        def _():
            z_to(w, block_out, up, 0, inner).wait_send()

        @pl.when(jnp.logical_not(edge))
        def _():
            z_to(w, block_out, across, 1, other).wait_send()
            z_to(w, down, down, 2, outer).wait_send()

        lcopy(down.at[w], grad_ref.at[w], store_sem.at[w]).wait()

    loop(subs, finish)
    for w in range(subs - SLOTS, subs):
        for i in sends_of(w):
            i.wait_send()
    for which in range(2):
        for k in range(1, nz):
            loop(PIECES, lambda i: act(which, k, i).wait_send())
        for k in range(nz):
            pass_copy(which, k).wait_send()
            pass_in(which, k).wait_recv()
    lcopy(small, small_out, keep_sem.at[2]).wait()


def backward(n, nz, full, x, q, k, v, o, p, n1, r1, u, h, gp, ds, dz, y, vec, small):
    _, units, model, width = full.shape
    e_units = h.shape[0]
    rows = model // n
    half = rows // 2
    slots = x.shape[0]
    block = slots // nz
    subs = 2 * units
    near = (subs, 2, 2, half, SUB) if n == 4 else (subs, n - 1, rows, SUB)
    near_sems = near[:3] if n == 4 else near[:2]
    far = (subs, 2, half, SUB) if n == 4 else (1, 2, 16, SUB)
    blocks = (subs, rows, SUB)
    hops = 1 + (n.bit_length() - 1) + (nz.bit_length() - 1)
    outs = [
        (blocks, BF16), ((2 * nz, block, model), BF16), ((2 * nz, block, model), BF16), ((24, UNIT), F32),
        ((units, 2, model, SUB), BF16), ((units, 2, model, SUB), BF16),
    ]
    scratch = [
        ((slots, model), BF16), ((3, slots, model), BF16), ((slots, model), BF16), ((2, 2, slots, slots), BF16),
        ((slots, model), F32), ((slots, 128), F32), ((slots, model), BF16), ((slots, model), BF16),
        ((slots, model), F32), ((model, 2 * UNIT), BF16), ((model, 2 * UNIT), BF16), ((slots, model), BF16),
        ((slots, model), BF16), ((e_units, slots, model), BF16), ((2, 2, model, SUB), BF16), ((24, UNIT), F32),
        ((hops, 24, UNIT), F32),
        ((2, model, SUB), BF16), ((2, model, SUB), BF16), ((SLOTS, model, SUB), BF16),
        (near, BF16), (far, BF16), (far, BF16), (blocks, BF16), (blocks, BF16), (blocks, BF16), (blocks, BF16),
    ]
    return pl.pallas_call(
        functools.partial(backward_kernel, n, nz),
        name="backward_and_reduce",
        out_shape=[jax.ShapeDtypeStruct(a, b) for a, b in outs],
        in_specs=[ANY] * 15 + [VMEM, ANY],
        out_specs=[ANY] * len(outs),
        scratch_shapes=[pltpu.VMEM(a, b) for a, b in scratch]
        + [
            DMA((12,)), DMA((3, 2)), DMA((2,)), DMA((1,)), DMA((units,)), DMA((units,)), DMA((2, 2)),
            DMA(near_sems), DMA(near_sems), DMA((subs, 2)), DMA((subs, 2)),
            DMA((subs, 3)), DMA((subs, 3)), DMA((subs,)),
            DMA((2, nz, PIECES)), DMA((2, nz, PIECES)), DMA((2, nz)), DMA((2, nz)), DMA((3,)), DMA((hops,)), DMA((hops,)),
        ],
        compiler_params=pltpu.CompilerParams(
            collective_id=1, has_side_effects=True, vmem_limit_bytes=61 * 2**20
        ),
    )(full, x, q, k, v, o, p, n1, r1, u, h, gp, ds, dz, y, vec, small)


def finish_kernel(
    n, grad_ref, ys_ref, dx_ref, small_ref,
    y_out, dx_out, dq_out, dk_out, dv_out, do_out, de_out, dr_out,
    qb_out, vb_out, eb_out, ob_out, rb_out, g1_out, s1_out, g2_out, s2_out,
    grads, act, act_wide, dq, dk, dv, do, de, dr, in_sem, out_sem, act_in, act_out,
):
    s, _, c = place()
    rows = dq.shape[0]
    seqs = act.shape[1]
    e_units = de.shape[1] // UNIT
    he = HD // n
    load = lcopy(grad_ref, grads, in_sem)
    load.start()

    def act_load(i, which):
        return lcopy((ys_ref, dx_ref)[which].at[i], act.at[which, i], act_in.at[which, i])

    def act_store(i, which):
        return lcopy(act_wide.at[which, i], (y_out, dx_out)[which].at[i], act_out.at[which, i])

    for which in range(2):
        loop(seqs, lambda i: act_load(i, which).start())
    load.wait()
    stores = []

    def store(src, dst):
        stores.append(lcopy(src, dst, out_sem.at[len(stores)]))
        stores[-1].start()

    def part(u, b):
        return grads[2 * u + b].astype(F32)

    spots = [e_units + 1, e_units + 2, e_units + 6, e_units + 7]
    for j in range(e_units):
        for b in range(2):
            at = j * UNIT + b * SUB
            dr[at : at + SUB, :] = part(j, b).T
            de[:, at : at + SUB] = part(spots[j], b)
    store(dr, dr_out)
    store(de, de_out)
    for i, (v, out) in enumerate(((dq, dq_out), (dk, dk_out), (dv, dv_out))):
        for b in range(2):
            v[:, b * SUB : (b + 1) * SUB] = part(e_units + 3 + i, b)
        store(v, out)
    for b in range(2):
        do[b * SUB : (b + 1) * SUB, :] = part(e_units, b).T
    store(do, do_out)
    for which in range(2):
        def widen(i):
            act_load(i, which).wait()
            act_wide[which, i] = act[which, i].astype(F32)
            act_store(i, which).start()

        loop(seqs, widen)

    at = lax.rem(UNIT - s * he, UNIT)
    turned = pltpu.roll(small_ref[...], at, 1)
    for out, base, count in ((qb_out, 0, 1), (vb_out, 2, 1), (eb_out, 4, e_units)):
        for i in range(count):
            line = jnp.where(c == 0, turned[base + i : base + i + 1, :], turned[base + count + i : base + count + i + 1, :])
            for h in range(8):
                out[8 * i + h : 8 * i + h + 1, :] = line[:, h * HD : h * HD + he]
    at = lax.rem(UNIT - lax.rem(s * rows, UNIT), UNIT)
    turned = pltpu.roll(small_ref[...], at, 1)
    late = s * rows >= UNIT
    for i, out in enumerate((ob_out, rb_out, g1_out, s1_out, g2_out, s2_out)):
        r = 4 + 2 * e_units + 2 * i
        line = jnp.where(late, turned[r + 1 : r + 2, :], turned[r : r + 1, :])
        out[...] = line[:, :rows].reshape(rows)
    for i in stores:
        i.wait()
    for which in range(2):
        loop(seqs, lambda i: act_store(i, which).wait())


def finish(n, grads, ys, dx, small, heads):
    _, rows, _ = grads.shape
    seqs, block, model = ys.shape
    wide = heads[2].shape[0] // 8 * UNIT
    square, tall = (rows, UNIT), (UNIT, rows)
    outs = [ys.shape, ys.shape, square, square, square, tall, (rows, wide), (wide, rows)]
    small_outs = [v.shape for v in heads] + [(rows,)] * 6
    return pl.pallas_call(
        functools.partial(finish_kernel, n),
        name="widen_results",
        out_shape=[jax.ShapeDtypeStruct(a, F32) for a in outs + small_outs],
        in_specs=[ANY] * 3 + [VMEM],
        out_specs=[ANY] * len(outs) + [VMEM] * len(small_outs),
        scratch_shapes=[pltpu.VMEM(grads.shape, BF16), pltpu.VMEM((2, *ys.shape), BF16), pltpu.VMEM((2, *ys.shape), F32)]
        + [pltpu.VMEM(a, F32) for a in outs[2:]]
        + [DMA, DMA((6,)), DMA((2, seqs)), DMA((2, seqs))],
        compiler_params=pltpu.CompilerParams(vmem_limit_bytes=61 * 2**20),
    )(grads, ys, dx, small)


def body(n, nz, inputs, lengths, wq, wk, wv, wo, we, wr, qb, vb, eb, ob, rb, g1, s1, g2, s2, cotangent):
    heads = (qb, vb, eb)
    (full, x, q, k, v, o, p, n1, r1, u, h, gp, ds, dz, y, vec, small) = forward(
        n, nz, lengths, inputs, cotangent, wq, wk, wv, wo, we, wr, heads, (ob, rb, g1, s1, g2, s2)
    )
    grads, ys, dx, small, _, _ = backward(
        n, nz, full, x, q, k, v, o, p, n1, r1, u, h, gp, ds, dz, y, vec, small
    )
    return tuple(finish(n, grads, ys, dx, small, heads))


def solution(mesh):
    w, wt, v = P("shard", "tp"), P("tp", "shard"), P("shard")
    rows = P("shard", "ctx", None)
    return jax.shard_map(
        functools.partial(body, mesh.shape["shard"], mesh.shape["ctx"]),
        mesh=mesh,
        in_specs=(rows, v, w, w, w, wt, w, wt, wt, wt, wt, v, v, v, v, v, v, rows),
        out_specs=(rows, rows, w, w, w, wt, w, wt, wt, wt, wt, v, v, v, v, v, v),
        check_vma=False,
    )
```

```python
import functools

import jax
import jax.numpy as jnp
from jax import lax
from jax.experimental import pallas as pl
from jax.experimental.pallas import tpu as pltpu
from jax.sharding import PartitionSpec as P

HD = 64
UNIT = 512
SUB = 256
SLOTS = 4
LAGS = (0, 5, 3, 1, 11, 9, 7)
PACE = 5
PASS = 22
PIECES = 8
ACTS = (0, 10)
EPSILON = 1e-05
MASKED = -1e30
MESH = pl.DeviceIdType.MESH
F32 = jnp.float32
BF16 = jnp.bfloat16
DMA = pltpu.SemaphoreType.DMA
ANY = pl.BlockSpec(memory_space=pl.ANY)
VMEM = pl.BlockSpec(memory_space=pltpu.VMEM)
SMEM = pl.BlockSpec(memory_space=pltpu.SMEM)


def place():
    return lax.axis_index("shard"), lax.axis_index("ctx"), lax.axis_index("tp")


def rcopy(src, dst, send, recv, dev):
    return pltpu.make_async_remote_copy(
        src_ref=src, dst_ref=dst, send_sem=send, recv_sem=recv, device_id=dev, device_id_type=MESH
    )


def lcopy(src, dst, sem):
    return pltpu.make_async_copy(src, dst, sem)


def greet(devices):
    barrier = pltpu.get_barrier_semaphore()
    for dev in devices:
        pl.semaphore_signal(barrier, inc=1, device_id=dev, device_id_type=MESH)
    pl.semaphore_wait(barrier, len(devices))


def rows_at(i, size):
    return pl.ds(pl.multiple_of(i * size, size), size)


def mm(a, b):
    return jnp.dot(a, b, preferred_element_type=F32)


def mm_nt(a, b):
    return lax.dot_general(a, b, (((1,), (1,)), ((), ())), preferred_element_type=F32)


def mm_tn(a, b):
    return lax.dot_general(a, b, (((0,), (0,)), ((), ())), preferred_element_type=F32)


def loop(count, fn):
    def step(i, carry):
        fn(i)
        return carry

    lax.fori_loop(0, count, step, 0)


def mean(v):
    return jnp.mean(v, -1, keepdims=True)


def forward_kernel(
    n, nz,
    len_ref, x_ref, g_ref, wq_ref, wk_ref, wv_ref, wo_ref, we_ref, wr_ref,
    qb_ref, vb_ref, eb_ref, ob_ref, rb_ref, g1_ref, s1_ref, g2_ref, s2_ref,
    full_ref, x_out, q_out, k_out, v_out, o_out, p_out, n1_out, r1_out, u_out, h_out, gp_out,
    ds_out, dz_out, y_out, vec_out, small_out,
    own, wo_in, wr_in, xin, act_low, xv, cotv, qkv, o_v, p_v, n1_v, r1_v, u_v, ulow_v, h_v, gp_v, acc,
    dz_v, y_v, wbuf, pk_ref, pk_wide, pkall, head_bias, bias, vec, small,
    own_send, own_recv, fwd_send, fwd_recv, core_send, core_recv, z_send, z_recv, act_send, act_recv,
    pk_send, pk_recv, in_sem, act_sem, fetch_sem, out_sem, p_sem,
):
    s, z, c = place()
    units, rows, width = own.shape
    half = rows // 2
    model = rows * n
    slots = xv.shape[0]
    block = slots // nz
    e_units = we_ref.shape[1] // width
    group = [(s ^ k, z, c if j == 0 else 1 - c) for k in range(n) for j in range(2) if k + j > 0]
    mine = rows_at(s, rows)
    zrows = rows_at(z, block)

    ins = [lcopy(r, own.at[i], in_sem.at[i]) for i, r in enumerate((wq_ref, wk_ref, wv_ref))]
    ins += [
        lcopy(we_ref.at[:, pl.ds(j * width, width)], own.at[4 + j], in_sem.at[3 + j]) for j in range(e_units)
    ]
    ins_o = lcopy(wo_ref, wo_in, in_sem.at[3 + e_units])
    ins_r = lcopy(wr_ref, wr_in, in_sem.at[4 + e_units])

    def to(k):
        return lax.rem(z + k, nz)

    def act_load(which, k):
        src = (x_ref, g_ref)[which]
        return lcopy(src.at[2 * to(k) + c], xin.at[k], act_sem.at[k])

    some = block // PIECES

    def act(which, k, i):
        dst = (xv, cotv)[which]
        at = pl.ds(pl.multiple_of(z * block + i * some, some), some)
        return rcopy(
            act_low.at[which, k, rows_at(i, some), :], dst.at[at, :],
            act_send.at[which, k, i], act_recv.at[which, k, i], (s, to(k), c),
        )

    def act_in(which, k, i):
        dst = (xv, cotv)[which]
        src = lax.rem(z + nz - k, nz)
        at = dst.at[pl.ds(pl.multiple_of(src * block + i * some, some), some), :]
        return rcopy(at, at, act_send.at[which, k, i], act_recv.at[which, k, i], (s, src, c))

    def act_some(which, i):
        for k in range(1, nz):
            act(which, k, i).start()

    def act_share(which, send):
        for k in range(1, nz):
            act_load(which, k).wait()
            act_low[which, k] = xin[k].astype(BF16)
            if send:
                loop(PIECES, lambda i: act(which, k, i).start())
        act_load(which, 0).wait()
        (xv, cotv)[which][zrows, :] = xin[0].astype(BF16)

    def act_arrive(which):
        for k in range(1, nz):
            loop(PIECES, lambda i: act_in(which, k, i).wait_recv())

    for k in range(1, nz):
        act_load(0, k).start()
    for i in ins:
        i.start()
    act_load(0, 0).start()
    ins_o.start()
    ins_r.start()

    he = HD // n
    heads = [qb_ref, vb_ref, eb_ref]
    head_rows = sum(r.shape[0] for r in heads)
    pk_wide[...] = jnp.zeros_like(pk_wide)
    at = 0
    for r in heads:
        pk_wide[at : at + r.shape[0], :he] = r[...].astype(F32)
        at += r.shape[0]
    for i, r in enumerate((ob_ref, rb_ref, g1_ref, s1_ref, g2_ref, s2_ref)):
        pk_wide[at + 8 + i : at + 9 + i, :rows] = r[...].reshape(1, rows).astype(F32)
    pk_ref[...] = pk_wide[...].astype(BF16)
    greet(group + [(s, lax.rem(z + k, nz), c) for k in range(1, nz)])

    def pk_copy(k, j):
        return rcopy(
            pk_ref, pkall.at[s, c], pk_send.at[k, j], pk_recv.at[k, j], (s ^ k, z, c if j == 0 else 1 - c)
        )

    def pk_in(k, j):
        at = pkall.at[s ^ k, c if j == 0 else 1 - c]
        return rcopy(at, at, pk_send.at[k, j], pk_recv.at[k, j], (s ^ k, z, c if j == 0 else 1 - c))

    pk_pairs = [(k, j) for k in range(n) for j in range(2) if k + j > 0]
    for k, j in pk_pairs:
        pk_copy(k, j).start()
    pkall[s, c] = pk_ref[...]

    direct = [1, 2] if n == 4 else list(range(1, n))

    def own_copy(u, k):
        return rcopy(
            own.at[u], full_ref.at[c, u, mine, :], own_send.at[u, k], own_recv.at[u, k], (s ^ k, z, c)
        )

    def own_in(u, k):
        at = full_ref.at[c, u, rows_at(s ^ k, rows), :]
        return rcopy(at, at, own_send.at[u, k], own_recv.at[u, k], (s ^ k, z, c))

    def half_at(k, h):
        return pl.ds(pl.multiple_of((s ^ k) * rows + h * half, half), half)

    def fwd_copy(u, h):
        at = full_ref.at[c, u, half_at(2 - h, h), :]
        return rcopy(at, at, fwd_send.at[u, h], fwd_recv.at[u, h], (s ^ (1 + h), z, c))

    def fwd_in(u, h):
        at = full_ref.at[c, u, half_at(3, h), :]
        return rcopy(at, at, fwd_send.at[u, h], fwd_recv.at[u, h], (s ^ (1 + h), z, c))

    def core_copy(u, k):
        at = full_ref.at[c, u, rows_at(s ^ k, rows), :]
        return rcopy(at, at, core_send.at[u, k], core_recv.at[u, k], (s, z, 1 - c))

    def core_in(u, k):
        at = full_ref.at[1 - c, u, rows_at(s ^ k, rows), :]
        return rcopy(at, at, core_send.at[u, k], core_recv.at[u, k], (s, z, 1 - c))

    par = lax.rem(z, 2)
    slots_of_units = units - 2

    def unit_at(i):
        u = jnp.where(i < 3, i, jnp.where(i == 3, 4 + par, jnp.where(i == 4, 3, 8 + par)))
        return jnp.where(i > 5, jnp.where(i < 8, i, i + 2), u)

    def theirs_at(i):
        return jnp.where(i == 3, 5 - par, 9 - par)

    def z_copy(u, k):
        at = full_ref.at[c, u, rows_at(s ^ k, rows), :]
        return rcopy(at, at, z_send.at[u, k], z_recv.at[u, k], (s, z + 1 - 2 * par, c))

    def is_paired(i):
        return jnp.logical_or(i == 3, i == 5)

    ahead = 1
    for i in ins[:ahead]:
        i.wait()
    for u in range(ahead):
        for k in direct:
            own_copy(u, k).start()
    act_share(0, True)
    for k in range(nz):
        act_load(1, k).start()
    for i in ins[ahead:]:
        i.wait()
    ins_o.wait()
    own[3] = wo_in[...].T
    ins_r.wait()

    def turn(j):
        own[4 + e_units + j] = wr_in[rows_at(j, width), :].T

    loop(e_units, turn)
    keep = lcopy(own, full_ref.at[c, :, mine, :], in_sem.at[5 + e_units])
    keep.start()
    share = rcopy(
        own, full_ref.at[c, :, mine, :], core_send.at[units, 0], core_recv.at[units, 0], (s, z, 1 - c)
    )
    share.start()
    theirs = full_ref.at[1 - c, :, mine, :]
    share_in = rcopy(theirs, theirs, core_send.at[units, 0], core_recv.at[units, 0], (s, z, 1 - c))
    act_share(1, False)

    for k, j in pk_pairs:
        pk_in(k, j).wait_recv()
    wide = pk_ref.shape[1]
    head_bias[...] = jnp.zeros_like(head_bias)
    vec[...] = jnp.zeros_like(vec)

    def place_one(sh):
        r = lax.broadcasted_iota(jnp.int32, (wide, width), 0)
        col = lax.broadcasted_iota(jnp.int32, (wide, width), 1)
        pick = jnp.where(jnp.logical_and(r < he, col % HD == sh * he + r), 1.0, 0.0).astype(BF16)
        row = lax.broadcasted_iota(jnp.int32, (head_rows, width), 0)
        col = lax.broadcasted_iota(jnp.int32, (head_rows, width), 1)
        own_head = col // HD == row % 8
        for j in range(2):
            head_bias[j] += jnp.where(own_head, mm(pkall[sh, j, :head_rows, :], pick), 0.0)
        r = lax.broadcasted_iota(jnp.int32, (wide, model), 0)
        col = lax.broadcasted_iota(jnp.int32, (wide, model), 1)
        hit = jnp.logical_and(r < rows, col == sh * rows + r)
        vec[...] += mm(pkall[sh, 0, head_rows:, :], jnp.where(hit, 1.0, 0.0).astype(BF16))

    loop(n, place_one)
    for j in range(2):
        for i in range(head_rows // 8):
            bias[i : i + 1, j * width : (j + 1) * width] = jnp.sum(
                head_bias[j, 8 * i : 8 * i + 8, :], 0, keepdims=True
            )
    small[...] = jnp.zeros_like(small)
    vec_copy = lcopy(vec, vec_out, out_sem.at[0])
    vec_copy.start()
    length = len_ref[2 * z + c]
    live_keys = lax.broadcasted_iota(jnp.int32, (1, slots), 1) < length
    lane = lax.broadcasted_iota(jnp.int32, (slots, 128), 1)
    outs = []

    def fetch(u):
        slot = lax.rem(u, 2)
        return [
            lcopy(full_ref.at[hf, u], wbuf.at[slot, :, hf * width : (hf + 1) * width], fetch_sem.at[slot, hf])
            for hf in range(2)
        ]

    def ready(u):
        @pl.when(u == 0)
        def _():
            keep.wait()
            share_in.wait_recv()

        for k in range(1, n):
            core_in(u, k).wait_recv()

    def p_copy(p):
        return lcopy(p_v.at[lax.rem(p, 2)], p_out.at[p], p_sem.at[lax.rem(p, 2)])

    def attention(p):
        at = rows_at(p, 128)
        q, k, v = qkv[0, :, at], qkv[1, :, at], qkv[2, :, at]

        @pl.when(p >= 2)
        def _():
            p_copy(p - 2).wait()

        out = None
        for h in range(2):
            part = lane < HD if h == 0 else lane >= HD
            scores = mm_nt(jnp.where(part, q, 0), k) * HD ** (-0.5)
            scores = jnp.where(live_keys, scores, MASKED)
            e = jnp.exp(scores - jnp.max(scores, -1, keepdims=True))
            low = (e * (1.0 / jnp.sum(e, -1, keepdims=True))).astype(BF16)
            p_v[lax.rem(p, 2), h] = low
            term = mm(low, jnp.where(part, v, 0))
            out = term if out is None else out + term
        o_v[:, at] = out.astype(BF16)
        p_copy(p).start()

    pairs = model // 128
    rb = 128

    def compute(u):
        w = wbuf.at[lax.rem(u, 2)]

        @pl.when(u == 0)
        def _():
            act_arrive(0)

        @pl.when(u < 3)
        def _():
            add = jnp.where(u == 0, bias[0:1, :], jnp.where(u == 2, bias[1:2, :], 0.0))
            qkv[u] = (mm(xv[...], w[...]) + add).astype(BF16)

        @pl.when(u == 3)
        def _():
            acc[...] = mm_nt(o_v[...], w[...]) + xv[...].astype(F32)

            def norm(i):
                at = rows_at(i, rb)
                first = acc[at, :] + vec[8:9, :]
                centred = first - mean(first)
                inv = lax.rsqrt(mean(centred * centred) + EPSILON)
                n1 = centred * inv
                n1_v[at, :] = n1
                r1_v[at, :] = jnp.broadcast_to(inv, (rb, 128))
                up = n1 * vec[10:11, :] + vec[11:12, :]
                ulow_v[at, :] = up.astype(BF16)
                u_v[at, :] = up

            loop(slots // rb, norm)
            for i, (src, dst) in enumerate(
                ((qkv.at[0], q_out), (qkv.at[1], k_out), (qkv.at[2], v_out), (o_v, o_out),
                 (n1_v, n1_out), (r1_v, r1_out), (ulow_v, u_out), (xv, x_out))
            ):
                lcopy(src, dst, out_sem.at[1 + i]).start()

        @pl.when(jnp.logical_and(u >= 4, u < 4 + e_units))
        def _():
            j = u - 4
            pre = mm(ulow_v[...], w[...]) + bias[pl.ds(2 + j, 1), :]
            phi = 0.5 * (1.0 + lax.erf(pre * 0.7071067811865476))
            h_v[j] = (pre * phi).astype(BF16)
            gp_v[j] = (phi + pre * jnp.exp(-0.5 * pre * pre) * 0.3989422804014327).astype(BF16)
            lcopy(h_v.at[j], h_out.at[j], out_sem.at[10]).start()
            lcopy(gp_v.at[j], gp_out.at[j], out_sem.at[11]).start()
            lcopy(h_v.at[j], h_out.at[j], out_sem.at[10]).wait()
            lcopy(gp_v.at[j], gp_out.at[j], out_sem.at[11]).wait()

        @pl.when(u >= 4 + e_units)
        def _():
            u_v[...] += mm_nt(h_v[u - 4 - e_units], w[...])

    def exchange(t):
        @pl.when(t < slots_of_units)
        def _():
            u = unit_at(t)

            @pl.when(t + ahead < slots_of_units)
            def _():
                for k in direct:
                    own_copy(unit_at(t + ahead), k).start()

            for k in direct:
                own_in(u, k).wait_recv()
                if n == 4:
                    fwd_copy(u, 2 - k).start()
                core_copy(u, k).start()

                @pl.when(is_paired(t))
                def _():
                    z_copy(u, k).start()

        if n == 4:
            @pl.when(jnp.logical_and(t > 0, t <= slots_of_units))
            def _():
                u = unit_at(t - 1)
                for h in range(2):
                    fwd_in(u, h).wait_recv()
                core_copy(u, 3).start()

                @pl.when(is_paired(t - 1))
                def _():
                    z_copy(u, 3).start()

        for late, ks in ((2, [k for k in range(1, n) if n != 4 or k < 3]), (3, [3] if n == 4 else [])):
            @pl.when(is_paired(t - late))
            def _(late=late, ks=ks):
                u = theirs_at(t - late)
                for k in ks:
                    z_copy(u, k).wait_recv()
                    core_copy(u, k).start()

        @pl.when(jnp.logical_and(t >= 1, t <= PIECES))
        def _():
            act_some(1, t - 1)

    def first_at(t):
        u = jnp.clip(t - 2, 0, 3)
        for late in (6, 7, 7, 8, 8, 9, 9, 9, 10):
            u = u + jnp.where(t > late, 1, 0)
        return u

    def start_fetch(u):
        ready(u)
        for i in fetch(u):
            i.start()

    def step(t):
        exchange(t)
        first, after = first_at(t), first_at(t + 1)
        pl.when(t == slots_of_units)(lambda: start_fetch(units - 1))

        def one(u, carry):
            for i in fetch(u):
                i.wait()
            pl.when(u + 1 < after)(lambda: start_fetch(u + 1))
            compute(u)
            return carry

        lax.fori_loop(first, after, one, 0)
        pl.when(jnp.logical_or(t == 4, t == 5))(
            lambda: loop(pairs // 2, lambda p: attention(p + (t - 4) * (pairs // 2)))
        )
        pl.when(jnp.logical_and(first_at(t + 2) > after, t + 1 < slots_of_units))(lambda: start_fetch(after))

    loop(slots_of_units + 1, step)

    act_arrive(1)

    def norm2(i):
        at = rows_at(i, rb)
        second = u_v[at, :] + vec[9:10, :]
        centred = second - mean(second)
        inv = lax.rsqrt(mean(centred * centred) + EPSILON)
        n2 = centred * inv
        gain = vec[12:13, :]
        y_v[at, :] = (n2 * gain + vec[13:14, :]).astype(BF16)
        row = lax.broadcasted_iota(jnp.int32, (rb, 1), 0) + i * rb
        grad = jnp.where(row < length, cotv[at, :].astype(F32), 0.0)
        scaled = grad * gain
        back = inv * (scaled - mean(scaled) - n2 * mean(scaled * n2))
        acc[at, :] = back
        low = back.astype(BF16)
        dz_v[at, :] = low
        for r, v in ((14, low.astype(F32)), (20, grad * n2), (22, grad)):
            v = jnp.sum(v, 0, keepdims=True)
            small[r : r + 1, :] += v[:, :width]
            small[r + 1 : r + 2, :] += v[:, width:]

    loop(slots // rb, norm2)
    last = [
        lcopy(src, dst, out_sem.at[12 + i])
        for i, (src, dst) in enumerate(((acc, ds_out), (dz_v, dz_out), (y_v, y_out), (small, small_out)))
    ]
    for i in last:
        i.start()

    def sent(t):
        u = unit_at(t)
        for k in direct:
            own_copy(u, k).wait_send()
        if n == 4:
            for h in range(2):
                fwd_copy(u, h).wait_send()

        @pl.when(is_paired(t))
        def _():
            for k in range(1, n):
                z_copy(u, k).wait_send()

    loop(slots_of_units, sent)

    def passed(u):
        for k in range(1, n):
            core_copy(u, k).wait_send()

    loop(units, passed)
    share.wait_send()
    for k, j in pk_pairs:
        pk_copy(k, j).wait_send()
    for which in range(2):
        for k in range(1, nz):
            loop(PIECES, lambda i: act(which, k, i).wait_send())
    vec_copy.wait()
    for p in (pairs - 2, pairs - 1):
        p_copy(p).wait()
    for i, (src, dst) in enumerate(
        ((qkv.at[0], q_out), (qkv.at[1], k_out), (qkv.at[2], v_out), (o_v, o_out),
         (n1_v, n1_out), (r1_v, r1_out), (ulow_v, u_out), (xv, x_out))
    ):
        lcopy(src, dst, out_sem.at[1 + i]).wait()
    for i in last:
        i.wait()


def forward(n, nz, lengths, inputs, cotangent, wq, wk, wv, wo, we, wr, heads, vectors):
    seqs, block, model = inputs.shape
    rows = wq.shape[0]
    e_units = we.shape[1] // UNIT
    units = 4 + 2 * e_units
    slots = nz * block
    head_rows = sum(v.shape[0] for v in heads)
    pk = (head_rows + 16, max(rows, 128))
    outs = [
        ((2, units, model, UNIT), BF16), ((slots, model), BF16),
        ((slots, model), BF16), ((slots, model), BF16), ((slots, model), BF16), ((slots, model), BF16),
        ((model // 128, 2, slots, slots), BF16), ((slots, model), F32), ((slots, 128), F32), ((slots, model), BF16),
        ((e_units, slots, model), BF16), ((e_units, slots, model), BF16),
        ((slots, model), F32), ((slots, model), BF16), ((slots, model), BF16), ((16, model), F32),
        ((24, UNIT), F32),
    ]
    scratch = [
        ((units, rows, UNIT), BF16), (wo.shape, BF16), (wr.shape, BF16), ((nz, block, model), F32),
        ((2, nz, block, model), BF16), ((slots, model), BF16), ((slots, model), BF16), ((3, slots, model), BF16),
        ((slots, model), BF16), ((2, 2, slots, slots), BF16), ((slots, model), F32), ((slots, 128), F32),
        ((slots, model), F32), ((slots, model), BF16), ((e_units, slots, model), BF16),
        ((e_units, slots, model), BF16), ((slots, model), F32),
        ((slots, model), BF16), ((slots, model), BF16), ((2, model, 2 * UNIT), BF16),
        (pk, BF16), (pk, F32), ((n, 2, *pk), BF16), ((2, head_rows, UNIT), F32), ((16, 2 * UNIT), F32), ((16, model), F32), ((24, UNIT), F32),
    ]
    return pl.pallas_call(
        functools.partial(forward_kernel, n, nz),
        name="gather_and_forward",
        out_shape=[jax.ShapeDtypeStruct(a, b) for a, b in outs],
        in_specs=[SMEM] + [ANY] * 8 + [VMEM] * 9,
        out_specs=[ANY] * len(outs),
        scratch_shapes=[pltpu.VMEM(a, b) for a, b in scratch]
        + [
            DMA((units, n)), DMA((units, n)), DMA((units, 2)), DMA((units, 2)),
            DMA((units + 1, n)), DMA((units + 1, n)), DMA((units, n)), DMA((units, n)),
            DMA((2, nz, PIECES)), DMA((2, nz, PIECES)),
            DMA((n, 2)), DMA((n, 2)), DMA((6 + e_units,)), DMA((nz,)), DMA((2, 2)), DMA((16,)), DMA((2,)),
        ],
        compiler_params=pltpu.CompilerParams(
            collective_id=0, has_side_effects=True, vmem_limit_bytes=60 * 2**20
        ),
    )(lengths, inputs, cotangent, wq, wk, wv, wo, we, wr, *heads, *vectors)


def backward_kernel(
    n, nz,
    full_ref, x_ref, q_ref, k_ref, v_ref, o_ref, p_ref, n1_ref, r1_ref, u_ref, h_ref, gp_ref,
    ds_ref, dz_ref, y_ref, vec_ref, small_ref,
    grad_ref, ys_ref, dx_ref, small_out, part_ref, got_ref,
    x_v, qkv, o_v, p_v, n1_v, r1_v, u_v, dz_v, du, wr_v, we_v, h_v, gp_v, dpre, pbuf, small, round_in,
    stage, gstage, total, near, pair_sum, far, up, across, down, block_out,
    load_sem, w_sem, p_sem, part_sem, core_send, core_recv, stage_sem, near_send, near_recv, far_send, far_recv,
    z_send, z_recv, store_sem, act_send, act_recv, pass_send, pass_recv, keep_sem, small_send, small_recv,
):
    s, z, c = place()
    units = part_ref.shape[0]
    subs = 2 * units
    e_units = h_ref.shape[0]
    model = total.shape[1]
    width = UNIT
    rows = model // n
    half = rows // 2
    slots = x_v.shape[0]
    block = slots // nz
    zrows = rows_at(z, block)
    mates = [(dz_ref, dz_v), (small_ref, small), (ds_ref, du), (n1_ref, n1_v), (r1_ref, r1_v), (o_ref, o_v),
             (u_ref, u_v), (q_ref, qkv.at[0]), (k_ref, qkv.at[1]), (v_ref, qkv.at[2]), (x_ref, x_v)]
    loads = [lcopy(a, b, load_sem.at[i]) for i, (a, b) in enumerate(mates)]

    class Weights:
        def __init__(self, buf, i):
            self.buf, self.i = buf, i

        def copies(self, u):
            return [
                lcopy(full_ref.at[hf, u], self.buf.at[:, hf * width : (hf + 1) * width], w_sem.at[self.i, hf])
                for hf in range(2)
            ]

        def start(self, u):
            for i in self.copies(u):
                i.start()

        def wait(self, u):
            for i in self.copies(u):
                i.wait()

    wr, we = Weights(wr_v, 0), Weights(we_v, 1)

    def load_h(j):
        return lcopy(h_ref.at[j], h_v, w_sem.at[2, 0])

    def load_gp(j):
        return lcopy(gp_ref.at[j], gp_v, w_sem.at[2, 1])

    def load_p(p):
        return lcopy(p_ref.at[p], p_v.at[lax.rem(p, 2)], p_sem.at[lax.rem(p, 2)])

    loads[0].start()
    load_h(0).start()
    loads[1].start()
    load_gp(0).start()
    wr.start(4 + e_units)
    we.start(4)
    for i in loads[2:]:
        i.start()
    for p in range(2):
        load_p(p).start()
    greet(
        [(s ^ k, z, c) for k in range(1, n)]
        + [(s, z, 1 - c)]
        + [(s, lax.rem(z + k, nz), c) for k in range(1, nz)]
    )

    def act(which, k, i):
        src, dst = ((y_ref, ys_ref), (dz_v, dx_ref))[which]
        to = lax.rem(z + k, nz)
        some = block // PIECES
        return rcopy(
            src.at[pl.ds(pl.multiple_of(to * block + i * some, some), some), :],
            dst.at[2 * z + c, rows_at(i, some), :],
            act_send.at[which, k, i], act_recv.at[which, k, i], (s, to, c),
        )

    def act_in(which, k, i):
        src = lax.rem(z + nz - k, nz)
        at = (ys_ref, dx_ref)[which].at[2 * src + c, rows_at(i, block // PIECES), :]
        return rcopy(at, at, act_send.at[which, k, i], act_recv.at[which, k, i], (s, src, c))

    def act_keep(which):
        src, dst = ((y_ref, ys_ref), (dz_v, dx_ref))[which]
        return lcopy(src.at[zrows, :], dst.at[2 * z + c], keep_sem.at[which])

    def pass_copy(which, k):
        at = (ys_ref, dx_ref)[which].at[2 * lax.rem(z + nz - k, nz) + c]
        return rcopy(at, at, pass_send.at[which, k], pass_recv.at[which, k], (s, z, 1 - c))

    def pass_in(which, k):
        at = (ys_ref, dx_ref)[which].at[2 * lax.rem(z + nz - k, nz) + 1 - c]
        return rcopy(at, at, pass_send.at[which, k], pass_recv.at[which, k], (s, z, 1 - c))

    def act_some(which, i):
        for k in range(1, nz):
            act(which, k, i).start()

    def act_pass(which):
        for k in range(1, nz):
            loop(PIECES, lambda i: act_in(which, k, i).wait_recv())
            pass_copy(which, k).start()
        act_keep(which).wait()
        pass_copy(which, 0).start()

    act_keep(0).start()

    def core_copy(u):
        return rcopy(pbuf.at[0], got_ref.at[u], core_send.at[u], core_recv.at[u], (s, z, 1 - c))

    def core_in(u):
        return rcopy(got_ref.at[u], got_ref.at[u], core_send.at[u], core_recv.at[u], (s, z, 1 - c))

    def part_copy(u):
        return lcopy(pbuf.at[1 + lax.rem(u, 3)], part_ref.at[u], part_sem.at[lax.rem(u, 3)])

    def emit(u, i, value):
        low = value.astype(BF16)
        for b in range(2):
            pbuf[jnp.where(i == 0, 0, 1 + lax.rem(u, 3)), b] = low[:, b * SUB : (b + 1) * SUB]

    def produce(u, make):
        pl.when(u > 0)(lambda: core_copy(u - 1).wait_send())

        def one(i):
            emit(u, i, make(lax.rem(1 - c + i, 2)))

            @pl.when(i == 0)
            def _():
                core_copy(u).start()

        loop(2, one)
        part_copy(u).start()

    lane = lax.broadcasted_iota(jnp.int32, (slots, 128), 1)
    rb = 128
    last_e = e_units - 1

    def cols(hf):
        return rows_at(hf, width)

    def add_small(r, v):
        v = jnp.sum(v, 0, keepdims=True)
        for hf in range(2):
            small[pl.ds(r[hf], 1), :] += v[:, hf * width : (hf + 1) * width]

    def make_r(j):
        load_h(j).wait()
        produce(j, lambda hf: mm_tn(dz_v[...], h_v[:, cols(hf)]))

        @pl.when(j < last_e)
        def _():
            load_h(j + 1).start()

    def make_dpre(j):
        wr.wait(4 + e_units + j)
        load_gp(j).wait()
        low = (mm(dz_v[...], wr_v[...]) * gp_v[...].astype(F32)).astype(BF16)
        dpre[j] = low
        add_small((4 + j, 4 + e_units + j), low.astype(F32))

        @pl.when(j < last_e)
        def _():
            wr.start(5 + e_units + j)
            load_gp(j + 1).start()

        @pl.when(j == last_e)
        def _():
            wr.start(3)

    def make_du(j):
        we.wait(4 + j)
        du[...] += mm_nt(dpre[j], we_v[...])

        @pl.when(j < last_e)
        def _():
            we.start(5 + j)

        @pl.when(j == last_e)
        def _():
            we.start(1)

    def make_e(u, j):
        produce(u, lambda hf: mm_tn(u_v[...], dpre[j, :, cols(hf)]))

    def norm(i):
        at = rows_at(i, rb)
        grad = du[at, :]
        n1 = n1_v[at, :]
        scaled = grad * vec_ref[10:11, :]
        back = r1_v[at, 0:1] * (scaled - mean(scaled) - n1 * mean(scaled * n1))
        du[at, :] = back
        low = back.astype(BF16)
        dz_v[at, :] = low
        for r, v in ((12, low.astype(F32)), (16, grad * n1), (18, grad)):
            add_small((r, r + 1), v)

    def make_o():
        for i in loads[3:6]:
            i.wait()
        loop(slots // rb, norm)
        produce(e_units, lambda hf: mm_tn(dz_v[...], o_v[:, cols(hf)]))

    def make_do():
        wr.wait(3)
        o_v[...] = mm(dz_v[...], wr_v[...]).astype(BF16)
        wr.start(0)

    def attention(p):
        at = rows_at(p, 128)
        q, k, v, do = qkv[0, :, at], qkv[1, :, at], qkv[2, :, at], o_v[:, at]
        load_p(p).wait()
        dq = dk = dv = None
        for h in range(2):
            part = lane < HD if h == 0 else lane >= HD
            qh, kh, doh = jnp.where(part, q, 0), jnp.where(part, k, 0), jnp.where(part, do, 0)
            low = p_v[lax.rem(p, 2), h]
            probs = low.astype(F32)
            dp = mm_nt(doh, v)
            ds = (probs * (dp - jnp.sum(dp * probs, -1, keepdims=True))).astype(BF16)
            tv, tk, tq = mm_tn(low, doh), mm_tn(ds, qh), mm(ds, kh)
            dv, dk, dq = (tv, tk, tq) if h == 0 else (dv + tv, dk + tk, dq + tq)
        qkv[0, :, at] = (dq * HD ** (-0.5)).astype(BF16)
        qkv[1, :, at] = (dk * HD ** (-0.5)).astype(BF16)
        qkv[2, :, at] = dv.astype(BF16)

        @pl.when(p + 2 < pairs)
        def _():
            load_p(p + 2).start()

    pairs = model // 128

    def make_w(u, i):
        produce(u, lambda hf: mm_tn(x_v[...], qkv[i, :, cols(hf)]))

    def make_dx(i, weights):
        weights.wait(i)
        du[...] += mm_nt(qkv[i], weights.buf[...])
        if i != 1:
            add_small((i, i + 1), qkv[i].astype(F32))

    def one_of(t, ticks):
        hit = t == ticks[0]
        for i in ticks[1:]:
            hit = jnp.logical_or(hit, t == i)
        return hit

    makes = {0: 0, 1: 1, 2: 2, 3: 3, 4: 4, 6: 5, 7: 6, 8: 7, 10: 8, 11: 9, 12: 10, 13: 11}

    def unit_of(t):
        return t - jnp.where(t > 4, 1, 0) - jnp.where(t > 9, 1, 0)

    def compute(t):
        @pl.when(t == 0)
        def _():
            loads[0].wait()
            loads[1].wait()

        pl.when(t < 4)(lambda: make_r(t))
        pl.when(t == 1)(lambda: loads[2].wait())
        pl.when(jnp.logical_and(t > 0, t < 5))(lambda: make_du(t - 1))
        pl.when(t < 4)(lambda: make_dpre(t))
        pl.when(t == 4)(make_o)

        @pl.when(t == 5)
        def _():
            make_do()
            for i in loads[6:]:
                i.wait()

        pl.when(jnp.logical_and(t > 4, t < 9))(lambda: loop(2, lambda i: attention(2 * (t - 5) + i)))

        @pl.when(one_of(t, (6, 7, 12, 13)))
        def _():
            make_e(unit_of(t), t - jnp.where(t > 7, 10, 6))

        @pl.when(one_of(t, (8, 10, 11)))
        def _():
            make_w(unit_of(t), t - jnp.where(t > 8, 9, 8))

        @pl.when(t == 9)
        def _():
            make_dx(0, wr)
            wr.start(2)
            make_dx(1, we)
            make_dx(2, wr)
            dz_v[...] = du[...].astype(BF16)
            act_keep(1).start()

    def loads_of(w):
        slot = lax.rem(w, 2)
        u, b = w // 2, lax.rem(w, 2)
        return [
            lcopy(part_ref.at[u, b], stage.at[slot], stage_sem.at[slot, 0]),
            lcopy(got_ref.at[u, b], gstage.at[slot], stage_sem.at[slot, 1]),
        ]

    def blk(k):
        return rows_at(s ^ k, rows)

    def blk_half(k, h):
        return pl.ds(pl.multiple_of((s ^ k) * rows + h * half, half), half)

    def near_copy(w, h, i):
        k = (1 + h, 3)[i]
        return rcopy(
            total.at[lax.rem(w, SLOTS), blk_half(k, h), :], near.at[w, h, i],
            near_send.at[w, h, i], near_recv.at[w, h, i], (s ^ (1 + h), z, c),
        )

    def far_copy(w, h):
        return rcopy(
            pair_sum.at[w, h], far.at[w, h], far_send.at[w, h], far_recv.at[w, h], (s ^ (2 - h), z, c)
        )

    def straight(w, k):
        return rcopy(
            total.at[lax.rem(w, SLOTS), blk(k), :], near.at[w, k - 1],
            near_send.at[w, k - 1], near_recv.at[w, k - 1], (s ^ k, z, c),
        )

    def sends_of(w):
        if n == 4:
            return [near_copy(w, h, i) for h in range(2) for i in range(2)]
        return [straight(w, k) for k in range(1, n)]

    def z_to(w, h, src, dst, i, to):
        at = pl.ds(h * half, half)
        return rcopy(src.at[w, at], dst.at[w, at], z_send.at[w, i, h], z_recv.at[w, i, h], (s, to, c))

    last = nz - 1
    edge = jnp.logical_or(z == 0, z == last)
    inner = jnp.where(z == 0, 1, nz - 2)
    outer = jnp.where(z == 1, 0, last)
    other = jnp.where(z == 1, 2, 1)

    def s0(w):
        @pl.when(lax.rem(w, 2) == 0)
        def _():
            part_copy(w // 2).wait()
            core_in(w // 2).wait_recv()

        for i in loads_of(w):
            i.start()

    def s1(w):
        @pl.when(w >= SLOTS)
        def _():
            for i in sends_of(w - SLOTS):
                i.wait_send()

        for i in loads_of(w):
            i.wait()
        slot, to = lax.rem(w, 2), lax.rem(w, SLOTS)

        def add(i):
            at = rows_at(i, 256)
            total[to, at, :] = (stage[slot, at, :].astype(F32) + gstage[slot, at, :].astype(F32)).astype(BF16)

        loop(model // 256, add)
        for i in sends_of(w):
            i.start()

    def s2(w):
        slot = lax.rem(w, SLOTS)
        for i in sends_of(w):
            i.wait_recv()
        if n == 4:
            for h in range(2):
                pair_sum[w, h] = (
                    total[slot, blk_half(2 - h, h), :].astype(F32) + near[w, h, 1].astype(F32)
                ).astype(BF16)
                far_copy(w, h).start()

    def s3(w):
        slot = lax.rem(w, SLOTS)
        if n != 4:
            acc = total[slot, blk(0), :].astype(F32)
            for k in range(1, n):
                acc = acc + near[w, k - 1].astype(F32)
            block_out[w] = acc.astype(BF16)
        for h in range(2):
            if n == 4:
                far_copy(w, h).wait_recv()
                block_out[w, h * half : (h + 1) * half] = (
                    total[slot, blk_half(0, h), :].astype(F32) + near[w, h, 0].astype(F32) + far[w, h].astype(F32)
                ).astype(BF16)
            pl.when(edge)(lambda: z_to(w, h, block_out, up, 0, inner).start())

    def s4(w):
        @pl.when(jnp.logical_not(edge))
        def _():
            for h in range(2):
                at = pl.ds(h * half, half)
                z_to(w, h, block_out, up, 0, outer).wait_recv()
                block_out[w, at] = (block_out[w, at].astype(F32) + up[w, at].astype(F32)).astype(BF16)
                z_to(w, h, block_out, across, 1, other).start()

    def s5(w):
        @pl.when(jnp.logical_not(edge))
        def _():
            for h in range(2):
                at = pl.ds(h * half, half)
                z_to(w, h, block_out, across, 1, other).wait_recv()
                down[w, at] = (block_out[w, at].astype(F32) + across[w, at].astype(F32)).astype(BF16)
                z_to(w, h, down, down, 2, outer).start()

    def s6(w):
        @pl.when(edge)
        def _():
            for h in range(2):
                z_to(w, h, down, down, 2, inner).wait_recv()

        lcopy(down.at[w], grad_ref.at[w], store_sem.at[w]).start()

    stages = list(zip(LAGS, (s0, s3, s2, s1, s6, s5, s4)))

    def serve(w):
        for lag, stage_of in stages:
            @pl.when(jnp.logical_and(w >= lag, w - lag < subs))
            def _(stage_of=stage_of, lag=lag):
                stage_of(w - lag)

    hops = [(s, z, 1 - c)]
    hops += [(s ^ (1 << b), z, c) for b in range(n.bit_length() - 1)]
    hops += [(s, z ^ (1 << b), c) for b in range(nz.bit_length() - 1)]

    def small_copy(i):
        return rcopy(small, round_in.at[i], small_send.at[i], small_recv.at[i], hops[i])

    done = max(makes) + 2

    def served(t):
        return jnp.clip(2 * (t - 1), 0, 4) + jnp.maximum(PACE * (t - 3) // 4, 0)

    def step(t):
        lax.fori_loop(served(t), served(t + 1), lambda w, carry: (serve(w), carry)[1], 0)
        pl.when(t <= max(makes))(lambda: compute(t))

        for which, first in enumerate(ACTS):
            pl.when(jnp.logical_and(t >= first, t < first + PIECES))(lambda: act_some(which, t - first))

        @pl.when(t == PIECES)
        def _():
            act_pass(0)

        @pl.when(t == PASS)
        def _():
            act_pass(1)

        for i in range(len(hops) + 1):
            @pl.when(t == done + i)
            def _(i=i):
                if i > 0:
                    small_copy(i - 1).wait_send()
                    small_copy(i - 1).wait_recv()
                    small[...] += round_in[i - 1]
                if i < len(hops):
                    small_copy(i).start()
                else:
                    lcopy(small, small_out, keep_sem.at[2]).start()

    ticks = (4 * (subs + max(LAGS) - 4) + PACE - 1) // PACE + 3
    loop(ticks, step)

    def finish(w):
        if n == 4:
            for h in range(2):
                far_copy(w, h).wait_send()

        for h in range(2):
            pl.when(edge)(lambda: z_to(w, h, block_out, up, 0, inner).wait_send())

            @pl.when(jnp.logical_not(edge))
            def _():
                z_to(w, h, block_out, across, 1, other).wait_send()
                z_to(w, h, down, down, 2, outer).wait_send()

        lcopy(down.at[w], grad_ref.at[w], store_sem.at[w]).wait()

    loop(subs, finish)
    core_copy(units - 1).wait_send()
    for w in range(subs - SLOTS, subs):
        for i in sends_of(w):
            i.wait_send()
    for which in range(2):
        for k in range(1, nz):
            loop(PIECES, lambda i: act(which, k, i).wait_send())
        for k in range(nz):
            pass_copy(which, k).wait_send()
            pass_in(which, k).wait_recv()
    lcopy(small, small_out, keep_sem.at[2]).wait()


def backward(n, nz, full, x, q, k, v, o, p, n1, r1, u, h, gp, ds, dz, y, vec, small):
    _, units, model, width = full.shape
    e_units = h.shape[0]
    rows = model // n
    half = rows // 2
    slots = x.shape[0]
    block = slots // nz
    subs = 2 * units
    near = (subs, 2, 2, half, SUB) if n == 4 else (subs, n - 1, rows, SUB)
    near_sems = near[:3] if n == 4 else near[:2]
    far = (subs, 2, half, SUB) if n == 4 else (1, 2, 16, SUB)
    blocks = (subs, rows, SUB)
    hops = 1 + (n.bit_length() - 1) + (nz.bit_length() - 1)
    outs = [
        (blocks, BF16), ((2 * nz, block, model), BF16), ((2 * nz, block, model), BF16), ((24, UNIT), F32),
        ((units, 2, model, SUB), BF16), ((units, 2, model, SUB), BF16),
    ]
    scratch = [
        ((slots, model), BF16), ((3, slots, model), BF16), ((slots, model), BF16), ((2, 2, slots, slots), BF16),
        ((slots, model), F32), ((slots, 128), F32), ((slots, model), BF16), ((slots, model), BF16),
        ((slots, model), F32), ((model, 2 * UNIT), BF16), ((model, 2 * UNIT), BF16), ((slots, model), BF16),
        ((slots, model), BF16), ((e_units, slots, model), BF16), ((4, 2, model, SUB), BF16), ((24, UNIT), F32),
        ((hops, 24, UNIT), F32),
        ((2, model, SUB), BF16), ((2, model, SUB), BF16), ((SLOTS, model, SUB), BF16),
        (near, BF16), (far, BF16), (far, BF16), (blocks, BF16), (blocks, BF16), (blocks, BF16), (blocks, BF16),
    ]
    return pl.pallas_call(
        functools.partial(backward_kernel, n, nz),
        name="backward_and_reduce",
        out_shape=[jax.ShapeDtypeStruct(a, b) for a, b in outs],
        in_specs=[ANY] * 15 + [VMEM, ANY],
        out_specs=[ANY] * len(outs),
        scratch_shapes=[pltpu.VMEM(a, b) for a, b in scratch]
        + [
            DMA((12,)), DMA((3, 2)), DMA((2,)), DMA((3,)), DMA((units,)), DMA((units,)), DMA((2, 2)),
            DMA(near_sems), DMA(near_sems), DMA((subs, 2)), DMA((subs, 2)),
            DMA((subs, 3, 2)), DMA((subs, 3, 2)), DMA((subs,)),
            DMA((2, nz, PIECES)), DMA((2, nz, PIECES)), DMA((2, nz)), DMA((2, nz)), DMA((3,)), DMA((hops,)), DMA((hops,)),
        ],
        compiler_params=pltpu.CompilerParams(
            collective_id=1, has_side_effects=True, vmem_limit_bytes=61 * 2**20
        ),
    )(full, x, q, k, v, o, p, n1, r1, u, h, gp, ds, dz, y, vec, small)


def finish_kernel(
    n, grad_ref, ys_ref, dx_ref, small_ref,
    y_out, dx_out, dq_out, dk_out, dv_out, do_out, de_out, dr_out,
    qb_out, vb_out, eb_out, ob_out, rb_out, g1_out, s1_out, g2_out, s2_out,
    grads, act, act_wide, dq, dk, dv, do, de, dr, in_sem, out_sem, act_in, act_out,
):
    s, _, c = place()
    rows = dq.shape[0]
    seqs = act.shape[1]
    e_units = de.shape[1] // UNIT
    he = HD // n
    load = lcopy(grad_ref, grads, in_sem)
    load.start()

    def act_load(i, which):
        return lcopy((ys_ref, dx_ref)[which].at[i], act.at[which, i], act_in.at[which, i])

    def act_store(i, which):
        return lcopy(act_wide.at[which, i], (y_out, dx_out)[which].at[i], act_out.at[which, i])

    for which in range(2):
        loop(seqs, lambda i: act_load(i, which).start())
    load.wait()
    stores = []

    def store(src, dst):
        stores.append(lcopy(src, dst, out_sem.at[len(stores)]))
        stores[-1].start()

    def part(u, b):
        return grads[2 * u + b].astype(F32)

    spots = [e_units + 1, e_units + 2, e_units + 6, e_units + 7]
    for j in range(e_units):
        for b in range(2):
            at = j * UNIT + b * SUB
            dr[at : at + SUB, :] = part(j, b).T
            de[:, at : at + SUB] = part(spots[j], b)
    store(dr, dr_out)
    store(de, de_out)
    for i, (v, out) in enumerate(((dq, dq_out), (dk, dk_out), (dv, dv_out))):
        for b in range(2):
            v[:, b * SUB : (b + 1) * SUB] = part(e_units + 3 + i, b)
        store(v, out)
    for b in range(2):
        do[b * SUB : (b + 1) * SUB, :] = part(e_units, b).T
    store(do, do_out)
    for which in range(2):
        def widen(i):
            act_load(i, which).wait()
            act_wide[which, i] = act[which, i].astype(F32)
            act_store(i, which).start()

        loop(seqs, widen)

    at = lax.rem(UNIT - s * he, UNIT)
    turned = pltpu.roll(small_ref[...], at, 1)
    for out, base, count in ((qb_out, 0, 1), (vb_out, 2, 1), (eb_out, 4, e_units)):
        for i in range(count):
            line = jnp.where(c == 0, turned[base + i : base + i + 1, :], turned[base + count + i : base + count + i + 1, :])
            for h in range(8):
                out[8 * i + h : 8 * i + h + 1, :] = line[:, h * HD : h * HD + he]
    at = lax.rem(UNIT - lax.rem(s * rows, UNIT), UNIT)
    turned = pltpu.roll(small_ref[...], at, 1)
    late = s * rows >= UNIT
    for i, out in enumerate((ob_out, rb_out, g1_out, s1_out, g2_out, s2_out)):
        r = 4 + 2 * e_units + 2 * i
        line = jnp.where(late, turned[r + 1 : r + 2, :], turned[r : r + 1, :])
        out[...] = line[:, :rows].reshape(rows)
    for i in stores:
        i.wait()
    for which in range(2):
        loop(seqs, lambda i: act_store(i, which).wait())


def finish(n, grads, ys, dx, small, heads):
    _, rows, _ = grads.shape
    seqs, block, model = ys.shape
    wide = heads[2].shape[0] // 8 * UNIT
    square, tall = (rows, UNIT), (UNIT, rows)
    outs = [ys.shape, ys.shape, square, square, square, tall, (rows, wide), (wide, rows)]
    small_outs = [v.shape for v in heads] + [(rows,)] * 6
    return pl.pallas_call(
        functools.partial(finish_kernel, n),
        name="widen_results",
        out_shape=[jax.ShapeDtypeStruct(a, F32) for a in outs + small_outs],
        in_specs=[ANY] * 3 + [VMEM],
        out_specs=[ANY] * len(outs) + [VMEM] * len(small_outs),
        scratch_shapes=[pltpu.VMEM(grads.shape, BF16), pltpu.VMEM((2, *ys.shape), BF16), pltpu.VMEM((2, *ys.shape), F32)]
        + [pltpu.VMEM(a, F32) for a in outs[2:]]
        + [DMA, DMA((6,)), DMA((2, seqs)), DMA((2, seqs))],
        compiler_params=pltpu.CompilerParams(vmem_limit_bytes=61 * 2**20),
    )(grads, ys, dx, small)


def body(n, nz, inputs, lengths, wq, wk, wv, wo, we, wr, qb, vb, eb, ob, rb, g1, s1, g2, s2, cotangent):
    heads = (qb, vb, eb)
    (full, x, q, k, v, o, p, n1, r1, u, h, gp, ds, dz, y, vec, small) = forward(
        n, nz, lengths, inputs, cotangent, wq, wk, wv, wo, we, wr, heads, (ob, rb, g1, s1, g2, s2)
    )
    grads, ys, dx, small, _, _ = backward(
        n, nz, full, x, q, k, v, o, p, n1, r1, u, h, gp, ds, dz, y, vec, small
    )
    return tuple(finish(n, grads, ys, dx, small, heads))


def solution(mesh):
    w, wt, v = P("shard", "tp"), P("tp", "shard"), P("shard")
    rows = P("shard", "ctx", None)
    return jax.shard_map(
        functools.partial(body, mesh.shape["shard"], mesh.shape["ctx"]),
        mesh=mesh,
        in_specs=(rows, v, w, w, w, wt, w, wt, wt, wt, wt, v, v, v, v, v, v, rows),
        out_specs=(rows, rows, w, w, w, wt, w, wt, wt, wt, wt, v, v, v, v, v, v),
        check_vma=False,
    )
```

```python
import functools

import jax
import jax.numpy as jnp
from jax import lax
from jax.experimental import pallas as pl
from jax.experimental.pallas import tpu as pltpu
from jax.sharding import PartitionSpec as P

HD = 64
UNIT = 512
SUB = 256
SLOTS = 4
LAGS = (0, 5, 3, 1, 11, 9, 7)
PACE = 5
PASS = 22
PIECES = 8
ACTS = (0, 10)
EPSILON = 1e-05
MASKED = -1e30
MESH = pl.DeviceIdType.MESH
F32 = jnp.float32
BF16 = jnp.bfloat16
DMA = pltpu.SemaphoreType.DMA
ANY = pl.BlockSpec(memory_space=pl.ANY)
VMEM = pl.BlockSpec(memory_space=pltpu.VMEM)
SMEM = pl.BlockSpec(memory_space=pltpu.SMEM)


def place():
    return lax.axis_index("shard"), lax.axis_index("ctx"), lax.axis_index("tp")


def rcopy(src, dst, send, recv, dev):
    return pltpu.make_async_remote_copy(
        src_ref=src, dst_ref=dst, send_sem=send, recv_sem=recv, device_id=dev, device_id_type=MESH
    )


def lcopy(src, dst, sem):
    return pltpu.make_async_copy(src, dst, sem)


def greet(devices):
    barrier = pltpu.get_barrier_semaphore()
    for dev in devices:
        pl.semaphore_signal(barrier, inc=1, device_id=dev, device_id_type=MESH)
    pl.semaphore_wait(barrier, len(devices))


def rows_at(i, size):
    return pl.ds(pl.multiple_of(i * size, size), size)


def mm(a, b):
    return jnp.dot(a, b, preferred_element_type=F32)


def mm_nt(a, b):
    return lax.dot_general(a, b, (((1,), (1,)), ((), ())), preferred_element_type=F32)


def mm_tn(a, b):
    return lax.dot_general(a, b, (((0,), (0,)), ((), ())), preferred_element_type=F32)


def loop(count, fn):
    def step(i, carry):
        fn(i)
        return carry

    lax.fori_loop(0, count, step, 0)


def mean(v):
    return jnp.mean(v, -1, keepdims=True)


def layer_kernel(
    n, nz,
    len_ref, x_ref, g_ref, wq_ref, wk_ref, wv_ref, wo_ref, we_ref, wr_ref,
    qb_ref, vb_ref, eb_ref, ob_ref, rb_ref, g1_ref, s1_ref, g2_ref, s2_ref,
    grad_ref, ys_ref, dx_ref, small_out, full_ref, p_ref, part_ref, got_ref,
    own, turn_in, xv, cotv, qkv, o_v, p_v, n1_v, r1_v, u_v, ulow_v, h_v, gp_v, dz_v, wbuf,
    pk_ref, pk_wide, turned, pkall, head_bias, bias, vec, small,
    pbuf, round_in, stage, gstage, total, near, pair_sum, far, up, across,
    own_send, own_recv, fwd_send, fwd_recv, core_send, core_recv, z_send, z_recv, act_send, act_recv,
    pk_send, pk_recv, in_sem, turn_sem, act_sem, fetch_sem, p_sem,
    *later_sems,
):
    s, z, c = place()
    units, rows, width = own.shape
    half = rows // 2
    model = rows * n
    slots = xv.shape[0]
    block = slots // nz
    e_units = we_ref.shape[1] // width
    group = [(s ^ k, z, c if j == 0 else 1 - c) for k in range(n) for j in range(2) if k + j > 0]
    mine = rows_at(s, rows)
    zrows = rows_at(z, block)

    ins = [lcopy(r, own.at[i], in_sem.at[i]) for i, r in enumerate((wq_ref, wk_ref, wv_ref))]
    ins += [
        lcopy(we_ref.at[:, pl.ds(j * width, width)], own.at[4 + j], in_sem.at[3 + j]) for j in range(e_units)
    ]
    tall = [(wo_ref, 3)] + [(wr_ref.at[rows_at(j, width), :], 4 + e_units + j) for j in range(e_units)]
    ins_t = [lcopy(r, turn_in.at[i % 2], turn_sem.at[i % 2]) for i, (r, _) in enumerate(tall)]

    def to(k):
        return lax.rem(z + k, nz)

    def act_load(which, k):
        src = (x_ref, g_ref)[which]
        return lcopy(src.at[2 * to(k) + c], u_v.at[rows_at(k, block), :], act_sem.at[k])

    chunks = model // SUB

    def held(which, k, i):
        q = (which * (nz - 1) + k - 1) * chunks
        return pbuf.at[q // 16, (q // 8) % 2, rows_at(q % 8 + i, block), :]

    def act(which, k, i):
        dst = (xv, cotv)[which]
        return rcopy(
            held(which, k, i), dst.at[zrows, rows_at(i, SUB)],
            act_send.at[which, k, i], act_recv.at[which, k, i], (s, to(k), c),
        )

    def act_in(which, k, i):
        at = (xv, cotv)[which].at[rows_at(lax.rem(z + nz - k, nz), block), rows_at(i, SUB)]
        return rcopy(at, at, act_send.at[which, k, i], act_recv.at[which, k, i], (s, lax.rem(z + nz - k, nz), c))

    def act_some(which, i):
        for k in range(1, nz):
            act(which, k, i).start()

    def act_share(which, send):
        for k in range(1, nz):
            act_load(which, k).wait()
            for i in range(chunks):
                held(which, k, i)[...] = u_v[rows_at(k, block), i * SUB : (i + 1) * SUB].astype(BF16)
                if send:
                    act(which, k, i).start()
        act_load(which, 0).wait()
        (xv, cotv)[which][zrows, :] = u_v[:block, :].astype(BF16)

    def act_arrive(which):
        for k in range(1, nz):
            loop(chunks, lambda i: act_in(which, k, i).wait_recv())

    for k in range(1, nz):
        act_load(0, k).start()
    for i in ins:
        i.start()
    act_load(0, 0).start()
    ins_t[0].start()
    ins_t[1].start()

    he = HD // n
    turned[:he, : eb_ref.shape[1]] = eb_ref[...].astype(F32)
    heads = [qb_ref[...].astype(F32), vb_ref[...].astype(F32), turned[...].T[: eb_ref.shape[1], :he]]
    head_rows = sum(r.shape[0] for r in heads)
    pk_wide[...] = jnp.zeros_like(pk_wide)
    at = 0
    for r in heads:
        pk_wide[at : at + r.shape[0], :he] = r
        at += r.shape[0]
    for i, r in enumerate((ob_ref, rb_ref, g1_ref, s1_ref, g2_ref, s2_ref)):
        pk_wide[at + 8 + i : at + 9 + i, :rows] = r[...].reshape(1, rows).astype(F32)
    pk_ref[...] = pk_wide[...].astype(BF16)
    greet(group + [(s, lax.rem(z + k, nz), c) for k in range(1, nz)])

    def pk_copy(k, j):
        return rcopy(
            pk_ref, pkall.at[s, c], pk_send.at[k, j], pk_recv.at[k, j], (s ^ k, z, c if j == 0 else 1 - c)
        )

    def pk_in(k, j):
        at = pkall.at[s ^ k, c if j == 0 else 1 - c]
        return rcopy(at, at, pk_send.at[k, j], pk_recv.at[k, j], (s ^ k, z, c if j == 0 else 1 - c))

    pk_pairs = [(k, j) for k in range(n) for j in range(2) if k + j > 0]
    for k, j in pk_pairs:
        pk_copy(k, j).start()
    pkall[s, c] = pk_ref[...]

    direct = [1, 2] if n == 4 else list(range(1, n))

    def own_copy(u, k):
        return rcopy(
            own.at[u], full_ref.at[c, u, mine, :], own_send.at[u, k], own_recv.at[u, k], (s ^ k, z, c)
        )

    def own_in(u, k):
        at = full_ref.at[c, u, rows_at(s ^ k, rows), :]
        return rcopy(at, at, own_send.at[u, k], own_recv.at[u, k], (s ^ k, z, c))

    def half_at(k, h):
        return pl.ds(pl.multiple_of((s ^ k) * rows + h * half, half), half)

    def fwd_copy(u, h):
        at = full_ref.at[c, u, half_at(2 - h, h), :]
        return rcopy(at, at, fwd_send.at[u, h], fwd_recv.at[u, h], (s ^ (1 + h), z, c))

    def fwd_in(u, h):
        at = full_ref.at[c, u, half_at(3, h), :]
        return rcopy(at, at, fwd_send.at[u, h], fwd_recv.at[u, h], (s ^ (1 + h), z, c))

    def core_copy(u, k):
        at = full_ref.at[c, u, rows_at(s ^ k, rows), :]
        return rcopy(at, at, core_send.at[u, k], core_recv.at[u, k], (s, z, 1 - c))

    def core_in(u, k):
        at = full_ref.at[1 - c, u, rows_at(s ^ k, rows), :]
        return rcopy(at, at, core_send.at[u, k], core_recv.at[u, k], (s, z, 1 - c))

    par = lax.rem(z, 2)
    slots_of_units = units - 2

    def unit_at(i):
        u = jnp.where(i < 3, i, jnp.where(i == 3, 4 + par, jnp.where(i == 4, 3, 8 + par)))
        return jnp.where(i > 5, jnp.where(i < 8, i, i + 2), u)

    def theirs_at(i):
        return jnp.where(i == 3, 5 - par, 9 - par)

    def z_copy(u, k):
        at = full_ref.at[c, u, rows_at(s ^ k, rows), :]
        i = lax.rem(u, 4) + jnp.where(u >= 4 + e_units, 2, 0)
        return rcopy(at, at, z_send.at[i, k], z_recv.at[i, k], (s, z + 1 - 2 * par, c))

    def is_paired(i):
        return jnp.logical_or(i == 3, i == 5)

    ahead = 1
    for i in ins[:ahead]:
        i.wait()
    for u in range(ahead):
        for k in direct:
            own_copy(u, k).start()
    act_share(0, True)
    for k in range(nz):
        act_load(1, k).start()
    for i in ins[ahead:]:
        i.wait()
    for i, (_, u) in enumerate(tall):
        ins_t[i].wait()
        own[u] = turn_in[i % 2].T
        if i + 2 < len(tall):
            ins_t[i + 2].start()
    keep = lcopy(own, full_ref.at[c, :, mine, :], in_sem.at[5 + e_units])
    keep.start()
    share = rcopy(
        own, full_ref.at[c, :, mine, :], core_send.at[units, 0], core_recv.at[units, 0], (s, z, 1 - c)
    )
    share.start()
    theirs = full_ref.at[1 - c, :, mine, :]
    share_in = rcopy(theirs, theirs, core_send.at[units, 0], core_recv.at[units, 0], (s, z, 1 - c))
    act_share(1, False)

    for k, j in pk_pairs:
        pk_in(k, j).wait_recv()
    wide = pk_ref.shape[1]
    head_bias[...] = jnp.zeros_like(head_bias)
    vec[...] = jnp.zeros_like(vec)

    def place_one(sh):
        r = lax.broadcasted_iota(jnp.int32, (wide, width), 0)
        col = lax.broadcasted_iota(jnp.int32, (wide, width), 1)
        pick = jnp.where(jnp.logical_and(r < he, col % HD == sh * he + r), 1.0, 0.0).astype(BF16)
        row = lax.broadcasted_iota(jnp.int32, (head_rows, width), 0)
        col = lax.broadcasted_iota(jnp.int32, (head_rows, width), 1)
        own_head = col // HD == row % 8
        for j in range(2):
            head_bias[j] += jnp.where(own_head, mm(pkall[sh, j, :head_rows, :], pick), 0.0)
        r = lax.broadcasted_iota(jnp.int32, (wide, model), 0)
        col = lax.broadcasted_iota(jnp.int32, (wide, model), 1)
        hit = jnp.logical_and(r < rows, col == sh * rows + r)
        vec[...] += mm(pkall[sh, 0, head_rows:, :], jnp.where(hit, 1.0, 0.0).astype(BF16))

    loop(n, place_one)
    for j in range(2):
        for i in range(head_rows // 8):
            bias[i : i + 1, j * width : (j + 1) * width] = jnp.sum(
                head_bias[j, 8 * i : 8 * i + 8, :], 0, keepdims=True
            )
    small[...] = jnp.zeros_like(small)
    length = len_ref[2 * z + c]
    live_keys = lax.broadcasted_iota(jnp.int32, (1, slots), 1) < length
    lane = lax.broadcasted_iota(jnp.int32, (slots, 128), 1)

    def fetch(u):
        slot = lax.rem(u, 2)
        return [
            lcopy(full_ref.at[hf, u], wbuf.at[slot, :, hf * width : (hf + 1) * width], fetch_sem.at[slot, hf])
            for hf in range(2)
        ]

    def ready(u):
        @pl.when(u == 0)
        def _():
            keep.wait()
            share_in.wait_recv()

        for k in range(1, n):
            core_in(u, k).wait_recv()

    def p_copy(p):
        return lcopy(p_v.at[lax.rem(p, 2)], p_ref.at[p], p_sem.at[lax.rem(p, 2)])

    class Weights:
        def __init__(self, buf, i):
            self.buf, self.i = buf, i

        def copies(self, u):
            return [
                lcopy(full_ref.at[hf, u], self.buf.at[:, hf * width : (hf + 1) * width], fetch_sem.at[self.i, hf])
                for hf in range(2)
            ]

        def start(self, u):
            for i in self.copies(u):
                i.start()

        def wait(self, u):
            for i in self.copies(u):
                i.wait()

    wr, we = Weights(wbuf.at[0], 0), Weights(wbuf.at[1], 1)

    def load_p(p):
        return lcopy(p_ref.at[p], p_v.at[lax.rem(p, 2)], p_sem.at[lax.rem(p, 2)])

    def started():
        wr.start(4 + e_units)
        we.start(4)
        for p in range(2):
            load_p(p).start()

    def attention(p):
        at = rows_at(p, 128)
        q, k, v = qkv[0, :, at], qkv[1, :, at], qkv[2, :, at]

        @pl.when(p >= 2)
        def _():
            p_copy(p - 2).wait()

        out = None
        for h in range(2):
            part = lane < HD if h == 0 else lane >= HD
            scores = mm_nt(jnp.where(part, q, 0), k) * HD ** (-0.5)
            scores = jnp.where(live_keys, scores, MASKED)
            e = jnp.exp(scores - jnp.max(scores, -1, keepdims=True))
            low = (e * (1.0 / jnp.sum(e, -1, keepdims=True))).astype(BF16)
            p_v[lax.rem(p, 2), h] = low
            term = mm(low, jnp.where(part, v, 0))
            out = term if out is None else out + term
        o_v[:, at] = out.astype(BF16)
        p_copy(p).start()

    pairs = model // 128
    rb = 128

    def compute(u):
        w = wbuf.at[lax.rem(u, 2)]

        @pl.when(u == 0)
        def _():
            act_arrive(0)

        @pl.when(u < 3)
        def _():
            add = jnp.where(u == 0, bias[0:1, :], jnp.where(u == 2, bias[1:2, :], 0.0))
            qkv[u] = (mm(xv[...], w[...]) + add).astype(BF16)

        @pl.when(u == 3)
        def _():
            u_v[...] = mm_nt(o_v[...], w[...]) + xv[...].astype(F32)

            def norm(i):
                at = rows_at(i, rb)
                first = u_v[at, :] + vec[8:9, :]
                centred = first - mean(first)
                inv = lax.rsqrt(mean(centred * centred) + EPSILON)
                n1 = centred * inv
                n1_v[at, :] = n1
                r1_v[at, :] = jnp.broadcast_to(inv, (rb, 128))
                up = n1 * vec[10:11, :] + vec[11:12, :]
                ulow_v[at, :] = up.astype(BF16)
                u_v[at, :] = up

            loop(slots // rb, norm)

        @pl.when(jnp.logical_and(u >= 4, u < 4 + e_units))
        def _():
            j = u - 4
            pre = mm(ulow_v[...], w[...]) + bias[pl.ds(2 + j, 1), :]
            phi = 0.5 * (1.0 + lax.erf(pre * 0.7071067811865476))
            h_v[j] = (pre * phi).astype(BF16)
            gp_v[j] = (phi + pre * jnp.exp(-0.5 * pre * pre) * 0.3989422804014327).astype(BF16)

        @pl.when(u >= 4 + e_units)
        def _():
            u_v[...] += mm_nt(h_v[u - 4 - e_units], w[...])

    def exchange(t):
        @pl.when(t < slots_of_units)
        def _():
            u = unit_at(t)

            @pl.when(t + ahead < slots_of_units)
            def _():
                for k in direct:
                    own_copy(unit_at(t + ahead), k).start()

            for k in direct:
                own_in(u, k).wait_recv()
                if n == 4:
                    fwd_copy(u, 2 - k).start()
                core_copy(u, k).start()

                @pl.when(is_paired(t))
                def _():
                    z_copy(u, k).start()

        if n == 4:
            @pl.when(jnp.logical_and(t > 0, t <= slots_of_units))
            def _():
                u = unit_at(t - 1)
                for h in range(2):
                    fwd_in(u, h).wait_recv()
                core_copy(u, 3).start()

                @pl.when(is_paired(t - 1))
                def _():
                    z_copy(u, 3).start()

        for late, ks in ((2, [k for k in range(1, n) if n != 4 or k < 3]), (3, [3] if n == 4 else [])):
            @pl.when(is_paired(t - late))
            def _(late=late, ks=ks):
                u = theirs_at(t - late)
                for k in ks:
                    z_copy(u, k).wait_recv()
                    core_copy(u, k).start()

        @pl.when(jnp.logical_and(lax.rem(t, 2) == 1, t < 2 * chunks))
        def _():
            act_some(1, t // 2)

    def first_at(t):
        u = jnp.clip(t - 2, 0, 3)
        for late in (6, 7, 7, 8, 8, 9, 9, 9, 10):
            u = u + jnp.where(t > late, 1, 0)
        return u

    def start_fetch(u):
        ready(u)
        for i in fetch(u):
            i.start()

    def step(t):
        exchange(t)
        first, after = first_at(t), first_at(t + 1)
        pl.when(t == slots_of_units)(lambda: start_fetch(units - 1))

        def one(u, carry):
            for i in fetch(u):
                i.wait()
            pl.when(u + 1 < after)(lambda: start_fetch(u + 1))
            compute(u)
            return carry

        lax.fori_loop(first, after, one, 0)
        pl.when(jnp.logical_or(t == 4, t == 5))(
            lambda: loop(pairs // 2, lambda p: attention(p + (t - 4) * (pairs // 2)))
        )
        pl.when(jnp.logical_and(first_at(t + 2) > after, t + 1 < slots_of_units))(lambda: start_fetch(after))

    loop(slots_of_units + 1, step)

    for p in (pairs - 2, pairs - 1):
        p_copy(p).wait()
    started()
    act_arrive(1)

    def norm2(i):
        at = rows_at(i, rb)
        second = u_v[at, :] + vec[9:10, :]
        centred = second - mean(second)
        inv = lax.rsqrt(mean(centred * centred) + EPSILON)
        n2 = centred * inv
        gain = vec[12:13, :]
        y = (n2 * gain + vec[13:14, :]).astype(BF16)
        row = lax.broadcasted_iota(jnp.int32, (rb, 1), 0) + i * rb
        grad = jnp.where(row < length, cotv[at, :].astype(F32), 0.0)
        scaled = grad * gain
        back = inv * (scaled - mean(scaled) - n2 * mean(scaled * n2))
        cotv[at, :] = y
        u_v[at, :] = back
        low = back.astype(BF16)
        dz_v[at, :] = low
        for r, v in ((14, low.astype(F32)), (20, grad * n2), (22, grad)):
            v = jnp.sum(v, 0, keepdims=True)
            small[r : r + 1, :] += v[:, :width]
            small[r + 1 : r + 2, :] += v[:, width:]

    loop(slots // rb, norm2)
    def sent(t):
        u = unit_at(t)
        for k in direct:
            own_copy(u, k).wait_send()
        if n == 4:
            for h in range(2):
                fwd_copy(u, h).wait_send()

        @pl.when(is_paired(t))
        def _():
            for k in range(1, n):
                z_copy(u, k).wait_send()

    loop(slots_of_units, sent)

    def passed(u):
        for k in range(1, n):
            core_copy(u, k).wait_send()

    loop(units, passed)
    share.wait_send()
    for k, j in pk_pairs:
        pk_copy(k, j).wait_send()
    for which in range(2):
        for k in range(1, nz):
            loop(chunks, lambda i: act(which, k, i).wait_send())

    (part_sem, give_send, give_recv, stage_sem, near_send, near_recv, far_send, far_recv, chain_send, chain_recv,
     store_sem, back_send, back_recv, pass_send, pass_recv, keep_sem, small_send, small_recv) = later_sems
    subs = 2 * units
    def back_act(which, k, i):
        src, dst = ((cotv, ys_ref), (dz_v, dx_ref))[which]
        to = lax.rem(z + k, nz)
        some = block // PIECES
        return rcopy(
            src.at[pl.ds(pl.multiple_of(to * block + i * some, some), some), :],
            dst.at[2 * z + c, rows_at(i, some), :],
            back_send.at[which, k, i], back_recv.at[which, k, i], (s, to, c),
        )

    def back_act_in(which, k, i):
        src = lax.rem(z + nz - k, nz)
        at = (ys_ref, dx_ref)[which].at[2 * src + c, rows_at(i, block // PIECES), :]
        return rcopy(at, at, back_send.at[which, k, i], back_recv.at[which, k, i], (s, src, c))

    def back_act_keep(which):
        src, dst = ((cotv, ys_ref), (dz_v, dx_ref))[which]
        return lcopy(src.at[zrows, :], dst.at[2 * z + c], keep_sem.at[which])

    def back_pass_copy(which, k):
        at = (ys_ref, dx_ref)[which].at[2 * lax.rem(z + nz - k, nz) + c]
        return rcopy(at, at, pass_send.at[which, k], pass_recv.at[which, k], (s, z, 1 - c))

    def back_pass_in(which, k):
        at = (ys_ref, dx_ref)[which].at[2 * lax.rem(z + nz - k, nz) + 1 - c]
        return rcopy(at, at, pass_send.at[which, k], pass_recv.at[which, k], (s, z, 1 - c))

    def back_act_some(which, i):
        for k in range(1, nz):
            back_act(which, k, i).start()

    def back_act_pass(which):
        for k in range(1, nz):
            loop(PIECES, lambda i: back_act_in(which, k, i).wait_recv())
            back_pass_copy(which, k).start()
        back_act_keep(which).wait()
        back_pass_copy(which, 0).start()

    back_act_keep(0).start()

    def back_core_copy(u):
        return rcopy(pbuf.at[0], got_ref.at[u], give_send.at[u], give_recv.at[u], (s, z, 1 - c))

    def back_core_in(u):
        return rcopy(got_ref.at[u], got_ref.at[u], give_send.at[u], give_recv.at[u], (s, z, 1 - c))

    def part_copy(u):
        return lcopy(pbuf.at[1 + lax.rem(u, 2)], part_ref.at[u], part_sem.at[lax.rem(u, 2)])

    def emit(u, i, value):
        low = value.astype(BF16)
        for b in range(2):
            pbuf[jnp.where(i == 0, 0, 1 + lax.rem(u, 2)), b] = low[:, b * SUB : (b + 1) * SUB]

    def produce(u, make):
        pl.when(u > 0)(lambda: back_core_copy(u - 1).wait_send())

        def one(i):
            emit(u, i, make(lax.rem(1 - c + i, 2)))

            @pl.when(i == 0)
            def _():
                back_core_copy(u).start()

        loop(2, one)
        part_copy(u).start()

    last_e = e_units - 1

    def cols(hf):
        return rows_at(hf, width)

    def add_small(r, v):
        v = jnp.sum(v, 0, keepdims=True)
        for hf in range(2):
            small[pl.ds(r[hf], 1), :] += v[:, hf * width : (hf + 1) * width]

    def make_r(j):
        produce(j, lambda hf: mm_tn(dz_v[...], h_v[j, :, cols(hf)]))

    def make_dpre(j):
        wr.wait(4 + e_units + j)
        low = (mm(dz_v[...], wr.buf[...]) * gp_v[j].astype(F32)).astype(BF16)
        gp_v[j] = low
        add_small((4 + j, 4 + e_units + j), low.astype(F32))

        @pl.when(j < last_e)
        def _():
            wr.start(5 + e_units + j)

        @pl.when(j == last_e)
        def _():
            wr.start(3)

    def make_du(j):
        we.wait(4 + j)
        u_v[...] += mm_nt(gp_v[j], we.buf[...])

        @pl.when(j < last_e)
        def _():
            we.start(5 + j)

        @pl.when(j == last_e)
        def _():
            we.start(1)

    def make_e(u, j):
        produce(u, lambda hf: mm_tn(ulow_v[...], gp_v[j, :, cols(hf)]))

    def norm_back(i):
        at = rows_at(i, rb)
        grad = u_v[at, :]
        n1 = n1_v[at, :]
        scaled = grad * vec[10:11, :]
        back = r1_v[at, 0:1] * (scaled - mean(scaled) - n1 * mean(scaled * n1))
        u_v[at, :] = back
        low = back.astype(BF16)
        dz_v[at, :] = low
        for r, v in ((12, low.astype(F32)), (16, grad * n1), (18, grad)):
            add_small((r, r + 1), v)

    def make_o():
        loop(slots // rb, norm_back)
        produce(e_units, lambda hf: mm_tn(dz_v[...], o_v[:, cols(hf)]))

    def make_do():
        wr.wait(3)
        o_v[...] = mm(dz_v[...], wr.buf[...]).astype(BF16)
        wr.start(0)

    def attention_back(p):
        at = rows_at(p, 128)
        q, k, v, do = qkv[0, :, at], qkv[1, :, at], qkv[2, :, at], o_v[:, at]
        load_p(p).wait()
        dq = dk = dv = None
        for h in range(2):
            part = lane < HD if h == 0 else lane >= HD
            qh, kh, doh = jnp.where(part, q, 0), jnp.where(part, k, 0), jnp.where(part, do, 0)
            low = p_v[lax.rem(p, 2), h]
            probs = low.astype(F32)
            dp = mm_nt(doh, v)
            ds = (probs * (dp - jnp.sum(dp * probs, -1, keepdims=True))).astype(BF16)
            tv, tk, tq = mm_tn(low, doh), mm_tn(ds, qh), mm(ds, kh)
            dv, dk, dq = (tv, tk, tq) if h == 0 else (dv + tv, dk + tk, dq + tq)
        qkv[0, :, at] = (dq * HD ** (-0.5)).astype(BF16)
        qkv[1, :, at] = (dk * HD ** (-0.5)).astype(BF16)
        qkv[2, :, at] = dv.astype(BF16)

        @pl.when(p + 2 < pairs)
        def _():
            load_p(p + 2).start()


    def make_w(u, i):
        produce(u, lambda hf: mm_tn(xv[...], qkv[i, :, cols(hf)]))

    def make_dx(i, weights):
        weights.wait(i)
        u_v[...] += mm_nt(qkv[i], weights.buf[...])
        if i != 1:
            add_small((i, i + 1), qkv[i].astype(F32))

    def one_of(t, ticks):
        hit = t == ticks[0]
        for i in ticks[1:]:
            hit = jnp.logical_or(hit, t == i)
        return hit

    makes = {0: 0, 1: 1, 2: 2, 3: 3, 4: 4, 6: 5, 7: 6, 8: 7, 10: 8, 11: 9, 12: 10, 13: 11}

    def unit_of(t):
        return t - jnp.where(t > 4, 1, 0) - jnp.where(t > 9, 1, 0)

    def work(t):
        pl.when(t < 4)(lambda: make_r(t))
        pl.when(jnp.logical_and(t > 0, t < 5))(lambda: make_du(t - 1))
        pl.when(t < 4)(lambda: make_dpre(t))
        pl.when(t == 4)(make_o)

        pl.when(t == 5)(make_do)

        pl.when(jnp.logical_and(t > 4, t < 9))(lambda: loop(2, lambda i: attention_back(2 * (t - 5) + i)))

        @pl.when(one_of(t, (6, 7, 12, 13)))
        def _():
            make_e(unit_of(t), t - jnp.where(t > 7, 10, 6))

        @pl.when(one_of(t, (8, 10, 11)))
        def _():
            make_w(unit_of(t), t - jnp.where(t > 8, 9, 8))

        @pl.when(t == 9)
        def _():
            make_dx(0, wr)
            wr.start(2)
            make_dx(1, we)
            make_dx(2, wr)
            dz_v[...] = u_v[...].astype(BF16)
            back_act_keep(1).start()

    def loads_of(w):
        slot = lax.rem(w, 2)
        u, b = w // 2, lax.rem(w, 2)
        return [
            lcopy(part_ref.at[u, b], stage.at[slot], stage_sem.at[slot, 0]),
            lcopy(got_ref.at[u, b], gstage.at[slot], stage_sem.at[slot, 1]),
        ]

    def blk(k):
        return rows_at(s ^ k, rows)

    def blk_half(k, h):
        return pl.ds(pl.multiple_of((s ^ k) * rows + h * half, half), half)

    def near_copy(w, h, i):
        k = (1 + h, 3)[i]
        return rcopy(
            total.at[lax.rem(w, SLOTS), blk_half(k, h), :], near.at[w, h, i],
            near_send.at[lax.rem(w, SLOTS), h, i], near_recv.at[w, h, i], (s ^ (1 + h), z, c),
        )

    def far_copy(w, h):
        return rcopy(
            pair_sum.at[w, h], far.at[w, h], far_send.at[w, h], far_recv.at[w, h], (s ^ (2 - h), z, c)
        )

    def straight(w, k):
        return rcopy(
            total.at[lax.rem(w, SLOTS), blk(k), :], near.at[w, k - 1],
            near_send.at[lax.rem(w, SLOTS), k - 1], near_recv.at[w, k - 1], (s ^ k, z, c),
        )

    def sends_of(w):
        if n == 4:
            return [near_copy(w, h, i) for h in range(2) for i in range(2)]
        return [straight(w, k) for k in range(1, n)]

    block_out = own

    def part_cols(w):
        return rows_at(lax.rem(w, 2), SUB)

    def z_to(w, h, src, dst, i, to):
        at = pl.ds(h * half, half)
        source = own.at[w // 2, at, part_cols(w)] if src is own else src.at[w, at]
        return rcopy(source, dst.at[w, at], chain_send.at[w, i, h], chain_recv.at[w, i, h], (s, to, c))

    last = nz - 1
    edge = jnp.logical_or(z == 0, z == last)
    inner = jnp.where(z == 0, 1, nz - 2)
    outer = jnp.where(z == 1, 0, last)
    other = jnp.where(z == 1, 2, 1)

    def s0(w):
        @pl.when(lax.rem(w, 2) == 0)
        def _():
            part_copy(w // 2).wait()
            back_core_in(w // 2).wait_recv()

        for i in loads_of(w):
            i.start()

    def s1(w):
        @pl.when(w >= SLOTS)
        def _():
            for i in sends_of(w - SLOTS):
                i.wait_send()

        for i in loads_of(w):
            i.wait()
        slot, to = lax.rem(w, 2), lax.rem(w, SLOTS)

        def add(i):
            at = rows_at(i, 256)
            total[to, at, :] = (stage[slot, at, :].astype(F32) + gstage[slot, at, :].astype(F32)).astype(BF16)

        loop(model // 256, add)
        for i in sends_of(w):
            i.start()

    def s2(w):
        slot = lax.rem(w, SLOTS)
        for i in sends_of(w):
            i.wait_recv()
        if n == 4:
            for h in range(2):
                pair_sum[w, h] = (
                    total[slot, blk_half(2 - h, h), :].astype(F32) + near[w, h, 1].astype(F32)
                ).astype(BF16)
                far_copy(w, h).start()

    def s3(w):
        slot = lax.rem(w, SLOTS)
        if n != 4:
            acc = total[slot, blk(0), :].astype(F32)
            for k in range(1, n):
                acc = acc + near[w, k - 1].astype(F32)
            block_out[w // 2, :, part_cols(w)] = acc.astype(BF16)
        for h in range(2):
            if n == 4:
                far_copy(w, h).wait_recv()
                block_out[w // 2, h * half : (h + 1) * half, part_cols(w)] = (
                    total[slot, blk_half(0, h), :].astype(F32) + near[w, h, 0].astype(F32) + far[w, h].astype(F32)
                ).astype(BF16)
            pl.when(edge)(lambda: z_to(w, h, block_out, up, 0, inner).start())

    def s4(w):
        @pl.when(jnp.logical_not(edge))
        def _():
            for h in range(2):
                at = pl.ds(h * half, half)
                z_to(w, h, block_out, up, 0, outer).wait_recv()
                block_out[w // 2, at, part_cols(w)] = (block_out[w // 2, at, part_cols(w)].astype(F32) + up[w, at].astype(F32)).astype(BF16)
                z_to(w, h, block_out, across, 1, other).start()

    def s5(w):
        @pl.when(jnp.logical_not(edge))
        def _():
            for h in range(2):
                at = pl.ds(h * half, half)
                z_to(w, h, block_out, across, 1, other).wait_recv()
                up[w, at] = (block_out[w // 2, at, part_cols(w)].astype(F32) + across[w, at].astype(F32)).astype(BF16)
                z_to(w, h, up, up, 2, outer).start()

    def s6(w):
        @pl.when(edge)
        def _():
            for h in range(2):
                z_to(w, h, up, up, 2, inner).wait_recv()

        lcopy(up.at[w], grad_ref.at[w], store_sem.at[w]).start()

    stages = list(zip(LAGS, (s0, s3, s2, s1, s6, s5, s4)))

    def serve(w):
        for lag, stage_of in stages:
            @pl.when(jnp.logical_and(w >= lag, w - lag < subs))
            def _(stage_of=stage_of, lag=lag):
                stage_of(w - lag)

    hops = [(s, z, 1 - c)]
    hops += [(s ^ (1 << b), z, c) for b in range(n.bit_length() - 1)]
    hops += [(s, z ^ (1 << b), c) for b in range(nz.bit_length() - 1)]

    def small_copy(i):
        return rcopy(small, round_in.at[i], small_send.at[i], small_recv.at[i], hops[i])

    done = max(makes) + 2

    def served(t):
        late = jnp.maximum((PACE * (t - 3) + 2) // 4, 0) + jnp.where(t > 13, 1, 0)
        return jnp.clip(2 * (t - 1), 0, 4) + late

    def tick(t):
        lax.fori_loop(served(t), served(t + 1), lambda w, carry: (serve(w), carry)[1], 0)
        pl.when(t <= max(makes))(lambda: work(t))

        for which, first in enumerate(ACTS):
            pl.when(jnp.logical_and(t >= first, t < first + PIECES))(lambda: back_act_some(which, t - first))

        @pl.when(t == PIECES)
        def _():
            back_act_pass(0)

        @pl.when(t == PASS)
        def _():
            back_act_pass(1)

        for i in range(len(hops) + 1):
            @pl.when(t == done + i)
            def _(i=i):
                if i > 0:
                    small_copy(i - 1).wait_send()
                    small_copy(i - 1).wait_recv()
                    small[...] += round_in[i - 1]
                if i < len(hops):
                    small_copy(i).start()
                else:
                    lcopy(small, small_out, keep_sem.at[2]).start()

    ticks = (4 * (subs + max(LAGS) - 4) + PACE - 1) // PACE + 3
    loop(ticks, tick)

    def finish(w):
        if n == 4:
            for h in range(2):
                far_copy(w, h).wait_send()

        for h in range(2):
            pl.when(edge)(lambda: z_to(w, h, block_out, up, 0, inner).wait_send())

            @pl.when(jnp.logical_not(edge))
            def _():
                z_to(w, h, block_out, across, 1, other).wait_send()
                z_to(w, h, up, up, 2, outer).wait_send()

        lcopy(up.at[w], grad_ref.at[w], store_sem.at[w]).wait()

    loop(subs, finish)
    back_core_copy(units - 1).wait_send()
    for w in range(subs - SLOTS, subs):
        for i in sends_of(w):
            i.wait_send()
    for which in range(2):
        for k in range(1, nz):
            loop(PIECES, lambda i: back_act(which, k, i).wait_send())
        for k in range(nz):
            back_pass_copy(which, k).wait_send()
            back_pass_in(which, k).wait_recv()
    lcopy(small, small_out, keep_sem.at[2]).wait()


def layer(n, nz, lengths, inputs, cotangent, wq, wk, wv, wo, we, wr, heads, vectors):
    seqs, block, model = inputs.shape
    rows = wq.shape[0]
    half = rows // 2
    e_units = we.shape[1] // UNIT
    units = 4 + 2 * e_units
    subs = 2 * units
    slots = nz * block
    head_rows = heads[0].shape[0] + heads[1].shape[0] + heads[2].shape[1]
    pk = (head_rows + 16, max(rows, 128))
    near = (subs, 2, 2, half, SUB) if n == 4 else (subs, n - 1, rows, SUB)
    near_sems = near[:3] if n == 4 else near[:2]
    far = (subs, 2, half, SUB) if n == 4 else (1, 2, 16, SUB)
    blocks = (subs, rows, SUB)
    hops = 1 + (n.bit_length() - 1) + (nz.bit_length() - 1)
    low, wide = ((slots, model), BF16), ((slots, model), F32)
    hidden = ((e_units, slots, model), BF16)
    outs = [
        (blocks, BF16), ((seqs, block, model), BF16), ((seqs, block, model), BF16), ((24, UNIT), F32),
        ((2, units, model, UNIT), BF16), ((model // 128, 2, slots, slots), BF16),
        ((units, 2, model, SUB), BF16), ((units, 2, model, SUB), BF16),
    ]
    scratch = [
        ((units, rows, UNIT), BF16), ((2, UNIT, rows), BF16),
        low, low, ((3, slots, model), BF16), low, ((2, 2, slots, slots), BF16), wide, ((slots, 128), F32), wide, low,
        hidden, hidden, low, ((2, model, 2 * UNIT), BF16),
        (pk, BF16), (pk, F32), ((128, 128), F32), ((n, 2, *pk), BF16), ((2, head_rows, UNIT), F32),
        ((16, 2 * UNIT), F32), ((16, model), F32), ((24, UNIT), F32),
        ((3, 2, model, SUB), BF16), ((hops, 24, UNIT), F32),
        ((2, model, SUB), BF16), ((2, model, SUB), BF16), ((SLOTS, model, SUB), BF16),
        (near, BF16), (far, BF16), (far, BF16), (blocks, BF16), (blocks, BF16),
    ]
    return pl.pallas_call(
        functools.partial(layer_kernel, n, nz),
        name="layer_forward_and_backward",
        out_shape=[jax.ShapeDtypeStruct(a, b) for a, b in outs],
        in_specs=[SMEM] + [ANY] * 8 + [VMEM] * 9,
        out_specs=[ANY] * len(outs),
        scratch_shapes=[pltpu.VMEM(a, b) for a, b in scratch]
        + [
            DMA((units, n)), DMA((units, n)), DMA((units, 2)), DMA((units, 2)),
            DMA((units + 1, n)), DMA((units + 1, n)), DMA((4, n)), DMA((4, n)),
            DMA((2, nz, model // SUB)), DMA((2, nz, model // SUB)),
            DMA((n, 2)), DMA((n, 2)), DMA((6 + e_units,)), DMA((2,)), DMA((nz,)), DMA((2, 2)), DMA((2,)),
            DMA((2,)), DMA((units,)), DMA((units,)), DMA((2, 2)),
            DMA((SLOTS, *near_sems[1:])), DMA(near_sems), DMA((subs, 2)), DMA((subs, 2)),
            DMA((subs, 3, 2)), DMA((subs, 3, 2)), DMA((subs,)),
            DMA((2, nz, PIECES)), DMA((2, nz, PIECES)), DMA((2, nz)), DMA((2, nz)), DMA((3,)),
            DMA((hops,)), DMA((hops,)),
        ],
        compiler_params=pltpu.CompilerParams(
            collective_id=0, has_side_effects=True, vmem_limit_bytes=63 * 2**20
        ),
    )(lengths, inputs, cotangent, wq, wk, wv, wo, we, wr, *heads, *vectors)


def finish_kernel(
    n, grad_ref, ys_ref, dx_ref, small_ref,
    y_out, dx_out, dq_out, dk_out, dv_out, do_out, de_out, dr_out,
    qb_out, vb_out, eb_out, ob_out, rb_out, g1_out, s1_out, g2_out, s2_out,
    grads, act, act_wide, dq, dk, dv, do, de, dr, eb_turned, in_sem, out_sem, act_in, act_out,
):
    s, _, c = place()
    rows = dq.shape[0]
    seqs = act.shape[1]
    e_units = de.shape[1] // UNIT
    he = HD // n
    load = lcopy(grad_ref, grads, in_sem)
    load.start()

    def act_load(i, which):
        return lcopy((ys_ref, dx_ref)[which].at[i], act.at[which, i], act_in.at[which, i])

    def act_store(i, which):
        return lcopy(act_wide.at[which, i], (y_out, dx_out)[which].at[i], act_out.at[which, i])

    for which in range(2):
        loop(seqs, lambda i: act_load(i, which).start())
    load.wait()
    stores = []

    def store(src, dst):
        stores.append(lcopy(src, dst, out_sem.at[len(stores)]))
        stores[-1].start()

    def part(u, b):
        return grads[2 * u + b].astype(F32)

    spots = [e_units + 1, e_units + 2, e_units + 6, e_units + 7]
    for j in range(e_units):
        for b in range(2):
            at = j * UNIT + b * SUB
            dr[at : at + SUB, :] = part(j, b).T
            de[:, at : at + SUB] = part(spots[j], b)
    store(dr, dr_out)
    store(de, de_out)
    for i, (v, out) in enumerate(((dq, dq_out), (dk, dk_out), (dv, dv_out))):
        for b in range(2):
            v[:, b * SUB : (b + 1) * SUB] = part(e_units + 3 + i, b)
        store(v, out)
    for b in range(2):
        do[b * SUB : (b + 1) * SUB, :] = part(e_units, b).T
    store(do, do_out)
    for which in range(2):
        def widen(i):
            act_load(i, which).wait()
            act_wide[which, i] = act[which, i].astype(F32)
            act_store(i, which).start()

        loop(seqs, widen)

    at = lax.rem(UNIT - s * he, UNIT)
    turned = pltpu.roll(small_ref[...], at, 1)
    for out, base, count in ((qb_out, 0, 1), (vb_out, 2, 1), (eb_turned, 4, e_units)):
        for i in range(count):
            line = jnp.where(c == 0, turned[base + i : base + i + 1, :], turned[base + count + i : base + count + i + 1, :])
            for h in range(8):
                out[8 * i + h : 8 * i + h + 1, :he] = line[:, h * HD : h * HD + he]
    eb_out[...] = eb_turned[...].T[:he, : 8 * e_units]
    at = lax.rem(UNIT - lax.rem(s * rows, UNIT), UNIT)
    turned = pltpu.roll(small_ref[...], at, 1)
    late = s * rows >= UNIT
    for i, out in enumerate((ob_out, rb_out, g1_out, s1_out, g2_out, s2_out)):
        r = 4 + 2 * e_units + 2 * i
        line = jnp.where(late, turned[r + 1 : r + 2, :], turned[r : r + 1, :])
        out[...] = line[:, :rows].reshape(rows)
    for i in stores:
        i.wait()
    for which in range(2):
        loop(seqs, lambda i: act_store(i, which).wait())


def finish(n, grads, ys, dx, small, heads):
    _, rows, _ = grads.shape
    seqs, block, model = ys.shape
    wide = heads[2].shape[1] // 8 * UNIT
    square, tall = (rows, UNIT), (UNIT, rows)
    outs = [ys.shape, ys.shape, square, square, square, tall, (rows, wide), (wide, rows)]
    small_outs = [v.shape for v in heads] + [(rows,)] * 6
    return pl.pallas_call(
        functools.partial(finish_kernel, n),
        name="widen_results",
        out_shape=[jax.ShapeDtypeStruct(a, F32) for a in outs + small_outs],
        in_specs=[ANY] * 3 + [VMEM],
        out_specs=[ANY] * len(outs) + [VMEM] * len(small_outs),
        scratch_shapes=[pltpu.VMEM(grads.shape, BF16), pltpu.VMEM((2, *ys.shape), BF16), pltpu.VMEM((2, *ys.shape), F32)]
        + [pltpu.VMEM(a, F32) for a in outs[2:]]
        + [pltpu.VMEM((128, 128), F32)]
        + [DMA, DMA((6,)), DMA((2, seqs)), DMA((2, seqs))],
        compiler_params=pltpu.CompilerParams(vmem_limit_bytes=61 * 2**20),
    )(grads, ys, dx, small)


def body(n, nz, inputs, lengths, wq, wk, wv, wo, we, wr, qb, vb, eb, ob, rb, g1, s1, g2, s2, cotangent):
    heads = (qb, vb, eb.T)
    grads, ys, dx, small, *_ = layer(
        n, nz, lengths, inputs, cotangent, wq, wk, wv, wo, we, wr, heads, (ob, rb, g1, s1, g2, s2)
    )
    results = list(finish(n, grads, ys, dx, small, heads))
    results[10] = results[10].T
    return tuple(results)


def solution(mesh):
    w, wt, v = P("shard", "tp"), P("tp", "shard"), P("shard")
    rows = P("shard", "ctx", None)
    return jax.shard_map(
        functools.partial(body, mesh.shape["shard"], mesh.shape["ctx"]),
        mesh=mesh,
        in_specs=(rows, v, w, w, w, wt, w, wt, wt, wt, wt, v, v, v, v, v, v, rows),
        out_specs=(rows, rows, w, w, w, wt, w, wt, wt, wt, wt, v, v, v, v, v, v),
        check_vma=False,
    )
```

```python
import functools

import jax
import jax.numpy as jnp
from jax import lax
from jax.experimental import pallas as pl
from jax.experimental.pallas import tpu as pltpu
from jax.sharding import PartitionSpec as P

HD = 64
UNIT = 512
SUB = 256
SLOTS = 4
LAGS = (0, 5, 3, 1, 11, 9, 7)
PACE = 5
PASS = 22
PIECES = 8
ACTS = (0, 9)
EPSILON = 1e-05
MASKED = -1e30
MESH = pl.DeviceIdType.MESH
F32 = jnp.float32
BF16 = jnp.bfloat16
DMA = pltpu.SemaphoreType.DMA
ANY = pl.BlockSpec(memory_space=pl.ANY)
VMEM = pl.BlockSpec(memory_space=pltpu.VMEM)
SMEM = pl.BlockSpec(memory_space=pltpu.SMEM)


def place():
    return lax.axis_index("shard"), lax.axis_index("ctx"), lax.axis_index("tp")


def rcopy(src, dst, send, recv, dev):
    return pltpu.make_async_remote_copy(
        src_ref=src, dst_ref=dst, send_sem=send, recv_sem=recv, device_id=dev, device_id_type=MESH
    )


def lcopy(src, dst, sem):
    return pltpu.make_async_copy(src, dst, sem)


def greet(devices):
    barrier = pltpu.get_barrier_semaphore()
    for dev in devices:
        pl.semaphore_signal(barrier, inc=1, device_id=dev, device_id_type=MESH)
    pl.semaphore_wait(barrier, len(devices))


def rows_at(i, size):
    return pl.ds(pl.multiple_of(i * size, size), size)


def mm(a, b):
    return jnp.dot(a, b, preferred_element_type=F32)


def mm_nt(a, b):
    return lax.dot_general(a, b, (((1,), (1,)), ((), ())), preferred_element_type=F32)


def mm_tn(a, b):
    return lax.dot_general(a, b, (((0,), (0,)), ((), ())), preferred_element_type=F32)


def loop(count, fn):
    def step(i, carry):
        fn(i)
        return carry

    lax.fori_loop(0, count, step, 0)


def mean(v):
    return jnp.mean(v, -1, keepdims=True)


def layer_kernel(
    n, nz,
    len_ref, x_ref, g_ref, wq_ref, wk_ref, wv_ref, wo_ref, we_ref, wr_ref,
    qb_ref, vb_ref, eb_ref, ob_ref, rb_ref, g1_ref, s1_ref, g2_ref, s2_ref,
    grad_ref, ys_ref, dx_ref, small_out, full_ref, p_ref, part_ref, got_ref,
    own, turn_in, xv, cotv, qkv, o_v, p_v, n1_v, r1_v, u_v, ulow_v, h_v, gp_v, dz_v, wbuf,
    pk_ref, pk_wide, turned, pkall, head_bias, bias, vec, small,
    pbuf, round_in, stage, gstage, total, near, pair_sum, far, up, across,
    own_send, own_recv, fwd_send, fwd_recv, core_send, core_recv, z_send, z_recv, act_send, act_recv,
    pk_send, pk_recv, in_sem, turn_sem, act_sem, fetch_sem, p_sem,
    *later_sems,
):
    s, z, c = place()
    units, rows, width = own.shape
    half = rows // 2
    model = rows * n
    slots = xv.shape[0]
    block = slots // nz
    e_units = we_ref.shape[1] // width
    group = [(s ^ k, z, c if j == 0 else 1 - c) for k in range(n) for j in range(2) if k + j > 0]
    mine = rows_at(s, rows)
    zrows = rows_at(z, block)

    ins = [lcopy(r, own.at[i], in_sem.at[i]) for i, r in enumerate((wq_ref, wk_ref, wv_ref))]
    ins += [
        lcopy(we_ref.at[:, pl.ds(j * width, width)], own.at[4 + j], in_sem.at[3 + j]) for j in range(e_units)
    ]
    tall = [(wo_ref, 3)] + [(wr_ref.at[rows_at(j, width), :], 4 + e_units + j) for j in range(e_units)]
    ins_t = [lcopy(r, turn_in.at[i % 2], turn_sem.at[i % 2]) for i, (r, _) in enumerate(tall)]

    def to(k):
        return lax.rem(z + k, nz)

    def act_load(which, k):
        src = (x_ref, g_ref)[which]
        return lcopy(src.at[2 * to(k) + c], u_v.at[rows_at(k, block), :], act_sem.at[k])

    chunks = model // SUB

    def held(which, k, i):
        q = (which * (nz - 1) + k - 1) * chunks
        return pbuf.at[q // 16, (q // 8) % 2, rows_at(q % 8 + i, block), :]

    def act(which, k, i):
        dst = (xv, cotv)[which]
        return rcopy(
            held(which, k, i), dst.at[zrows, rows_at(i, SUB)],
            act_send.at[which, k, i], act_recv.at[which, k, i], (s, to(k), c),
        )

    def act_in(which, k, i):
        at = (xv, cotv)[which].at[rows_at(lax.rem(z + nz - k, nz), block), rows_at(i, SUB)]
        return rcopy(at, at, act_send.at[which, k, i], act_recv.at[which, k, i], (s, lax.rem(z + nz - k, nz), c))

    def act_some(which, i):
        for k in range(1, nz):
            act(which, k, i).start()

    def act_share(which, send):
        for k in range(1, nz):
            act_load(which, k).wait()
            for i in range(chunks):
                held(which, k, i)[...] = u_v[rows_at(k, block), i * SUB : (i + 1) * SUB].astype(BF16)
                if send:
                    act(which, k, i).start()
        act_load(which, 0).wait()
        (xv, cotv)[which][zrows, :] = u_v[:block, :].astype(BF16)

    def act_arrive(which):
        for k in range(1, nz):
            loop(chunks, lambda i: act_in(which, k, i).wait_recv())

    for k in range(1, nz):
        act_load(0, k).start()
    for i in ins:
        i.start()
    act_load(0, 0).start()
    ins_t[0].start()
    ins_t[1].start()

    he = HD // n
    turned[:he, : eb_ref.shape[1]] = eb_ref[...].astype(F32)
    heads = [qb_ref[...].astype(F32), vb_ref[...].astype(F32), turned[...].T[: eb_ref.shape[1], :he]]
    head_rows = sum(r.shape[0] for r in heads)
    pk_wide[...] = jnp.zeros_like(pk_wide)
    at = 0
    for r in heads:
        pk_wide[at : at + r.shape[0], :he] = r
        at += r.shape[0]
    for i, r in enumerate((ob_ref, rb_ref, g1_ref, s1_ref, g2_ref, s2_ref)):
        pk_wide[at + 8 + i : at + 9 + i, :rows] = r[...].reshape(1, rows).astype(F32)
    pk_ref[...] = pk_wide[...].astype(BF16)
    greet(group + [(s, lax.rem(z + k, nz), c) for k in range(1, nz)])

    def pk_copy(k, j):
        return rcopy(
            pk_ref, pkall.at[s, c], pk_send.at[k, j], pk_recv.at[k, j], (s ^ k, z, c if j == 0 else 1 - c)
        )

    def pk_in(k, j):
        at = pkall.at[s ^ k, c if j == 0 else 1 - c]
        return rcopy(at, at, pk_send.at[k, j], pk_recv.at[k, j], (s ^ k, z, c if j == 0 else 1 - c))

    pk_pairs = [(k, j) for k in range(n) for j in range(2) if k + j > 0]
    for k, j in pk_pairs:
        pk_copy(k, j).start()
    pkall[s, c] = pk_ref[...]

    direct = [1, 2] if n == 4 else list(range(1, n))

    def own_copy(u, k):
        return rcopy(
            own.at[u], full_ref.at[c, u, mine, :], own_send.at[u, k], own_recv.at[u, k], (s ^ k, z, c)
        )

    def own_in(u, k):
        at = full_ref.at[c, u, rows_at(s ^ k, rows), :]
        return rcopy(at, at, own_send.at[u, k], own_recv.at[u, k], (s ^ k, z, c))

    def half_at(k, h):
        return pl.ds(pl.multiple_of((s ^ k) * rows + h * half, half), half)

    def fwd_copy(u, h):
        at = full_ref.at[c, u, half_at(2 - h, h), :]
        return rcopy(at, at, fwd_send.at[u, h], fwd_recv.at[u, h], (s ^ (1 + h), z, c))

    def fwd_in(u, h):
        at = full_ref.at[c, u, half_at(3, h), :]
        return rcopy(at, at, fwd_send.at[u, h], fwd_recv.at[u, h], (s ^ (1 + h), z, c))

    def core_copy(u, k):
        at = full_ref.at[c, u, rows_at(s ^ k, rows), :]
        return rcopy(at, at, core_send.at[u, k], core_recv.at[u, k], (s, z, 1 - c))

    def core_in(u, k):
        at = full_ref.at[1 - c, u, rows_at(s ^ k, rows), :]
        return rcopy(at, at, core_send.at[u, k], core_recv.at[u, k], (s, z, 1 - c))

    par = lax.rem(z, 2)
    slots_of_units = units - 2

    def unit_at(i):
        u = jnp.where(i < 3, i, jnp.where(i == 3, 4 + par, jnp.where(i == 4, 3, 8 + par)))
        return jnp.where(i > 5, jnp.where(i < 8, i, i + 2), u)

    def theirs_at(i):
        return jnp.where(i == 3, 5 - par, 9 - par)

    def z_copy(u, k):
        at = full_ref.at[c, u, rows_at(s ^ k, rows), :]
        i = lax.rem(u, 4) + jnp.where(u >= 4 + e_units, 2, 0)
        return rcopy(at, at, z_send.at[i, k], z_recv.at[i, k], (s, z + 1 - 2 * par, c))

    def is_paired(i):
        return jnp.logical_or(i == 3, i == 5)

    ahead = 2
    for i in ins[:ahead]:
        i.wait()
    for u in range(ahead):
        for k in direct:
            own_copy(u, k).start()
    act_share(0, True)
    for k in range(nz):
        act_load(1, k).start()
    for i in ins[ahead:]:
        i.wait()
    for i, (_, u) in enumerate(tall):
        ins_t[i].wait()
        own[u] = turn_in[i % 2].T
        if i + 2 < len(tall):
            ins_t[i + 2].start()
    keep = lcopy(own, full_ref.at[c, :, mine, :], in_sem.at[5 + e_units])
    keep.start()
    share = rcopy(
        own, full_ref.at[c, :, mine, :], core_send.at[units, 0], core_recv.at[units, 0], (s, z, 1 - c)
    )
    share.start()
    theirs = full_ref.at[1 - c, :, mine, :]
    share_in = rcopy(theirs, theirs, core_send.at[units, 0], core_recv.at[units, 0], (s, z, 1 - c))
    act_share(1, False)

    for k, j in pk_pairs:
        pk_in(k, j).wait_recv()
    wide = pk_ref.shape[1]
    head_bias[...] = jnp.zeros_like(head_bias)
    vec[...] = jnp.zeros_like(vec)

    def place_one(sh):
        r = lax.broadcasted_iota(jnp.int32, (wide, width), 0)
        col = lax.broadcasted_iota(jnp.int32, (wide, width), 1)
        pick = jnp.where(jnp.logical_and(r < he, col % HD == sh * he + r), 1.0, 0.0).astype(BF16)
        row = lax.broadcasted_iota(jnp.int32, (head_rows, width), 0)
        col = lax.broadcasted_iota(jnp.int32, (head_rows, width), 1)
        own_head = col // HD == row % 8
        for j in range(2):
            head_bias[j] += jnp.where(own_head, mm(pkall[sh, j, :head_rows, :], pick), 0.0)
        r = lax.broadcasted_iota(jnp.int32, (wide, model), 0)
        col = lax.broadcasted_iota(jnp.int32, (wide, model), 1)
        hit = jnp.logical_and(r < rows, col == sh * rows + r)
        vec[...] += mm(pkall[sh, 0, head_rows:, :], jnp.where(hit, 1.0, 0.0).astype(BF16))

    loop(n, place_one)
    for j in range(2):
        for i in range(head_rows // 8):
            bias[i : i + 1, j * width : (j + 1) * width] = jnp.sum(
                head_bias[j, 8 * i : 8 * i + 8, :], 0, keepdims=True
            )
    small[...] = jnp.zeros_like(small)
    length = len_ref[2 * z + c]
    live_keys = lax.broadcasted_iota(jnp.int32, (1, slots), 1) < length
    lane = lax.broadcasted_iota(jnp.int32, (slots, 128), 1)

    def fetch(u):
        slot = lax.rem(u, 2)
        return [
            lcopy(full_ref.at[hf, u], wbuf.at[slot, :, hf * width : (hf + 1) * width], fetch_sem.at[slot, hf])
            for hf in range(2)
        ]

    def ready(u):
        @pl.when(u == 0)
        def _():
            keep.wait()
            share_in.wait_recv()

        for k in range(1, n):
            core_in(u, k).wait_recv()

    def p_copy(p):
        return lcopy(p_v.at[lax.rem(p, 2)], p_ref.at[p], p_sem.at[lax.rem(p, 2)])

    class Weights:
        def __init__(self, buf, i):
            self.buf, self.i = buf, i

        def copies(self, u):
            return [
                lcopy(full_ref.at[hf, u], self.buf.at[:, hf * width : (hf + 1) * width], fetch_sem.at[self.i, hf])
                for hf in range(2)
            ]

        def start(self, u):
            for i in self.copies(u):
                i.start()

        def wait(self, u):
            for i in self.copies(u):
                i.wait()

    wr, we = Weights(wbuf.at[0], 0), Weights(wbuf.at[1], 1)

    def load_p(p):
        return lcopy(p_ref.at[p], p_v.at[lax.rem(p, 2)], p_sem.at[lax.rem(p, 2)])

    def started():
        wr.start(4 + e_units)
        we.start(4)
        for p in range(2):
            load_p(p).start()

    def attention(p):
        at = rows_at(p, 128)
        q, k, v = qkv[0, :, at], qkv[1, :, at], qkv[2, :, at]

        @pl.when(p >= 2)
        def _():
            p_copy(p - 2).wait()

        out = None
        for h in range(2):
            part = lane < HD if h == 0 else lane >= HD
            scores = mm_nt(jnp.where(part, q, 0), k) * HD ** (-0.5)
            scores = jnp.where(live_keys, scores, MASKED)
            e = jnp.exp(scores - jnp.max(scores, -1, keepdims=True))
            low = (e * (1.0 / jnp.sum(e, -1, keepdims=True))).astype(BF16)
            p_v[lax.rem(p, 2), h] = low
            term = mm(low, jnp.where(part, v, 0))
            out = term if out is None else out + term
        o_v[:, at] = out.astype(BF16)
        p_copy(p).start()

    pairs = model // 128
    rb = 128

    def compute(u):
        w = wbuf.at[lax.rem(u, 2)]

        @pl.when(u == 0)
        def _():
            act_arrive(0)

        @pl.when(u < 3)
        def _():
            add = jnp.where(u == 0, bias[0:1, :], jnp.where(u == 2, bias[1:2, :], 0.0))
            qkv[u] = (mm(xv[...], w[...]) + add).astype(BF16)

        @pl.when(u == 3)
        def _():
            u_v[...] = mm_nt(o_v[...], w[...]) + xv[...].astype(F32)

            def norm(i):
                at = rows_at(i, rb)
                first = u_v[at, :] + vec[8:9, :]
                centred = first - mean(first)
                inv = lax.rsqrt(mean(centred * centred) + EPSILON)
                n1 = centred * inv
                n1_v[at, :] = n1
                r1_v[at, :] = jnp.broadcast_to(inv, (rb, 128))
                up = n1 * vec[10:11, :] + vec[11:12, :]
                ulow_v[at, :] = up.astype(BF16)
                u_v[at, :] = up

            loop(slots // rb, norm)

        @pl.when(jnp.logical_and(u >= 4, u < 4 + e_units))
        def _():
            j = u - 4
            pre = mm(ulow_v[...], w[...]) + bias[pl.ds(2 + j, 1), :]
            phi = 0.5 * (1.0 + lax.erf(pre * 0.7071067811865476))
            h_v[j] = (pre * phi).astype(BF16)
            gp_v[j] = (phi + pre * jnp.exp(-0.5 * pre * pre) * 0.3989422804014327).astype(BF16)

        @pl.when(u >= 4 + e_units)
        def _():
            u_v[...] += mm_nt(h_v[u - 4 - e_units], w[...])

    def exchange(t):
        @pl.when(t < slots_of_units)
        def _():
            u = unit_at(t)

            @pl.when(jnp.logical_and(t > 0, t + 1 < slots_of_units))
            def _():
                for k in direct:
                    own_copy(unit_at(t + 1), k).start()

            for k in direct:
                own_in(u, k).wait_recv()
                if n == 4:
                    fwd_copy(u, 2 - k).start()
                core_copy(u, k).start()

                @pl.when(is_paired(t))
                def _():
                    z_copy(u, k).start()

        if n == 4:
            @pl.when(jnp.logical_and(t > 0, t <= slots_of_units))
            def _():
                u = unit_at(t - 1)
                for h in range(2):
                    fwd_in(u, h).wait_recv()
                core_copy(u, 3).start()

                @pl.when(is_paired(t - 1))
                def _():
                    z_copy(u, 3).start()

        for late, ks in ((2, [k for k in range(1, n) if n != 4 or k < 3]), (3, [3] if n == 4 else [])):
            @pl.when(is_paired(t - late))
            def _(late=late, ks=ks):
                u = theirs_at(t - late)
                for k in ks:
                    z_copy(u, k).wait_recv()
                    core_copy(u, k).start()

        @pl.when(jnp.logical_and(lax.rem(t, 2) == 1, t < 2 * chunks))
        def _():
            act_some(1, t // 2)

    def first_at(t):
        u = jnp.clip(t - 2, 0, 3)
        for late in (6, 7, 7, 8, 8, 9, 9, 9, 10):
            u = u + jnp.where(t > late, 1, 0)
        return u

    def start_fetch(u):
        ready(u)
        for i in fetch(u):
            i.start()

    def step(t):
        exchange(t)
        first, after = first_at(t), first_at(t + 1)
        pl.when(t == slots_of_units)(lambda: start_fetch(units - 1))

        def one(u, carry):
            for i in fetch(u):
                i.wait()
            pl.when(u + 1 < after)(lambda: start_fetch(u + 1))
            compute(u)
            return carry

        lax.fori_loop(first, after, one, 0)
        pl.when(jnp.logical_or(t == 4, t == 5))(
            lambda: loop(pairs // 2, lambda p: attention(p + (t - 4) * (pairs // 2)))
        )
        pl.when(jnp.logical_and(first_at(t + 2) > after, t + 1 < slots_of_units))(lambda: start_fetch(after))

    loop(slots_of_units + 1, step)

    for p in (pairs - 2, pairs - 1):
        p_copy(p).wait()
    started()
    act_arrive(1)

    def norm2(i):
        at = rows_at(i, rb)
        second = u_v[at, :] + vec[9:10, :]
        centred = second - mean(second)
        inv = lax.rsqrt(mean(centred * centred) + EPSILON)
        n2 = centred * inv
        gain = vec[12:13, :]
        y = (n2 * gain + vec[13:14, :]).astype(BF16)
        row = lax.broadcasted_iota(jnp.int32, (rb, 1), 0) + i * rb
        grad = jnp.where(row < length, cotv[at, :].astype(F32), 0.0)
        scaled = grad * gain
        back = inv * (scaled - mean(scaled) - n2 * mean(scaled * n2))
        cotv[at, :] = y
        u_v[at, :] = back
        low = back.astype(BF16)
        dz_v[at, :] = low
        for r, v in ((14, low.astype(F32)), (20, grad * n2), (22, grad)):
            v = jnp.sum(v, 0, keepdims=True)
            small[r : r + 1, :] += v[:, :width]
            small[r + 1 : r + 2, :] += v[:, width:]

    loop(slots // rb, norm2)
    def sent(t):
        u = unit_at(t)
        for k in direct:
            own_copy(u, k).wait_send()
        if n == 4:
            for h in range(2):
                fwd_copy(u, h).wait_send()

        @pl.when(is_paired(t))
        def _():
            for k in range(1, n):
                z_copy(u, k).wait_send()

    loop(slots_of_units, sent)

    def passed(u):
        for k in range(1, n):
            core_copy(u, k).wait_send()

    loop(units, passed)
    share.wait_send()
    for k, j in pk_pairs:
        pk_copy(k, j).wait_send()
    for which in range(2):
        for k in range(1, nz):
            loop(chunks, lambda i: act(which, k, i).wait_send())

    (part_sem, give_send, give_recv, stage_sem, near_send, near_recv, far_send, far_recv, chain_send, chain_recv,
     store_sem, back_send, back_recv, pass_send, pass_recv, keep_sem, small_send, small_recv) = later_sems
    subs = 2 * units
    def back_act(which, k, i):
        src, dst = ((cotv, ys_ref), (dz_v, dx_ref))[which]
        to = lax.rem(z + k, nz)
        some = block // PIECES
        return rcopy(
            src.at[pl.ds(pl.multiple_of(to * block + i * some, some), some), :],
            dst.at[2 * z + c, rows_at(i, some), :],
            back_send.at[which, k, i], back_recv.at[which, k, i], (s, to, c),
        )

    def back_act_in(which, k, i):
        src = lax.rem(z + nz - k, nz)
        at = (ys_ref, dx_ref)[which].at[2 * src + c, rows_at(i, block // PIECES), :]
        return rcopy(at, at, back_send.at[which, k, i], back_recv.at[which, k, i], (s, src, c))

    def back_act_keep(which):
        src, dst = ((cotv, ys_ref), (dz_v, dx_ref))[which]
        return lcopy(src.at[zrows, :], dst.at[2 * z + c], keep_sem.at[which])

    def back_pass_copy(which, k):
        at = (ys_ref, dx_ref)[which].at[2 * lax.rem(z + nz - k, nz) + c]
        return rcopy(at, at, pass_send.at[which, k], pass_recv.at[which, k], (s, z, 1 - c))

    def back_pass_in(which, k):
        at = (ys_ref, dx_ref)[which].at[2 * lax.rem(z + nz - k, nz) + 1 - c]
        return rcopy(at, at, pass_send.at[which, k], pass_recv.at[which, k], (s, z, 1 - c))

    def back_act_some(which, i):
        for k in range(1, nz):
            back_act(which, k, i).start()

    def back_act_pass(which):
        for k in range(1, nz):
            loop(PIECES, lambda i: back_act_in(which, k, i).wait_recv())
            back_pass_copy(which, k).start()
        back_act_keep(which).wait()
        back_pass_copy(which, 0).start()

    back_act_keep(0).start()

    def back_core_copy(u):
        return rcopy(pbuf.at[0], got_ref.at[u], give_send.at[u], give_recv.at[u], (s, z, 1 - c))

    def back_core_in(u):
        return rcopy(got_ref.at[u], got_ref.at[u], give_send.at[u], give_recv.at[u], (s, z, 1 - c))

    def part_copy(u):
        return lcopy(pbuf.at[1 + lax.rem(u, 2)], part_ref.at[u], part_sem.at[lax.rem(u, 2)])

    def emit(u, i, value):
        low = value.astype(BF16)
        for b in range(2):
            pbuf[jnp.where(i == 0, 0, 1 + lax.rem(u, 2)), b] = low[:, b * SUB : (b + 1) * SUB]

    def produce(u, make):
        pl.when(u > 0)(lambda: back_core_copy(u - 1).wait_send())

        def one(i):
            emit(u, i, make(lax.rem(1 - c + i, 2)))

            @pl.when(i == 0)
            def _():
                back_core_copy(u).start()

        loop(2, one)
        part_copy(u).start()

    last_e = e_units - 1

    def cols(hf):
        return rows_at(hf, width)

    def add_small(r, v):
        v = jnp.sum(v, 0, keepdims=True)
        for hf in range(2):
            small[pl.ds(r[hf], 1), :] += v[:, hf * width : (hf + 1) * width]

    def make_r(j):
        produce(j, lambda hf: mm_tn(dz_v[...], h_v[j, :, cols(hf)]))

    def make_dpre(j):
        wr.wait(4 + e_units + j)
        low = (mm(dz_v[...], wr.buf[...]) * gp_v[j].astype(F32)).astype(BF16)
        gp_v[j] = low
        add_small((4 + j, 4 + e_units + j), low.astype(F32))

        @pl.when(j < last_e)
        def _():
            wr.start(5 + e_units + j)

        @pl.when(j == last_e)
        def _():
            wr.start(3)

    def make_du(j):
        we.wait(4 + j)
        u_v[...] += mm_nt(gp_v[j], we.buf[...])

        @pl.when(j < last_e)
        def _():
            we.start(5 + j)

        @pl.when(j == last_e)
        def _():
            we.start(1)

    def make_e(u, j):
        produce(u, lambda hf: mm_tn(ulow_v[...], gp_v[j, :, cols(hf)]))

    def norm_back(i):
        at = rows_at(i, rb)
        grad = u_v[at, :]
        n1 = n1_v[at, :]
        scaled = grad * vec[10:11, :]
        back = r1_v[at, 0:1] * (scaled - mean(scaled) - n1 * mean(scaled * n1))
        u_v[at, :] = back
        low = back.astype(BF16)
        dz_v[at, :] = low
        for r, v in ((12, low.astype(F32)), (16, grad * n1), (18, grad)):
            add_small((r, r + 1), v)

    def make_o():
        loop(slots // rb, norm_back)
        produce(e_units, lambda hf: mm_tn(dz_v[...], o_v[:, cols(hf)]))

    def make_do():
        wr.wait(3)
        o_v[...] = mm(dz_v[...], wr.buf[...]).astype(BF16)
        wr.start(0)

    def attention_back(p):
        at = rows_at(p, 128)
        q, k, v, do = qkv[0, :, at], qkv[1, :, at], qkv[2, :, at], o_v[:, at]
        load_p(p).wait()
        dq = dk = dv = None
        for h in range(2):
            part = lane < HD if h == 0 else lane >= HD
            qh, kh, doh = jnp.where(part, q, 0), jnp.where(part, k, 0), jnp.where(part, do, 0)
            low = p_v[lax.rem(p, 2), h]
            probs = low.astype(F32)
            dp = mm_nt(doh, v)
            ds = (probs * (dp - jnp.sum(dp * probs, -1, keepdims=True))).astype(BF16)
            tv, tk, tq = mm_tn(low, doh), mm_tn(ds, qh), mm(ds, kh)
            dv, dk, dq = (tv, tk, tq) if h == 0 else (dv + tv, dk + tk, dq + tq)
        qkv[0, :, at] = (dq * HD ** (-0.5)).astype(BF16)
        qkv[1, :, at] = (dk * HD ** (-0.5)).astype(BF16)
        qkv[2, :, at] = dv.astype(BF16)

        @pl.when(p + 2 < pairs)
        def _():
            load_p(p + 2).start()


    def make_w(u, i):
        produce(u, lambda hf: mm_tn(xv[...], qkv[i, :, cols(hf)]))

    def make_dx(i, weights):
        weights.wait(i)
        u_v[...] += mm_nt(qkv[i], weights.buf[...])
        if i != 1:
            add_small((i, i + 1), qkv[i].astype(F32))

    def one_of(t, ticks):
        hit = t == ticks[0]
        for i in ticks[1:]:
            hit = jnp.logical_or(hit, t == i)
        return hit

    makes = {0: 0, 1: 1, 2: 2, 3: 3, 4: 4, 6: 5, 7: 6, 8: 7, 10: 8, 11: 9, 12: 10, 13: 11}

    def unit_of(t):
        return t - jnp.where(t > 4, 1, 0) - jnp.where(t > 9, 1, 0)

    def work(t):
        pl.when(t < 4)(lambda: make_r(t))
        pl.when(jnp.logical_and(t > 0, t < 5))(lambda: make_du(t - 1))
        pl.when(t < 4)(lambda: make_dpre(t))
        pl.when(t == 4)(make_o)

        pl.when(t == 5)(make_do)

        pl.when(jnp.logical_and(t > 4, t < 9))(lambda: loop(2, lambda i: attention_back(2 * (t - 5) + i)))

        @pl.when(one_of(t, (6, 7, 12, 13)))
        def _():
            make_e(unit_of(t), t - jnp.where(t > 7, 10, 6))

        @pl.when(one_of(t, (8, 10, 11)))
        def _():
            make_w(unit_of(t), t - jnp.where(t > 8, 9, 8))

        @pl.when(t == 9)
        def _():
            make_dx(0, wr)
            wr.start(2)
            make_dx(1, we)
            make_dx(2, wr)
            dz_v[...] = u_v[...].astype(BF16)
            back_act_keep(1).start()

    def loads_of(w):
        slot = lax.rem(w, 2)
        u, b = w // 2, lax.rem(w, 2)
        return [
            lcopy(part_ref.at[u, b], stage.at[slot], stage_sem.at[slot, 0]),
            lcopy(got_ref.at[u, b], gstage.at[slot], stage_sem.at[slot, 1]),
        ]

    def blk(k):
        return rows_at(s ^ k, rows)

    def blk_half(k, h):
        return pl.ds(pl.multiple_of((s ^ k) * rows + h * half, half), half)

    def near_copy(w, h, i):
        k = (1 + h, 3)[i]
        return rcopy(
            total.at[lax.rem(w, SLOTS), blk_half(k, h), :], near.at[w, h, i],
            near_send.at[lax.rem(w, SLOTS), h, i], near_recv.at[w, h, i], (s ^ (1 + h), z, c),
        )

    def far_copy(w, h):
        return rcopy(
            pair_sum.at[w, h], far.at[w, h], far_send.at[w, h], far_recv.at[w, h], (s ^ (2 - h), z, c)
        )

    def straight(w, k):
        return rcopy(
            total.at[lax.rem(w, SLOTS), blk(k), :], near.at[w, k - 1],
            near_send.at[lax.rem(w, SLOTS), k - 1], near_recv.at[w, k - 1], (s ^ k, z, c),
        )

    def sends_of(w):
        if n == 4:
            return [near_copy(w, h, i) for h in range(2) for i in range(2)]
        return [straight(w, k) for k in range(1, n)]

    block_out = own

    def part_cols(w):
        return rows_at(lax.rem(w, 2), SUB)

    def z_to(w, h, src, dst, i, to):
        at = pl.ds(h * half, half)
        source = own.at[w // 2, at, part_cols(w)] if src is own else src.at[w, at]
        return rcopy(source, dst.at[w, at], chain_send.at[w, i, h], chain_recv.at[w, i, h], (s, to, c))

    last = nz - 1
    edge = jnp.logical_or(z == 0, z == last)
    inner = jnp.where(z == 0, 1, nz - 2)
    outer = jnp.where(z == 1, 0, last)
    other = jnp.where(z == 1, 2, 1)

    def s0(w):
        @pl.when(lax.rem(w, 2) == 0)
        def _():
            part_copy(w // 2).wait()
            back_core_in(w // 2).wait_recv()

        for i in loads_of(w):
            i.start()

    def s1(w):
        @pl.when(w >= SLOTS)
        def _():
            for i in sends_of(w - SLOTS):
                i.wait_send()

        for i in loads_of(w):
            i.wait()
        slot, to = lax.rem(w, 2), lax.rem(w, SLOTS)

        def add(i):
            at = rows_at(i, 256)
            total[to, at, :] = (stage[slot, at, :].astype(F32) + gstage[slot, at, :].astype(F32)).astype(BF16)

        loop(model // 256, add)
        for i in sends_of(w):
            i.start()

    def s2(w):
        slot = lax.rem(w, SLOTS)
        for i in sends_of(w):
            i.wait_recv()
        if n == 4:
            for h in range(2):
                pair_sum[w, h] = (
                    total[slot, blk_half(2 - h, h), :].astype(F32) + near[w, h, 1].astype(F32)
                ).astype(BF16)
                far_copy(w, h).start()

    def s3(w):
        slot = lax.rem(w, SLOTS)
        if n != 4:
            acc = total[slot, blk(0), :].astype(F32)
            for k in range(1, n):
                acc = acc + near[w, k - 1].astype(F32)
            block_out[w // 2, :, part_cols(w)] = acc.astype(BF16)
        for h in range(2):
            if n == 4:
                far_copy(w, h).wait_recv()
                block_out[w // 2, h * half : (h + 1) * half, part_cols(w)] = (
                    total[slot, blk_half(0, h), :].astype(F32) + near[w, h, 0].astype(F32) + far[w, h].astype(F32)
                ).astype(BF16)
            pl.when(edge)(lambda: z_to(w, h, block_out, up, 0, inner).start())

    def s4(w):
        @pl.when(jnp.logical_not(edge))
        def _():
            for h in range(2):
                at = pl.ds(h * half, half)
                z_to(w, h, block_out, up, 0, outer).wait_recv()
                block_out[w // 2, at, part_cols(w)] = (block_out[w // 2, at, part_cols(w)].astype(F32) + up[w, at].astype(F32)).astype(BF16)
                z_to(w, h, block_out, across, 1, other).start()

    def s5(w):
        @pl.when(jnp.logical_not(edge))
        def _():
            for h in range(2):
                at = pl.ds(h * half, half)
                z_to(w, h, block_out, across, 1, other).wait_recv()
                up[w, at] = (block_out[w // 2, at, part_cols(w)].astype(F32) + across[w, at].astype(F32)).astype(BF16)
                z_to(w, h, up, up, 2, outer).start()

    def s6(w):
        @pl.when(edge)
        def _():
            for h in range(2):
                z_to(w, h, up, up, 2, inner).wait_recv()

        lcopy(up.at[w], grad_ref.at[w], store_sem.at[w]).start()

    stages = list(zip(LAGS, (s0, s3, s2, s1, s6, s5, s4)))

    def serve(w):
        for lag, stage_of in stages:
            @pl.when(jnp.logical_and(w >= lag, w - lag < subs))
            def _(stage_of=stage_of, lag=lag):
                stage_of(w - lag)

    hops = [(s, z, 1 - c)]
    hops += [(s ^ (1 << b), z, c) for b in range(n.bit_length() - 1)]
    hops += [(s, z ^ (1 << b), c) for b in range(nz.bit_length() - 1)]

    def small_copy(i):
        return rcopy(small, round_in.at[i], small_send.at[i], small_recv.at[i], hops[i])

    done = max(makes) + 2

    def served(t):
        late = jnp.maximum((PACE * (t - 3) + 2) // 4, 0) + jnp.where(t > 13, 1, 0)
        return jnp.clip(2 * (t - 1), 0, 4) + late

    def tick(t):
        lax.fori_loop(served(t), served(t + 1), lambda w, carry: (serve(w), carry)[1], 0)
        pl.when(t <= max(makes))(lambda: work(t))

        for which, first in enumerate(ACTS):
            pl.when(jnp.logical_and(t >= first, t < first + PIECES))(lambda: back_act_some(which, t - first))

        @pl.when(t == PIECES)
        def _():
            back_act_pass(0)

        @pl.when(t == PASS)
        def _():
            back_act_pass(1)

        for i in range(len(hops) + 1):
            @pl.when(t == done + 2 * i)
            def _(i=i):
                if i > 0:
                    small_copy(i - 1).wait_send()
                    small_copy(i - 1).wait_recv()
                    small[...] += round_in[i - 1]
                if i < len(hops):
                    small_copy(i).start()
                else:
                    lcopy(small, small_out, keep_sem.at[2]).start()

    ticks = (4 * (subs + max(LAGS) - 4) + PACE - 1) // PACE + 3
    loop(ticks, tick)

    def finish(w):
        if n == 4:
            for h in range(2):
                far_copy(w, h).wait_send()

        for h in range(2):
            pl.when(edge)(lambda: z_to(w, h, block_out, up, 0, inner).wait_send())

            @pl.when(jnp.logical_not(edge))
            def _():
                z_to(w, h, block_out, across, 1, other).wait_send()
                z_to(w, h, up, up, 2, outer).wait_send()

        lcopy(up.at[w], grad_ref.at[w], store_sem.at[w]).wait()

    loop(subs, finish)
    back_core_copy(units - 1).wait_send()
    for w in range(subs - SLOTS, subs):
        for i in sends_of(w):
            i.wait_send()
    for which in range(2):
        for k in range(1, nz):
            loop(PIECES, lambda i: back_act(which, k, i).wait_send())
        for k in range(nz):
            back_pass_copy(which, k).wait_send()
            back_pass_in(which, k).wait_recv()
    lcopy(small, small_out, keep_sem.at[2]).wait()


def layer(n, nz, lengths, inputs, cotangent, wq, wk, wv, wo, we, wr, heads, vectors):
    seqs, block, model = inputs.shape
    rows = wq.shape[0]
    half = rows // 2
    e_units = we.shape[1] // UNIT
    units = 4 + 2 * e_units
    subs = 2 * units
    slots = nz * block
    head_rows = heads[0].shape[0] + heads[1].shape[0] + heads[2].shape[1]
    pk = (head_rows + 16, max(rows, 128))
    near = (subs, 2, 2, half, SUB) if n == 4 else (subs, n - 1, rows, SUB)
    near_sems = near[:3] if n == 4 else near[:2]
    far = (subs, 2, half, SUB) if n == 4 else (1, 2, 16, SUB)
    blocks = (subs, rows, SUB)
    hops = 1 + (n.bit_length() - 1) + (nz.bit_length() - 1)
    low, wide = ((slots, model), BF16), ((slots, model), F32)
    hidden = ((e_units, slots, model), BF16)
    outs = [
        (blocks, BF16), ((seqs, block, model), BF16), ((seqs, block, model), BF16), ((24, UNIT), F32),
        ((2, units, model, UNIT), BF16), ((model // 128, 2, slots, slots), BF16),
        ((units, 2, model, SUB), BF16), ((units, 2, model, SUB), BF16),
    ]
    scratch = [
        ((units, rows, UNIT), BF16), ((2, UNIT, rows), BF16),
        low, low, ((3, slots, model), BF16), low, ((2, 2, slots, slots), BF16), wide, ((slots, 128), F32), wide, low,
        hidden, hidden, low, ((2, model, 2 * UNIT), BF16),
        (pk, BF16), (pk, F32), ((128, 128), F32), ((n, 2, *pk), BF16), ((2, head_rows, UNIT), F32),
        ((16, 2 * UNIT), F32), ((16, model), F32), ((24, UNIT), F32),
        ((3, 2, model, SUB), BF16), ((hops, 24, UNIT), F32),
        ((2, model, SUB), BF16), ((2, model, SUB), BF16), ((SLOTS, model, SUB), BF16),
        (near, BF16), (far, BF16), (far, BF16), (blocks, BF16), (blocks, BF16),
    ]
    return pl.pallas_call(
        functools.partial(layer_kernel, n, nz),
        name="layer_forward_and_backward",
        out_shape=[jax.ShapeDtypeStruct(a, b) for a, b in outs],
        in_specs=[SMEM] + [ANY] * 8 + [VMEM] * 9,
        out_specs=[ANY] * len(outs),
        scratch_shapes=[pltpu.VMEM(a, b) for a, b in scratch]
        + [
            DMA((units, n)), DMA((units, n)), DMA((units, 2)), DMA((units, 2)),
            DMA((units + 1, n)), DMA((units + 1, n)), DMA((4, n)), DMA((4, n)),
            DMA((2, nz, model // SUB)), DMA((2, nz, model // SUB)),
            DMA((n, 2)), DMA((n, 2)), DMA((6 + e_units,)), DMA((2,)), DMA((nz,)), DMA((2, 2)), DMA((2,)),
            DMA((2,)), DMA((units,)), DMA((units,)), DMA((2, 2)),
            DMA((SLOTS, *near_sems[1:])), DMA(near_sems), DMA((subs, 2)), DMA((subs, 2)),
            DMA((subs, 3, 2)), DMA((subs, 3, 2)), DMA((subs,)),
            DMA((2, nz, PIECES)), DMA((2, nz, PIECES)), DMA((2, nz)), DMA((2, nz)), DMA((3,)),
            DMA((hops,)), DMA((hops,)),
        ],
        compiler_params=pltpu.CompilerParams(
            collective_id=0, has_side_effects=True, vmem_limit_bytes=63 * 2**20
        ),
    )(lengths, inputs, cotangent, wq, wk, wv, wo, we, wr, *heads, *vectors)


def finish_kernel(
    n, grad_ref, ys_ref, dx_ref, small_ref,
    y_out, dx_out, dq_out, dk_out, dv_out, do_out, de_out, dr_out,
    qb_out, vb_out, eb_out, ob_out, rb_out, g1_out, s1_out, g2_out, s2_out,
    grads, act, act_wide, dq, dk, dv, do, de, dr, eb_turned, in_sem, out_sem, act_in, act_out,
):
    s, _, c = place()
    rows = dq.shape[0]
    seqs = act.shape[1]
    e_units = de.shape[1] // UNIT
    he = HD // n
    units = grads.shape[0] // 2

    def load(u):
        at = pl.ds(2 * u, 2)
        return lcopy(grad_ref.at[at], grads.at[at], in_sem.at[u])

    loop(units, lambda u: load(u).start())

    def act_load(i, which):
        return lcopy((ys_ref, dx_ref)[which].at[i], act.at[which, i], act_in.at[which, i])

    def act_store(i, which):
        return lcopy(act_wide.at[which, i], (y_out, dx_out)[which].at[i], act_out.at[which, i])

    for which in range(2):
        loop(seqs, lambda i: act_load(i, which).start())
    stores = []

    def store(src, dst):
        stores.append(lcopy(src, dst, out_sem.at[len(stores)]))
        stores[-1].start()

    def part(u, b):
        return grads[2 * u + b].astype(F32)

    spots = [e_units + 1, e_units + 2, e_units + 6, e_units + 7]
    for j in range(e_units):
        load(j).wait()
        load(spots[j]).wait()
        for b in range(2):
            at = j * UNIT + b * SUB
            dr[at : at + SUB, :] = grads[2 * j + b].T.astype(F32)
            de[:, at : at + SUB] = part(spots[j], b)
    store(dr, dr_out)
    store(de, de_out)
    for i, (v, out) in enumerate(((dq, dq_out), (dk, dk_out), (dv, dv_out))):
        load(e_units + 3 + i).wait()
        for b in range(2):
            v[:, b * SUB : (b + 1) * SUB] = part(e_units + 3 + i, b)
        store(v, out)
    load(e_units).wait()
    for b in range(2):
        do[b * SUB : (b + 1) * SUB, :] = grads[2 * e_units + b].T.astype(F32)
    store(do, do_out)
    for which in range(2):
        def widen(i):
            act_load(i, which).wait()
            act_wide[which, i] = act[which, i].astype(F32)
            act_store(i, which).start()

        loop(seqs, widen)

    at = lax.rem(UNIT - s * he, UNIT)
    turned = pltpu.roll(small_ref[...], at, 1)
    for out, base, count in ((qb_out, 0, 1), (vb_out, 2, 1), (eb_turned, 4, e_units)):
        for i in range(count):
            line = jnp.where(c == 0, turned[base + i : base + i + 1, :], turned[base + count + i : base + count + i + 1, :])
            for h in range(8):
                out[8 * i + h : 8 * i + h + 1, :he] = line[:, h * HD : h * HD + he]
    eb_out[...] = eb_turned[...].T[:he, : 8 * e_units]
    at = lax.rem(UNIT - lax.rem(s * rows, UNIT), UNIT)
    turned = pltpu.roll(small_ref[...], at, 1)
    late = s * rows >= UNIT
    for i, out in enumerate((ob_out, rb_out, g1_out, s1_out, g2_out, s2_out)):
        r = 4 + 2 * e_units + 2 * i
        line = jnp.where(late, turned[r + 1 : r + 2, :], turned[r : r + 1, :])
        out[...] = line[:, :rows].reshape(rows)
    for i in stores:
        i.wait()
    for which in range(2):
        loop(seqs, lambda i: act_store(i, which).wait())


def finish(n, grads, ys, dx, small, heads):
    _, rows, _ = grads.shape
    seqs, block, model = ys.shape
    wide = heads[2].shape[1] // 8 * UNIT
    square, tall = (rows, UNIT), (UNIT, rows)
    outs = [ys.shape, ys.shape, square, square, square, tall, (rows, wide), (wide, rows)]
    small_outs = [v.shape for v in heads] + [(rows,)] * 6
    return pl.pallas_call(
        functools.partial(finish_kernel, n),
        name="widen_results",
        out_shape=[jax.ShapeDtypeStruct(a, F32) for a in outs + small_outs],
        in_specs=[ANY] * 3 + [VMEM],
        out_specs=[ANY] * len(outs) + [VMEM] * len(small_outs),
        scratch_shapes=[pltpu.VMEM(grads.shape, BF16), pltpu.VMEM((2, *ys.shape), BF16), pltpu.VMEM((2, *ys.shape), F32)]
        + [pltpu.VMEM(a, F32) for a in outs[2:]]
        + [pltpu.VMEM((128, 128), F32)]
        + [DMA((grads.shape[0] // 2,)), DMA((6,)), DMA((2, seqs)), DMA((2, seqs))],
        compiler_params=pltpu.CompilerParams(vmem_limit_bytes=61 * 2**20),
    )(grads, ys, dx, small)


def body(n, nz, inputs, lengths, wq, wk, wv, wo, we, wr, qb, vb, eb, ob, rb, g1, s1, g2, s2, cotangent):
    heads = (qb, vb, eb.T)
    grads, ys, dx, small, *_ = layer(
        n, nz, lengths, inputs, cotangent, wq, wk, wv, wo, we, wr, heads, (ob, rb, g1, s1, g2, s2)
    )
    results = list(finish(n, grads, ys, dx, small, heads))
    results[10] = results[10].T
    return tuple(results)


def solution(mesh):
    w, wt, v = P("shard", "tp"), P("tp", "shard"), P("shard")
    rows = P("shard", "ctx", None)
    return jax.shard_map(
        functools.partial(body, mesh.shape["shard"], mesh.shape["ctx"]),
        mesh=mesh,
        in_specs=(rows, v, w, w, w, wt, w, wt, wt, wt, wt, v, v, v, v, v, v, rows),
        out_specs=(rows, rows, w, w, w, wt, w, wt, wt, wt, wt, v, v, v, v, v, v),
        check_vma=False,
    )
```
